128 devices in a mesh: section: 2 (over core), dp: 8 (over x, y_lo), seq: 8 (over z, y_hi).
Axes of the slice: x: 4, y: 4 (y_hi: 2, y_lo: 2; y = y_hi * 2 + y_lo), z: 4, core: 2. Of those that a mesh axis runs over, the one named last changes fastest.
Arguments:
- inputs: bfloat16 [2, 8, 1024, 1024], P(None, 'dp', 'seq'), may hold values from -6 to 6
- cotangent: bfloat16 [2, 8, 1024, 1024], P(None, 'dp', 'seq'), may hold values from -6 to 6
- conv_in: bfloat16 [1024, 3072], P(('section', 'dp', 'seq')), may hold values from -0.1875 to 0.1875
- conv_kernel: bfloat16 [3, 1024], P(None, ('section', 'dp', 'seq')), may hold values from -3.5 to 3.5
- qkv_weight: bfloat16 [1024, 2048], P(('section', 'dp', 'seq')), may hold values from -0.1875 to 0.1875
- qk_gain: bfloat16 [2, 64], replicated, may hold values from 0.5 to 1.5
- mix_gain: bfloat16 [2, 1024], P('section'), may hold values from 0.5 to 1.5
- ffn_gain: bfloat16 [2, 1024], P('section'), may hold values from 0.5 to 1.5
- mix_out: bfloat16 [2, 1024, 1024], P('section', ('dp', 'seq')), may hold values from -0.375 to 0.375
- w_gate: bfloat16 [2, 1024, 4608], P('section', ('dp', 'seq')), may hold values from -0.1875 to 0.1875
- w_up: bfloat16 [2, 1024, 4608], P('section', ('dp', 'seq')), may hold values from -0.1875 to 0.1875
- w_down: bfloat16 [2, 4608, 1024], P('section', None, ('dp', 'seq')), may hold values from -0.09375 to 0.09375
Outputs:
- outputs: bfloat16 [2, 8, 1024, 1024], P(None, 'dp', 'seq', 'section')
- input_grad: bfloat16 [2, 8, 1024, 1024], P(None, 'dp', 'seq', 'section')
- conv_in_grad: float32 [1024, 3072], P(('section', 'dp', 'seq'))
- conv_kernel_grad: float32 [3, 1024], P(None, ('section', 'dp', 'seq'))
- qkv_grad: float32 [1024, 2048], P(('section', 'dp', 'seq'))
- qk_gain_grad: float32 [2, 64], replicated
- mix_gain_grad: float32 [2, 1024], P('section')
- ffn_gain_grad: float32 [2, 1024], P('section')
- mix_out_grad: float32 [2, 1024, 1024], P('section', ('dp', 'seq'))
- gate_grad: float32 [2, 1024, 4608], P('section', ('dp', 'seq'))
- up_grad: float32 [2, 1024, 4608], P('section', ('dp', 'seq'))
- down_grad: float32 [2, 4608, 1024], P('section', None, ('dp', 'seq'))
The draws below stay inside these ranges and needn't reach their ends.
All inputs are finite; a program needn't handle non-finite values.
Results may differ from the reference program's by a relative error of at most 0.018.
Values may be sent and summed in bfloat16 or wider, within the bound.
A program may use at most 384 MiB of HBM per device.

```python
import jax
import jax.numpy as jnp
from jax import lax

D = 1024
FF = 4608
KV_HEADS = 8
HEAD_DIM = 64
CONV_WIDTH = 3
MICRO = 2
LENGTH = 1024
SEQS = 8


def block_scale(stream_key, extent, cuts, least, high):
    loudness = 1.0
    for position, parts in cuts:
        draws = jax.random.uniform(jax.random.fold_in(jax.random.fold_in(stream_key, 6), position), (parts,), jnp.float32, least / len(cuts), high / len(cuts))
        loudness = loudness * jnp.repeat(jnp.exp(draws), extent[position] // parts).reshape((-1,) + (1,) * (len(extent) - 1 - position))
    return loudness


def normal_values(stream_key, extent, spread, reach, split=(), dtype=jnp.bfloat16):
    drawn = spread * jax.random.normal(stream_key, extent, jnp.float32)
    if split:
        drawn = drawn * block_scale(stream_key, extent, split, -0.22, 0.18)
    return jnp.clip(drawn, -reach, reach).astype(dtype)


def setup_inputs(seed: int = 0) -> dict:
    seeds = jax.random.split(jax.random.key(seed), 13)
    return {
        "inputs": normal_values(seeds[0], (MICRO, SEQS, LENGTH, D), 1.0, 6.0, ((1, 8), (2, 8))),
        "cotangent": normal_values(seeds[1], (MICRO, SEQS, LENGTH, D), 1.0, 6.0, ((1, 8), (2, 8))),
        "conv_in": normal_values(seeds[2], (D, 3 * D), D ** -0.5, 0.1875, ((0, 128),)),
        "conv_kernel": normal_values(seeds[3], (CONV_WIDTH, D), CONV_WIDTH ** -0.5, 3.5, ((1, 128),)),
        "qkv_weight": normal_values(seeds[4], (D, D + 2 * KV_HEADS * HEAD_DIM), D ** -0.5, 0.1875, ((0, 128),)),
        "qk_gain": jnp.clip(1.0 + 0.1 * jax.random.normal(seeds[5], (2, HEAD_DIM), jnp.float32), 0.5, 1.5).astype(jnp.bfloat16),
        "mix_gain": jnp.clip(1.0 + 0.1 * jax.random.normal(seeds[6], (2, D), jnp.float32), 0.5, 1.5).astype(jnp.bfloat16),
        "ffn_gain": jnp.clip(1.0 + 0.1 * jax.random.normal(seeds[7], (2, D), jnp.float32), 0.5, 1.5).astype(jnp.bfloat16),
        "mix_out": normal_values(seeds[8], (2, D, D), (D // 4) ** -0.5, 0.375, ((0, 2), (1, 64))),
        "w_gate": normal_values(seeds[9], (2, D, FF), D ** -0.5, 0.1875, ((0, 2), (1, 64))),
        "w_up": normal_values(seeds[10], (2, D, FF), D ** -0.5, 0.1875, ((0, 2), (1, 64))),
        "w_down": normal_values(seeds[11], (2, FF, D), FF ** -0.5, 0.09375, ((0, 2), (2, 64))),
    }


@jax.custom_vjp
def low(v):
    return lax.optimization_barrier(v.astype(jnp.bfloat16)).astype(jnp.float32)

@jax.custom_vjp
def low_back(v):
    return v

def low_keep(v):
    return (low(v), None)

def low_pass(kept, grad):
    return (grad,)

def back_keep(v):
    return (v, None)

def back_low(kept, grad):
    return (low(grad),)
low.defvjp(low_keep, low_pass)
low_back.defvjp(back_keep, back_low)

def rms_norm(values, gain_vec):
    return values * lax.rsqrt(lax.optimization_barrier(jnp.mean(values * values, axis=-1, keepdims=True)) + 1e-05) * gain_vec

def matmul(left, right):
    in_shape = left.shape
    flattened = left.reshape(-1, in_shape[-1])
    result = jnp.dot(flattened, right, precision=lax.Precision.HIGHEST, preferred_element_type=jnp.float32)
    return result.reshape(in_shape[:-1] + (right.shape[1],))

def rope_tables(length, head_dim):
    half_dim = head_dim // 2
    positions = jnp.arange(length).astype(jnp.float32)
    frequency = 1000000.0 ** (-jnp.arange(half_dim).astype(jnp.float32) * 2.0 / head_dim)
    angles = positions[:, None] * frequency[None, :]
    return (jnp.cos(angles)[:, None, :], jnp.sin(angles)[:, None, :])

def rotate(values, cosine_table, sine_table):
    half_dim = values.shape[-1] // 2
    first_half, second = (values[..., :half_dim], values[..., half_dim:])
    return jnp.concatenate([first_half * cosine_table - second * sine_table, second * cosine_table + first_half * sine_table], -1)

def feed_forward(hidden, gain_vec, w_gate, w_up, w_down):
    normed = low(rms_norm(hidden, gain_vec))
    gate_out = low_back(matmul(normed, w_gate))
    up_out = low_back(matmul(normed, w_up))
    activated = low(jax.nn.silu(gate_out) * up_out)
    return low_back(matmul(activated, w_down))

def conv_block(block_in, mix_gain, ffn_gain, conv_in, conv_kernel, mix_out, w_gate, w_up, w_down):
    model_width = block_in.shape[-1]
    length = block_in.shape[1]
    kernel_len = conv_kernel.shape[0]
    normed = low(rms_norm(block_in, mix_gain))
    projected = low_back(matmul(normed, conv_in))
    b_gate = projected[..., :model_width]
    c_gate = projected[..., model_width:2 * model_width]
    values = projected[..., 2 * model_width:]
    mixed_in = low(b_gate * values)
    padded = jnp.pad(mixed_in, ((0, 0), (kernel_len - 1, 0), (0, 0)))
    convolved = sum((conv_kernel[j] * padded[:, j:j + length] for j in range(kernel_len)))
    branch = low_back(matmul(low(c_gate * convolved), mix_out))
    hidden = block_in + branch
    return hidden + feed_forward(hidden, ffn_gain, w_gate, w_up, w_down)

def attend(pieces):
    queries, key_rows, value_rows = pieces
    length, head_count, head_dim = queries.shape
    kv_heads = key_rows.shape[1]
    grouped = queries.reshape(length, kv_heads, head_count // kv_heads, head_dim)
    scores = jnp.einsum('qkgd,skd->kgqs', grouped, key_rows, precision=lax.Precision.HIGHEST) * head_dim ** (-0.5)
    scores = low_back(scores)
    allowed = jnp.arange(length)[:, None] >= jnp.arange(length)[None, :]
    attn_probs = jax.nn.softmax(jnp.where(allowed, scores, -1000000000.0), axis=-1)
    attended = jnp.einsum('kgqs,skd->qkgd', low(attn_probs), value_rows, precision=lax.Precision.HIGHEST)
    return low_back(attended.reshape(length, head_count * head_dim))

def attention_block(block_in, mix_gain, ffn_gain, qkv_weight, qk_gain, mix_out, w_gate, w_up, w_down):
    batch_rows, length, model_width = block_in.shape
    head_dim = qk_gain.shape[1]
    kv_width = (qkv_weight.shape[1] - model_width) // 2
    normed = low(rms_norm(block_in, mix_gain))
    projected = low_back(matmul(normed, qkv_weight))
    cosine_table, sine_table = rope_tables(length, head_dim)
    query_raw = projected[..., :model_width].reshape(batch_rows, length, model_width // head_dim, head_dim)
    key_raw = projected[..., model_width:model_width + kv_width].reshape(batch_rows, length, kv_width // head_dim, head_dim)
    value_raw = projected[..., model_width + kv_width:].reshape(batch_rows, length, kv_width // head_dim, head_dim)
    queries = low(rotate(rms_norm(query_raw, qk_gain[0]), cosine_table, sine_table))
    key_rows = low(rotate(rms_norm(key_raw, qk_gain[1]), cosine_table, sine_table))
    value_rows = low(value_raw)
    attended = lax.map(jax.checkpoint(attend), (queries, key_rows, value_rows))
    branch = low_back(matmul(low(attended), mix_out))
    hidden = block_in + branch
    return hidden + feed_forward(hidden, ffn_gain, w_gate, w_up, w_down)

def forward(inputs, conv_in, conv_kernel, qkv_weight, qk_gain, mix_gain, ffn_gain, mix_out, w_gate, w_up, w_down):
    micro_count, seq_count, length, model_width = inputs.shape
    flattened = inputs.reshape(micro_count * seq_count, length, model_width)
    conv_out = jax.checkpoint(conv_block)(flattened, mix_gain[0], ffn_gain[0], conv_in, conv_kernel, mix_out[0], w_gate[0], w_up[0], w_down[0])
    passed = low_back(low(conv_out))
    second = jax.checkpoint(attention_block)(passed, mix_gain[1], ffn_gain[1], qkv_weight, qk_gain, mix_out[1], w_gate[1], w_up[1], w_down[1])
    return second.reshape(micro_count, seq_count, length, model_width)

def reference(inputs, cotangent, conv_in, conv_kernel, qkv_weight, qk_gain, mix_gain, ffn_gain, mix_out, w_gate, w_up, w_down):
    as_float = [a.astype(jnp.float32) for a in (inputs, conv_in, conv_kernel, qkv_weight, qk_gain, mix_gain, ffn_gain, mix_out, w_gate, w_up, w_down)]
    result, pullback = jax.vjp(forward, *as_float)
    gradients = pullback(cotangent.astype(jnp.float32))
    return (result.astype(jnp.bfloat16), gradients[0].astype(jnp.bfloat16), gradients[1], gradients[2], gradients[3], gradients[4], gradients[5], gradients[6], gradients[7], gradients[8], gradients[9], gradients[10])
```

```python
import functools

import jax
import jax.numpy as jnp
from jax import lax
from jax.experimental import pallas as pl
from jax.experimental.pallas import tpu as pltpu
from jax.sharding import PartitionSpec as P

EPSILON = 1e-05
S, DP, SQ = "section", "dp", "seq"
MESH = pl.DeviceIdType.MESH
ANY = pl.BlockSpec(memory_space=pl.ANY)
BF, F32 = jnp.bfloat16, jnp.float32
ORDERS = ((0, 1, 2), (1, 2, 0), (2, 0, 1))
MIB = 2**20


def chip():
    dp, sq = lax.axis_index(DP), lax.axis_index(SQ)
    return (dp // 2, 2 * (sq % 2) + dp % 2, sq // 2)


def device_at(place):
    x, y, z = place
    return {DP: x * 2 + y % 2, SQ: z * 2 + y // 2}


def moved(place, axis, by):
    return tuple((v + by) % 4 if i == axis else v for i, v in enumerate(place))


def spot(place, kept=(0, 1, 2)):
    x, y, z = place

    def one(axis, value, take):
        if axis not in kept:
            return 0
        return slice(None) if value is None else take(value)

    return (
        one(0, x, lambda v: v),
        one(1, y, lambda v: v % 2),
        one(2, z, lambda v: v),
        one(1, y, lambda v: v // 2),
    )


def halves(width):
    first = (width // 256) * 128
    return (pl.ds(0, first), pl.ds(first, width - first))


def greet(devices):
    barrier = pltpu.get_barrier_semaphore()
    for device in devices:
        pl.semaphore_signal(barrier, inc=1, device_id=device, device_id_type=MESH)
    pl.semaphore_wait(barrier, len(devices))


def neighbours():
    here = chip()
    return [device_at(moved(here, axis, by)) for axis in range(3) for by in (1, -1)]


class Gather:
    def __init__(self, bufs, send, recv):
        self.bufs, self.send, self.recv = bufs, send, recv
        self.here = chip()

    def copy(self, colour, phase, kind):
        order = ORDERS[colour]
        axis, done = order[phase], order[:phase]
        buf = self.bufs[colour]
        half = halves(buf.shape[-1])
        step, part, to = ((0, 0, 1), (0, 1, 1), (0, 1, -1), (0, 0, -1), (-1, 0, 1), (1, 1, -1))[kind]
        source = moved(self.here, axis, step)
        block = tuple(None if i in done else v for i, v in enumerate(source))
        ref = buf.at[spot(block) + (slice(None), half[part])]
        slot = (colour * 3 + phase) * 6 + kind
        return pltpu.make_async_remote_copy(
            src_ref=ref,
            dst_ref=ref,
            send_sem=self.send.at[slot],
            recv_sem=self.recv.at[slot],
            device_id=device_at(moved(self.here, axis, to)),
            device_id_type=MESH,
        )

    def start(self, phase):
        for pair in ((0, 2), (1, 3)):
            for kind in pair:
                for colour in range(3):
                    self.copy(colour, phase, kind).start()

    def forward(self, phase):
        for got, then in ((0, 4), (2, 5)):
            for colour in range(3):
                self.copy(colour, phase, got).wait_recv()
                self.copy(colour, phase, then).start()

    def finish(self, phase):
        for kind in (1, 3, 4, 5):
            for colour in range(3):
                self.copy(colour, phase, kind).wait_recv()

    def settle(self):
        for phase in range(3):
            for kind in range(6):
                for colour in range(3):
                    self.copy(colour, phase, kind).wait_send()


def gather_kernel(*refs):
    shards, bufs, (own, send, recv) = refs[:3], refs[3:6], refs[6:]
    here = chip()
    greet(neighbours())
    local = [
        pltpu.make_async_copy(shards[c], bufs[c].at[spot(here)], own.at[c]) for c in range(3)
    ]
    for copy in local:
        copy.start()
    for copy in local:
        copy.wait()
    ring = Gather(bufs, send, recv)
    for phase in range(3):
        ring.start(phase)
        ring.forward(phase)
        ring.finish(phase)
    ring.settle()


def gathered(shards, cid):
    return pl.pallas_call(
        gather_kernel,
        name="gather",
        out_shape=[jax.ShapeDtypeStruct((4, 2, 4, 2) + s.shape, s.dtype) for s in shards],
        in_specs=[ANY] * 3,
        out_specs=[ANY] * 3,
        scratch_shapes=[
            pltpu.SemaphoreType.DMA((3,)),
            pltpu.SemaphoreType.DMA((54,)),
            pltpu.SemaphoreType.DMA((54,)),
        ],
        compiler_params=pltpu.CompilerParams(collective_id=cid, has_side_effects=True),
    )(*shards)


def lead(kept):
    return (4 if 0 in kept else 1, 2 if 1 in kept else 1, 4 if 2 in kept else 1, 2 if 1 in kept else 1)


def one_block(place, axis):
    x, y, z = place
    every = slice(None)
    return (
        pl.ds(x, 1) if axis == 0 else every,
        pl.ds(y % 2, 1) if axis == 1 else every,
        pl.ds(z, 1) if axis == 2 else every,
        pl.ds(y // 2, 1) if axis == 1 else every,
        every,
    )


def scatter_scratch(widths):
    shapes = []
    for colour, width in enumerate(widths):
        for phase in range(3):
            rows = lead(ORDERS[colour][phase + 1 :]) + (16,)
            pair = [rows + (h.size,) for h in halves(width)]
            shapes += [rows + (width,)] + pair + pair + [rows + (width,)] * 2
    return [pltpu.VMEM(s, BF) for s in shapes]


class Scatter:
    def __init__(self, parts, bufs, results, send, recv, load):
        self.parts, self.results = parts, results
        self.bufs = [[bufs[(c * 3 + p) * 7 :][:7] for p in range(3)] for c in range(3)]
        self.send, self.recv, self.load = send, recv, load
        self.here = chip()

    def source(self, colour, phase, by, half=None):
        axis = ORDERS[colour][phase]
        ref = self.parts[colour] if phase == 0 else self.bufs[colour][phase - 1][0]
        half = slice(None) if half is None else half
        return ref.at[one_block(moved(self.here, axis, by), axis) + (half,)]

    def loads(self, colour, phase):
        half = halves(self.parts[colour].shape[-1])
        own, ahead0, ahead1 = self.bufs[colour][phase][:3]
        pairs = (
            (self.source(colour, phase, 1, half[0]), ahead0),
            (self.source(colour, phase, -1, half[1]), ahead1),
            (self.source(colour, phase, 0), own),
        )
        return [
            functools.partial(pltpu.make_async_copy, a, b, self.load.at[(colour * 3 + phase) * 3 + i])
            for i, (a, b) in enumerate(pairs)
        ]

    def copy(self, colour, phase, kind):
        half = halves(self.parts[colour].shape[-1])
        own, ahead0, ahead1, first0, first1, last0, last1 = self.bufs[colour][phase]
        side = kind % 2
        to = (1, -1)[side]
        last = (last0, last1)[side]
        if kind < 2:
            src, dst = self.source(colour, phase, 2, half[side]), (first0, first1)[side]
        elif kind < 4:
            src, dst = self.source(colour, phase, to, half[1 - side]), last.at[..., half[1 - side]]
        else:
            src, dst = (ahead0, ahead1)[side], last.at[..., half[side]]
        slot = (colour * 3 + phase) * 6 + kind
        return pltpu.make_async_remote_copy(
            src_ref=src,
            dst_ref=dst,
            send_sem=self.send.at[slot],
            recv_sem=self.recv.at[slot],
            device_id=device_at(moved(self.here, ORDERS[colour][phase], to)),
            device_id_type=MESH,
        )

    def start(self, phase):
        for kind in range(4):
            for colour in range(3):
                self.copy(colour, phase, kind).start()
        for colour in range(3):
            for load in self.loads(colour, phase):
                load().start()

    def forward(self, phase):
        for side in range(2):
            for colour in range(3):
                self.loads(colour, phase)[side]().wait()
                self.copy(colour, phase, side).wait_recv()
                bufs = self.bufs[colour][phase]
                added(bufs[1 + side], (bufs[3 + side],), bufs[1 + side])
                self.copy(colour, phase, 4 + side).start()

    def finish(self, phase):
        for colour in range(3):
            self.loads(colour, phase)[2]().wait()
            for kind in range(2, 6):
                self.copy(colour, phase, kind).wait_recv()
            bufs = self.bufs[colour][phase]
            if phase < 2:
                added(bufs[0], (bufs[5], bufs[6]), bufs[0])
            else:
                added(bufs[0], (bufs[5], bufs[6]), self.results[colour])

    def settle(self):
        for phase in range(3):
            for kind in range(6):
                for colour in range(3):
                    self.copy(colour, phase, kind).wait_send()


def added(base, others, out):
    sizes = base.shape[:4]
    _, b, c, d = sizes

    def step(i, carry):
        at = (i // (b * c * d), (i // (c * d)) % b, (i // d) % c, i % d)
        total = base[at].astype(F32)
        for other in others:
            total = total + other[at].astype(F32)
        if len(out.shape) == 2:
            out[...] = total.astype(out.dtype)
        else:
            out[at] = total.astype(out.dtype)
        return carry

    lax.fori_loop(0, sizes[0] * b * c * d, step, 0)


class Small:
    def __init__(self, value, sums, other, slots, send, recv):
        self.value, self.sums, self.other, self.slots = value, sums, other, slots
        self.send, self.recv = send, recv
        self.here = chip()

    def sibling(self):
        return pltpu.make_async_remote_copy(
            src_ref=self.value.at[pl.ds(16, 8)],
            dst_ref=self.other,
            send_sem=self.send.at[9],
            recv_sem=self.recv.at[9],
            device_id={S: 1 - lax.axis_index(S)},
            device_id_type=MESH,
        )

    def copy(self, phase, by):
        slot = phase * 3 + by - 1
        return pltpu.make_async_remote_copy(
            src_ref=self.sums.at[phase],
            dst_ref=self.slots.at[slot],
            send_sem=self.send.at[slot],
            recv_sem=self.recv.at[slot],
            device_id=device_at(moved(self.here, phase, by)),
            device_id_type=MESH,
        )

    def start(self, phase):
        if phase == 0:
            self.sibling().start()
            self.sibling().wait_recv()
            self.sums[0] = self.value[...]
            self.sums[0, 16:24] = self.value[16:24] + self.other[...]
        for by in (1, 2, 3):
            self.copy(phase, by).start()

    def finish(self, phase):
        for by in (1, 2, 3):
            self.copy(phase, by).wait_recv()
        one, two, three = [self.slots[phase * 3 + i] for i in range(3)]
        self.sums[phase + 1] = (self.sums[phase] + two) + (one + three)

    def settle(self):
        self.sibling().wait_send()
        for phase in range(3):
            for by in (1, 2, 3):
                self.copy(phase, by).wait_send()


def line_mates():
    here = chip()
    return [device_at(moved(here, axis, by)) for axis in range(3) for by in (1, 2, 3)]


def scatter_kernel(with_small, *refs):
    refs = list(refs)
    parts = [refs.pop(0) for _ in range(3)]
    value = refs.pop(0) if with_small else None
    results = [refs.pop(0) for _ in range(3)]
    out = refs.pop(0) if with_small else None
    bufs, refs = refs[:63], refs[63:]
    send, recv, load = refs[:3]
    ring = Scatter(parts, bufs, results, send, recv, load)
    if with_small:
        sums, other, slots, ssend, srecv = refs[3:]
        small = Small(value, sums, other, slots, ssend, srecv)
        greet(line_mates() + [{S: 1 - lax.axis_index(S)}])
    else:
        greet(neighbours())
    for phase in range(3):
        ring.start(phase)
        if with_small:
            small.start(phase)
        ring.forward(phase)
        ring.finish(phase)
        if with_small:
            small.finish(phase)
    ring.settle()
    if with_small:
        small.settle()
        out[...] = small.sums[3]


def scattered(parts, cid, small=None):
    parts = [p.reshape((4, 2, 4, 2, 16, p.shape[-1])) for p in parts]
    widths = [p.shape[-1] for p in parts]
    vmem = pl.BlockSpec(memory_space=pltpu.VMEM)
    extra = [] if small is None else [small]
    scratch = scatter_scratch(widths) + [
        pltpu.SemaphoreType.DMA((54,)),
        pltpu.SemaphoreType.DMA((54,)),
        pltpu.SemaphoreType.DMA((27,)),
    ]
    if extra:
        rows = small.shape
        scratch += [
            pltpu.VMEM((4,) + rows, F32),
            pltpu.VMEM((8, 128), F32),
            pltpu.VMEM((9,) + rows, F32),
            pltpu.SemaphoreType.DMA((10,)),
            pltpu.SemaphoreType.DMA((10,)),
        ]
    return pl.pallas_call(
        functools.partial(scatter_kernel, bool(extra)),
        name="scatter",
        out_shape=[jax.ShapeDtypeStruct((16, w), F32) for w in widths]
        + [jax.ShapeDtypeStruct(e.shape, F32) for e in extra],
        in_specs=[ANY] * 3 + [vmem] * len(extra),
        out_specs=[vmem] * (3 + len(extra)),
        scratch_shapes=scratch,
        compiler_params=pltpu.CompilerParams(
            collective_id=cid, has_side_effects=True, vmem_limit_bytes=56 * MIB
        ),
    )(*parts, *extra)


def low(v):
    return v.astype(BF)


def matmul(left, right):
    return jnp.dot(left, right, preferred_element_type=F32)


def times_transposed(left, right):
    return lax.dot_general(left, right, (((1,), (1,)), ((), ())), preferred_element_type=F32)


def transposed_times(left, right):
    return lax.dot_general(left, right, (((0,), (0,)), ((), ())), preferred_element_type=F32)


def rms_norm(values, gain):
    return values * lax.rsqrt(jnp.mean(values * values, axis=-1, keepdims=True) + EPSILON) * gain


def rotate(values, cosine, sine):
    half = values.shape[-1] // 2
    a, b = values[..., :half], values[..., half:]
    return jnp.concatenate([a * cosine - b * sine, b * cosine + a * sine], -1)


def glu(gate, up):
    return jax.nn.silu(gate) * up


def swapped(value):
    return lax.ppermute(value, S, [(0, 1), (1, 0)])


def other_added(value):
    return value + swapped(value)


def joined(mine, axis):
    theirs = swapped(mine)
    first = lax.axis_index(S) == 0
    return jnp.concatenate([jnp.where(first, mine, theirs), jnp.where(first, theirs, mine)], axis)


def core_half(value, which, axis=1):
    size = value.shape[axis] // 2
    return lax.dynamic_slice_in_dim(value, which * size, size, axis)


def row_homes(turn):
    pairs = []
    for s in range(2):
        for i in range(64):
            core = (i % 2) ^ turn
            pairs.append((s * 64 + i, core * 64 + s * 32 + i // 2))
    return pairs


def mixer_halves(conv_in, qkv):
    def half(core):
        b = conv_in.reshape(8, 3, 2, 512)
        b = lax.dynamic_index_in_dim(b, core, 2, False).reshape(8, 1536)
        q = core_half(qkv[:, :1024], core)
        k = core_half(qkv[:, 1024:1536], core)
        v = core_half(qkv[:, 1536:], core)
        return jnp.concatenate([b, q, k, v], 1)

    odd = lax.axis_index(SQ) % 2
    got = [
        lax.ppermute(half(jnp.bitwise_xor(odd, turn)), (S, DP, SQ), row_homes(turn))
        for turn in range(2)
    ]
    first = lax.axis_index(S) == 0
    return jnp.concatenate([jnp.where(first, got[0], got[1]), jnp.where(first, got[1], got[0])], 0)


def mixer_homes(grads):
    core = lax.axis_index(S)
    got = []
    for turn in range(2):
        parity = jnp.bitwise_xor(core, turn)
        rows = lax.dynamic_slice_in_dim(grads, parity * 8, 8, 0)
        got.append(lax.ppermute(rows, (S, DP, SQ), [(b, a) for a, b in row_homes(turn)]))
    even = lax.axis_index(SQ) % 2 == 0
    lower = jnp.where(even, got[0], got[1])
    upper = jnp.where(even, got[1], got[0])
    both = jnp.stack([lower, upper], 1)
    conv = both[:, :, :1536].reshape(8, 2, 3, 512).transpose(0, 2, 1, 3).reshape(8, 3072)

    def side(start, stop):
        return both[:, :, start:stop].reshape(8, -1)

    return conv, jnp.concatenate([side(1536, 2048), side(2048, 2304), side(2304, 2560)], 1)


def to_heads(packed):
    width = packed.shape[1] // 4
    parts = packed.reshape(2, 128, 4, width).transpose(0, 2, 1, 3).reshape(8, 128, width)
    return lax.all_to_all(parts, SQ, 0, 0).reshape(1024, width)


def to_tokens(rows):
    width = rows.shape[1]
    parts = lax.all_to_all(rows.reshape(8, 128, width), SQ, 0, 0)
    return parts.reshape(2, 4, 128, width).transpose(0, 2, 1, 3).reshape(256, 4, width)


def rope_tables():
    positions = (lax.axis_index(SQ) * 128 + jnp.arange(128)).astype(F32)
    frequency = 1000000.0 ** (-jnp.arange(32).astype(F32) * 2.0 / 64)
    angles = positions[:, None] * frequency[None, :]
    tile = lambda t: jnp.concatenate([t, t], 0)[:, None, :]
    return tile(jnp.cos(angles)), tile(jnp.sin(angles))


def attention_probs(q, k):
    scores = jnp.einsum("qhd,kd->hqk", q, k, preferred_element_type=F32) * 0.125
    order = jnp.arange(1024)
    scores = jnp.where(order[:, None] >= order[None, :], scores, -1e9)
    return jax.nn.softmax(scores, axis=-1)


def attention(packed):
    q, k, v = packed[:, :128].reshape(1024, 2, 64), packed[:, 128:192], packed[:, 192:]
    probs = attention_probs(q, k)
    return jnp.einsum("hqk,kd->qhd", low(probs), v, preferred_element_type=F32).reshape(1024, 128)


def attention_back(packed, upstream):
    q, k, v = packed[:, :128].reshape(1024, 2, 64), packed[:, 128:192], packed[:, 192:]
    up = upstream.reshape(1024, 2, 64)
    probs = attention_probs(q, k)
    dv = jnp.einsum("hqk,qhd->kd", low(probs), up, preferred_element_type=F32)
    dp = jnp.einsum("qhd,kd->hqk", up, v, preferred_element_type=F32)
    ds = low(probs * (dp - jnp.sum(dp * probs, -1, keepdims=True)))
    dq = jnp.einsum("hqk,kd->qhd", ds, k, preferred_element_type=F32) * 0.125
    dk = jnp.einsum("hqk,qhd->kd", ds, q, preferred_element_type=F32) * 0.125
    return low(jnp.concatenate([dq.reshape(1024, 128), dk, dv], 1))


def ffn(hidden, gain, gate, up, down):
    normed = low(rms_norm(hidden, gain))
    g, u = matmul(normed, gate), matmul(normed, up)
    active = low(glu(g, u))
    return (normed, g, u, active), other_added(times_transposed(active, down))


def ffn_back(hidden, gain, gate, up, down, saved, upstream):
    normed, g, u, active = saved
    df = low(upstream)
    _, pull = jax.vjp(glu, g, u)
    dg, du = pull(matmul(df, down))
    dg, du = low(dg), low(du)
    d_normed = other_added(times_transposed(dg, gate) + times_transposed(du, up))
    _, pull = jax.vjp(rms_norm, hidden, gain)
    d_hidden, d_gain = pull(d_normed)
    grads = [low(transposed_times(a, b)) for a, b in ((normed, dg), (normed, du), (df, active))]
    return upstream + d_hidden, d_gain, grads


def shards(
    inputs,
    cotangent,
    conv_in,
    conv_kernel,
    qkv_weight,
    qk_gain,
    mix_gain,
    ffn_gain,
    mix_out,
    w_gate,
    w_up,
    w_down,
):
    core = lax.axis_index(S)
    first = core == 0
    x = inputs.reshape(256, 1024).astype(F32)
    cot = cotangent.reshape(256, 1024).astype(F32)
    gains = lax.all_gather(jnp.concatenate([mix_gain, ffn_gain], 0), S).astype(F32)
    qk = qk_gain.astype(F32)

    own = [mix_out[0], w_gate[0], w_up[0], w_down[0].T]
    keep = jnp.concatenate([core_half(w, core) for w in own], 1)
    got = swapped(jnp.concatenate([core_half(w, 1 - core) for w in own], 1))
    block0, block1 = jnp.where(first, keep, got), jnp.where(first, got, keep)
    cuts = (512, 2816, 5120)
    mo0, g0, u0, d0 = jnp.split(block0, cuts, 1)
    mo1, g1, u1, d1 = jnp.split(block1, cuts, 1)
    mixers = mixer_halves(conv_in, qkv_weight)
    ci, qw = mixers[:, :1536], mixers[:, 1536:]
    taps = jnp.pad(conv_kernel, ((0, 13), (0, 120)))
    early = [
        jnp.concatenate([g0, ci[:, :768], qw[:, :512]], 1),
        jnp.concatenate([u0, ci[:, 768:], qw[:, 512:]], 1),
        jnp.concatenate([d0, mo0, mo1, taps], 1),
    ]
    wide = [b.reshape(1024, -1) for b in gathered(early, 0)]
    late = [b.reshape(1024, -1) for b in gathered([g1, u1, d1], 1)]
    g0, u0, d0 = [w[:, :2304] for w in wide]
    g1, u1, d1 = late
    ci = jnp.concatenate([w[:, 2304:3072] for w in wide[:2]], 1)
    qw = jnp.concatenate([w[:, 3072:] for w in wide[:2]], 1)
    mo0 = joined(wide[2][:, 2304:2816], 1)
    mo1 = joined(wide[2][:, 2816:3328], 1)
    taps = wide[2][:, 3328:].reshape(64, 16, 128)[:, :3, :8].transpose(1, 0, 2).reshape(3, 512)
    taps = taps.astype(F32)

    n1 = low(rms_norm(x, gains[0, 0]))
    p1 = matmul(n1, ci)
    b_gate, c_gate, value = p1[:, :512], p1[:, 512:1024], p1[:, 1024:]
    bx = low(b_gate * value).reshape(2, 128, 512)
    rim = lax.ppermute(bx[:, 126:], SQ, [(i, i + 1) for i in range(7)])
    padded = jnp.concatenate([rim, bx], 1).astype(F32)
    conv = sum(taps[j] * padded[:, j : j + 128] for j in range(3)).reshape(256, 512)
    m1 = joined(low(c_gate * conv), 1)
    h1 = x + matmul(m1, mo0)
    saved0, f0 = ffn(h1, gains[0, 1], g0, u0, d0)
    z = low(h1 + f0).astype(F32)

    n2 = low(rms_norm(z, gains[1, 0]))
    p2 = matmul(n2, qw)
    cosine, sine = rope_tables()

    def head(raw, gain):
        return rotate(rms_norm(raw, gain), cosine, sine)

    q_raw, k_raw = p2[:, :512].reshape(256, 8, 64), p2[:, 512:768].reshape(256, 4, 64)
    q, q_pull = jax.vjp(head, q_raw, qk[0])
    k, k_pull = jax.vjp(head, k_raw, qk[1])
    packed = jnp.concatenate(
        [low(q).reshape(256, 4, 128), low(k), low(p2[:, 768:]).reshape(256, 4, 64)], 2
    )
    packed = to_heads(packed.reshape(256, 1024))
    att = to_tokens(low(attention(packed))).reshape(256, 512)
    att = joined(att, 1)
    h2 = z + matmul(att, mo1)
    saved1, f1 = ffn(h2, gains[1, 1], g1, u1, d1)
    result = low(h2 + f1)

    dh2, d_ffn1, late_grads = ffn_back(h2, gains[1, 1], g1, u1, d1, saved1, cot)
    late_sums = scattered(late_grads, 2)
    do2 = low(dh2)
    mo1_grad = low(transposed_times(att, core_half(do2, core)))
    d_att = low(times_transposed(do2, core_half(mo1, core, 0)))
    d_packed = to_tokens(attention_back(packed, to_heads(d_att))).astype(F32)
    dq_raw, dq_gain = q_pull(d_packed[:, :, :128].reshape(256, 8, 64))
    dk_raw, dk_gain = k_pull(d_packed[:, :, 128:192])
    dp2 = low(
        jnp.concatenate(
            [dq_raw.reshape(256, 512), dk_raw.reshape(256, 256), d_packed[:, :, 192:].reshape(256, 256)],
            1,
        )
    )
    qw_grad = low(transposed_times(n2, dp2))
    dn2 = other_added(times_transposed(dp2, qw))
    dz, d_mix1 = jax.vjp(rms_norm, z, gains[1, 0])[1](dn2)
    dz = low(dh2 + dz).astype(F32)

    dh1, d_ffn0, grads0 = ffn_back(h1, gains[0, 1], g0, u0, d0, saved0, dz)
    do1 = low(dh1)
    mo0_grad = low(transposed_times(m1, core_half(do1, core)))
    dm1 = times_transposed(do1, core_half(mo0, core, 0))
    dc = dm1 * conv
    dconv = (dm1 * c_gate).reshape(2, 128, 512)
    taps_grad = jnp.stack([jnp.sum(dconv * padded[:, j : j + 128], (0, 1)) for j in range(3)])
    d_padded = sum(jnp.pad(taps[j] * dconv, ((0, 0), (j, 2 - j), (0, 0))) for j in range(3))
    returned = lax.ppermute(d_padded[:, :2], SQ, [(i + 1, i) for i in range(7)])
    dbx = d_padded[:, 2:] + jnp.pad(returned, ((0, 0), (126, 0), (0, 0)))
    dbx = dbx.reshape(256, 512)
    dp1 = low(jnp.concatenate([dbx * value, dc, dbx * b_gate], 1))
    ci_grad = low(transposed_times(n1, dp1))
    dn1 = other_added(times_transposed(dp1, ci))
    dx, d_mix0 = jax.vjp(rms_norm, x, gains[0, 0])[1](dn1)
    input_grad = low(dh1 + dx)

    taps_grad = jnp.pad(taps_grad.reshape(3, 64, 8).transpose(1, 0, 2), ((0, 0), (0, 13), (0, 120)))
    parts = [
        jnp.concatenate([grads0[0], ci_grad[:, :768], qw_grad[:, :512]], 1),
        jnp.concatenate([grads0[1], ci_grad[:, 768:], qw_grad[:, 512:]], 1),
        jnp.concatenate([grads0[2], mo0_grad, mo1_grad, low(taps_grad.reshape(1024, 128))], 1),
    ]
    d_gains = jnp.stack([jnp.where(first, d_mix0, d_mix1), jnp.where(first, d_ffn0, d_ffn1)])
    d_qk = jnp.stack([dq_gain, dk_gain]).reshape(1, 128)
    small = jnp.concatenate([d_gains.reshape(16, 128), jnp.pad(d_qk, ((0, 7), (0, 0)))], 0)
    *sums, small = scattered(parts, 3, small)

    block0 = [sums[2][:, 2304:2816], sums[0][:, :2304], sums[1][:, :2304], sums[2][:, :2304]]
    block1 = [sums[2][:, 2816:3328]] + list(late_sums)
    block0, block1 = jnp.concatenate(block0, 1), jnp.concatenate(block1, 1)
    mine = jnp.where(first, block0, block1)
    theirs = swapped(jnp.where(first, block1, block0))
    lower = jnp.split(jnp.where(first, mine, theirs), cuts, 1)
    upper = jnp.split(jnp.where(first, theirs, mine), cuts, 1)
    mo_grad, g_grad, u_grad, d_grad = [jnp.concatenate(p, 1) for p in zip(lower, upper)]
    mixers = jnp.concatenate([sums[0][:, 2304:3072], sums[1][:, 2304:3072], sums[0][:, 3072:], sums[1][:, 3072:]], 1)
    conv_in_grad, qkv_grad = mixer_homes(mixers)
    return (
        core_half(result, core).reshape(2, 1, 128, 512),
        core_half(input_grad, core).reshape(2, 1, 128, 512),
        conv_in_grad,
        sums[2][:3, 3328:3336],
        qkv_grad,
        small[16].reshape(2, 64),
        small[:8].reshape(1, 1024),
        small[8:16].reshape(1, 1024),
        mo_grad[None],
        g_grad[None],
        u_grad[None],
        d_grad.T[None],
    )


def solution(mesh):
    every = (S, DP, SQ)
    weight = P(S, (DP, SQ), None)
    tokens = P(None, DP, SQ, None)
    in_specs = (
        tokens,
        tokens,
        P(every, None),
        P(None, every),
        P(every, None),
        P(),
        P(S, None),
        P(S, None),
        weight,
        weight,
        weight,
        P(S, None, (DP, SQ)),
    )
    tokens = P(None, DP, SQ, S)
    out_specs = (
        tokens,
        tokens,
        P(every, None),
        P(None, every),
        P(every, None),
        P(),
        P(S, None),
        P(S, None),
        weight,
        weight,
        weight,
        P(S, None, (DP, SQ)),
    )
    return jax.shard_map(shards, mesh=mesh, in_specs=in_specs, out_specs=out_specs, check_vma=False)
```

```python
import functools

import jax
import jax.numpy as jnp
from jax import lax
from jax.experimental import pallas as pl
from jax.experimental.pallas import tpu as pltpu
from jax.sharding import PartitionSpec as P

EPSILON = 1e-05
S, DP, SQ = "section", "dp", "seq"
MESH = pl.DeviceIdType.MESH
ANY = pl.BlockSpec(memory_space=pl.ANY)
BF, F32 = jnp.bfloat16, jnp.float32
ORDERS = ((0, 1, 2), (1, 2, 0), (2, 0, 1))
MIB = 2**20


def chip():
    dp, sq = lax.axis_index(DP), lax.axis_index(SQ)
    return (dp // 2, 2 * (sq % 2) + dp % 2, sq // 2)


def device_at(place):
    x, y, z = place
    return {DP: x * 2 + y % 2, SQ: z * 2 + y // 2}


def moved(place, axis, by):
    return tuple((v + by) % 4 if i == axis else v for i, v in enumerate(place))


def spot(place, kept=(0, 1, 2)):
    x, y, z = place

    def one(axis, value, take):
        if axis not in kept:
            return 0
        return slice(None) if value is None else take(value)

    return (
        one(0, x, lambda v: v),
        one(1, y, lambda v: v % 2),
        one(2, z, lambda v: v),
        one(1, y, lambda v: v // 2),
    )


def halves(width):
    first = (width // 256) * 128
    return (pl.ds(0, first), pl.ds(first, width - first))


def greet(devices):
    barrier = pltpu.get_barrier_semaphore()
    for device in devices:
        pl.semaphore_signal(barrier, inc=1, device_id=device, device_id_type=MESH)
    pl.semaphore_wait(barrier, len(devices))


def neighbours():
    here = chip()
    return [device_at(moved(here, axis, by)) for axis in range(3) for by in (1, -1)]


class Gather:
    def __init__(self, bufs, send, recv):
        self.bufs, self.send, self.recv = bufs, send, recv
        self.here = chip()

    def copy(self, colour, phase, kind):
        order = ORDERS[colour]
        axis, done = order[phase], order[:phase]
        buf = self.bufs[colour]
        half = halves(buf.shape[-1])
        step, part, to = ((0, 0, 1), (0, 1, 1), (0, 1, -1), (0, 0, -1), (-1, 0, 1), (1, 1, -1))[kind]
        source = moved(self.here, axis, step)
        block = tuple(None if i in done else v for i, v in enumerate(source))
        ref = buf.at[spot(block) + (slice(None), half[part])]
        slot = (colour * 3 + phase) * 6 + kind
        return pltpu.make_async_remote_copy(
            src_ref=ref,
            dst_ref=ref,
            send_sem=self.send.at[slot],
            recv_sem=self.recv.at[slot],
            device_id=device_at(moved(self.here, axis, to)),
            device_id_type=MESH,
        )

    def start(self, phase):
        for pair in ((0, 2), (1, 3)):
            for kind in pair:
                for colour in range(3):
                    self.copy(colour, phase, kind).start()

    def forward(self, phase):
        for got, then in ((0, 4), (2, 5)):
            for colour in range(3):
                self.copy(colour, phase, got).wait_recv()
                self.copy(colour, phase, then).start()

    def finish(self, phase):
        for kind in (1, 3, 4, 5):
            for colour in range(3):
                self.copy(colour, phase, kind).wait_recv()

    def settle(self):
        for phase in range(3):
            for kind in range(6):
                for colour in range(3):
                    self.copy(colour, phase, kind).wait_send()


def gather_kernel(*refs):
    shards, bufs, (own, send, recv) = refs[:3], refs[3:6], refs[6:]
    here = chip()
    greet(neighbours())
    local = [
        pltpu.make_async_copy(shards[c], bufs[c].at[spot(here)], own.at[c]) for c in range(3)
    ]
    for copy in local:
        copy.start()
    for copy in local:
        copy.wait()
    ring = Gather(bufs, send, recv)
    for phase in range(3):
        ring.start(phase)
        ring.forward(phase)
        ring.finish(phase)
    ring.settle()


def gathered(shards, cid):
    return pl.pallas_call(
        gather_kernel,
        name="gather",
        out_shape=[jax.ShapeDtypeStruct((4, 2, 4, 2) + s.shape, s.dtype) for s in shards],
        in_specs=[ANY] * 3,
        out_specs=[ANY] * 3,
        scratch_shapes=[
            pltpu.SemaphoreType.DMA((3,)),
            pltpu.SemaphoreType.DMA((54,)),
            pltpu.SemaphoreType.DMA((54,)),
        ],
        compiler_params=pltpu.CompilerParams(collective_id=cid, has_side_effects=True),
    )(*shards)


def lead(kept):
    return (4 if 0 in kept else 1, 2 if 1 in kept else 1, 4 if 2 in kept else 1, 2 if 1 in kept else 1)


def one_block(place, axis):
    x, y, z = place
    every = slice(None)
    return (
        pl.ds(x, 1) if axis == 0 else every,
        pl.ds(y % 2, 1) if axis == 1 else every,
        pl.ds(z, 1) if axis == 2 else every,
        pl.ds(y // 2, 1) if axis == 1 else every,
        every,
    )


def scatter_scratch(widths):
    shapes = []
    for colour, width in enumerate(widths):
        for phase in range(3):
            rows = lead(ORDERS[colour][phase + 1 :]) + (16,)
            pair = [rows + (h.size,) for h in halves(width)]
            shapes += [rows + (width,)] + pair + pair + [rows + (width,)] * 2
    return [pltpu.VMEM(s, BF) for s in shapes]


class Scatter:
    def __init__(self, parts, bufs, results, send, recv, load):
        self.parts, self.results = parts, results
        self.bufs = [[bufs[(c * 3 + p) * 7 :][:7] for p in range(3)] for c in range(3)]
        self.send, self.recv, self.load = send, recv, load
        self.here = chip()

    def source(self, colour, phase, by, half=None):
        axis = ORDERS[colour][phase]
        ref = self.parts[colour] if phase == 0 else self.bufs[colour][phase - 1][0]
        half = slice(None) if half is None else half
        return ref.at[one_block(moved(self.here, axis, by), axis) + (half,)]

    def loads(self, colour, phase):
        half = halves(self.parts[colour].shape[-1])
        own, ahead0, ahead1 = self.bufs[colour][phase][:3]
        pairs = (
            (self.source(colour, phase, 1, half[0]), ahead0),
            (self.source(colour, phase, -1, half[1]), ahead1),
            (self.source(colour, phase, 0), own),
        )
        return [
            functools.partial(pltpu.make_async_copy, a, b, self.load.at[(colour * 3 + phase) * 3 + i])
            for i, (a, b) in enumerate(pairs)
        ]

    def copy(self, colour, phase, kind):
        half = halves(self.parts[colour].shape[-1])
        own, ahead0, ahead1, first0, first1, last0, last1 = self.bufs[colour][phase]
        side = kind % 2
        to = (1, -1)[side]
        last = (last0, last1)[side]
        if kind < 2:
            src, dst = self.source(colour, phase, 2, half[side]), (first0, first1)[side]
        elif kind < 4:
            src, dst = self.source(colour, phase, to, half[1 - side]), last.at[..., half[1 - side]]
        else:
            src, dst = (ahead0, ahead1)[side], last.at[..., half[side]]
        slot = (colour * 3 + phase) * 6 + kind
        return pltpu.make_async_remote_copy(
            src_ref=src,
            dst_ref=dst,
            send_sem=self.send.at[slot],
            recv_sem=self.recv.at[slot],
            device_id=device_at(moved(self.here, ORDERS[colour][phase], to)),
            device_id_type=MESH,
        )

    def start(self, phase):
        for kind in range(4):
            for colour in range(3):
                self.copy(colour, phase, kind).start()
        for colour in range(3):
            for load in self.loads(colour, phase):
                load().start()

    def forward(self, phase):
        for side in range(2):
            for colour in range(3):
                self.loads(colour, phase)[side]().wait()
                self.copy(colour, phase, side).wait_recv()
                bufs = self.bufs[colour][phase]
                added(bufs[1 + side], (bufs[3 + side],), bufs[1 + side])
                self.copy(colour, phase, 4 + side).start()

    def finish(self, phase):
        for colour in range(3):
            self.loads(colour, phase)[2]().wait()
            for kind in range(2, 6):
                self.copy(colour, phase, kind).wait_recv()
            bufs = self.bufs[colour][phase]
            if phase < 2:
                added(bufs[0], (bufs[5], bufs[6]), bufs[0])
            else:
                added(bufs[0], (bufs[5], bufs[6]), self.results[colour])

    def settle(self):
        for phase in range(3):
            for kind in range(6):
                for colour in range(3):
                    self.copy(colour, phase, kind).wait_send()


def added(base, others, out):
    sizes = base.shape[:4]
    _, b, c, d = sizes

    def step(i, carry):
        at = (i // (b * c * d), (i // (c * d)) % b, (i // d) % c, i % d)
        total = base[at].astype(F32)
        for other in others:
            total = total + other[at].astype(F32)
        if len(out.shape) == 2:
            out[...] = total.astype(out.dtype)
        else:
            out[at] = total.astype(out.dtype)
        return carry

    lax.fori_loop(0, sizes[0] * b * c * d, step, 0)


class Small:
    def __init__(self, value, sums, other, slots, send, recv):
        self.value, self.sums, self.other, self.slots = value, sums, other, slots
        self.send, self.recv = send, recv
        self.here = chip()

    def sibling(self):
        return pltpu.make_async_remote_copy(
            src_ref=self.value.at[pl.ds(16, 8)],
            dst_ref=self.other,
            send_sem=self.send.at[9],
            recv_sem=self.recv.at[9],
            device_id={S: 1 - lax.axis_index(S)},
            device_id_type=MESH,
        )

    def copy(self, phase, by):
        slot = phase * 3 + by - 1
        return pltpu.make_async_remote_copy(
            src_ref=self.sums.at[phase],
            dst_ref=self.slots.at[slot],
            send_sem=self.send.at[slot],
            recv_sem=self.recv.at[slot],
            device_id=device_at(moved(self.here, phase, by)),
            device_id_type=MESH,
        )

    def start(self, phase):
        if phase == 0:
            self.sibling().start()
            self.sibling().wait_recv()
            self.sums[0] = self.value[...]
            self.sums[0, 16:24] = self.value[16:24] + self.other[...]
        for by in (1, 2, 3):
            self.copy(phase, by).start()

    def finish(self, phase):
        for by in (1, 2, 3):
            self.copy(phase, by).wait_recv()
        one, two, three = [self.slots[phase * 3 + i] for i in range(3)]
        self.sums[phase + 1] = (self.sums[phase] + two) + (one + three)

    def settle(self):
        self.sibling().wait_send()
        for phase in range(3):
            for by in (1, 2, 3):
                self.copy(phase, by).wait_send()


def line_mates():
    here = chip()
    return [device_at(moved(here, axis, by)) for axis in range(3) for by in (1, 2, 3)]


def scatter_kernel(with_small, *refs):
    refs = list(refs)
    parts = [refs.pop(0) for _ in range(3)]
    value = refs.pop(0) if with_small else None
    results = [refs.pop(0) for _ in range(3)]
    out = refs.pop(0) if with_small else None
    bufs, refs = refs[:63], refs[63:]
    send, recv, load = refs[:3]
    ring = Scatter(parts, bufs, results, send, recv, load)
    if with_small:
        sums, other, slots, ssend, srecv = refs[3:]
        small = Small(value, sums, other, slots, ssend, srecv)
        greet(line_mates() + [{S: 1 - lax.axis_index(S)}])
    else:
        greet(neighbours())
    for phase in range(3):
        ring.start(phase)
        if with_small:
            small.start(phase)
        ring.forward(phase)
        ring.finish(phase)
        if with_small:
            small.finish(phase)
    ring.settle()
    if with_small:
        small.settle()
        out[...] = small.sums[3]


def scattered(parts, cid, small=None):
    parts = [p.reshape((4, 2, 4, 2, 16, p.shape[-1])) for p in parts]
    widths = [p.shape[-1] for p in parts]
    vmem = pl.BlockSpec(memory_space=pltpu.VMEM)
    extra = [] if small is None else [small]
    scratch = scatter_scratch(widths) + [
        pltpu.SemaphoreType.DMA((54,)),
        pltpu.SemaphoreType.DMA((54,)),
        pltpu.SemaphoreType.DMA((27,)),
    ]
    if extra:
        rows = small.shape
        scratch += [
            pltpu.VMEM((4,) + rows, F32),
            pltpu.VMEM((8, 128), F32),
            pltpu.VMEM((9,) + rows, F32),
            pltpu.SemaphoreType.DMA((10,)),
            pltpu.SemaphoreType.DMA((10,)),
        ]
    return pl.pallas_call(
        functools.partial(scatter_kernel, bool(extra)),
        name="scatter",
        out_shape=[jax.ShapeDtypeStruct((16, w), F32) for w in widths]
        + [jax.ShapeDtypeStruct(e.shape, F32) for e in extra],
        in_specs=[ANY] * 3 + [vmem] * len(extra),
        out_specs=[vmem] * (3 + len(extra)),
        scratch_shapes=scratch,
        compiler_params=pltpu.CompilerParams(
            collective_id=cid, has_side_effects=True, vmem_limit_bytes=56 * MIB
        ),
    )(*parts, *extra)


class Bag:
    def __init__(self, **items):
        self.__dict__.update(items)


def launch(body, name, cid, ins, outs, scratch):
    def kernel(*refs):
        body(Bag(**dict(zip([*ins, *outs, *scratch], refs))))

    got = pl.pallas_call(
        kernel,
        name=name,
        out_shape=[jax.ShapeDtypeStruct(shape, dtype) for shape, dtype, _ in outs.values()],
        in_specs=[where for _, where in ins.values()],
        out_specs=[where for _, _, where in outs.values()],
        scratch_shapes=list(scratch.values()),
        compiler_params=pltpu.CompilerParams(
            collective_id=cid, has_side_effects=True, vmem_limit_bytes=60 * MIB
        ),
    )(*[value for value, _ in ins.values()])
    return Bag(**dict(zip(outs, got)))


VM = pl.BlockSpec(memory_space=pltpu.VMEM)


def vm(*shape, dtype=F32):
    return pltpu.VMEM(shape, dtype)


class Moves:
    def __init__(self, local, send, recv):
        self.sems = local, send, recv
        self.kept, self.sent = [], []
        self.locals = self.remotes = 0

    def local(self, src, dst):
        copy = pltpu.make_async_copy(src, dst, self.sems[0].at[self.locals])
        self.locals += 1
        copy.start()
        return copy

    def keep(self, src, dst):
        self.kept.append(self.local(src, dst))

    def remote(self, src, dst, device):
        slot = self.remotes
        self.remotes += 1
        copy = pltpu.make_async_remote_copy(
            src_ref=src,
            dst_ref=dst,
            send_sem=self.sems[1].at[slot],
            recv_sem=self.sems[2].at[slot],
            device_id=device,
            device_id_type=MESH,
        )
        copy.start()
        self.sent.append(copy)
        return copy

    def sibling(self, src, dst):
        return self.remote(src, dst, {S: 1 - lax.axis_index(S)})

    def mates(self, src, dst):
        me = lax.axis_index(SQ)
        copies = [self.remote(src(lax.rem(me + j, 8)), dst, {SQ: lax.rem(me + j, 8)}) for j in range(1, 8)]
        return [self.local(src(me), dst)], copies

    def done(self, copy):
        copy.wait_send()
        self.sent = [c for c in self.sent if c is not copy]

    def flush(self):
        for copy in self.kept:
            copy.wait()
        self.kept = []

    def settle(self):
        self.flush()
        for copy in self.sent:
            copy.wait_send()


def arrived(moves):
    own, copies = moves
    for copy in own:
        copy.wait()
    for copy in copies:
        copy.wait_recv()


def mate_devices():
    me = lax.axis_index(SQ)
    return [{SQ: lax.rem(me + j, 8)} for j in range(1, 8)]


def across_devices():
    here = chip()
    return [device_at(moved(here, axis, by)) for axis in range(2) for by in (1, -1)]


def sibling_device():
    return {S: 1 - lax.axis_index(S)}


def by_rows(rows, step, size=32):
    def body(i, carry):
        step(pl.ds(pl.multiple_of(i * size, size), size))
        return carry

    lax.fori_loop(0, rows // size, body, 0)


def by_columns(width, step, size=256):
    def body(i, carry):
        step(pl.ds(pl.multiple_of(i * size, size), size))
        return carry

    lax.fori_loop(0, width // size, body, 0)


def core_columns(size):
    return pl.ds(pl.multiple_of(lax.axis_index(S) * size, size), size)


def inverse_norm(v):
    return lax.rsqrt(jnp.mean(v * v, axis=-1, keepdims=True) + EPSILON)


def norm_rows(src, gain, dst):
    def step(rows):
        v = src[rows].astype(F32)
        dst[rows] = low(v * inverse_norm(v) * gain)

    by_rows(256, step)


def norm_back_rows(src, gain, upstreams, residual, out, d_gain):
    d_gain[...] = jnp.zeros_like(d_gain)

    def step(rows):
        v = src[rows].astype(F32)
        up = sum(u[rows] for u in upstreams)
        r = inverse_norm(v)
        t = up * gain
        dv = r * (t - v * (r * r * jnp.mean(t * v, axis=-1, keepdims=True)))
        out[rows] = (residual[rows].astype(F32) + dv).astype(out.dtype)
        scaled = up * (v * r)
        d_gain[...] += scaled[:8] + scaled[8:16] + scaled[16:24] + scaled[24:]

    by_rows(256, step)


def transpose_into(src, dst):
    def step(cols):
        dst[cols, :] = src[:, cols].astype(F32).T.astype(BF)

    by_columns(1024, step, 128)


def lanes(width=128):
    return lax.broadcasted_iota(jnp.int32, (1, width), 1)


def head_mean(v, ones):
    return jnp.dot(v, ones, precision=lax.Precision.HIGHEST, preferred_element_type=F32)


def half_turn(v):
    return jnp.where(lanes() % 64 < 32, pltpu.roll(v, 96, 1), pltpu.roll(v, 32, 1))


def head_lanes(v, head, upper):
    v = v.astype(F32)
    if head != upper:
        v = pltpu.roll(v, 64, 1)
    return jnp.where(lanes() >= 64 if upper else lanes() < 64, v, 0.0)


def block_probs(b, block, head):
    count = 256 * (block + 1)
    q = head_lanes(b.packed[2 * block : 2 * block + 2, :, :128].reshape(256, 128), head, 0)
    kv = b.packed[: 2 * block + 2, :, 128:].reshape(count, 128)
    scores = times_transposed(low(q), kv) * 0.125
    row = lax.broadcasted_iota(jnp.int32, (256, count), 0) + 256 * block
    col = lax.broadcasted_iota(jnp.int32, (256, count), 1)
    e = jnp.exp(jnp.where(row >= col, scores, -1e9))
    return q, kv, e * (1.0 / jnp.sum(e, -1, keepdims=True))


def forward_kernel(b):
    core, seq = lax.axis_index(S), lax.axis_index(SQ)
    greet(across_devices() + mate_devices() + [sibling_device()])
    moves = Moves(b.local, b.send, b.recv)
    here = chip()
    shards, bufs = (b.gs, b.us, b.ds), (b.g1, b.u1, b.d1)
    own = [moves.local(s, w.at[spot(here)]) for s, w in zip(shards, bufs)]
    ci_loads = [
        moves.local(w.at[:, pl.ds(2304, 768)], b.ci.at[:, pl.ds(i * 768, 768)])
        for i, w in enumerate((b.w0, b.w1))
    ]
    for copy in own:
        copy.wait()
    ring = Gather(bufs, b.gsend, b.grecv)
    ring.start(0)
    half = core_columns(512)
    mo_source = [b.w2.at[:, pl.ds(2304 + 512 * i, 512)] for i in range(2)]
    mo_loads = [moves.local(s, d.at[:, half]) for s, d in zip(mo_source, (b.mo0, b.mo1))]
    mo_swaps = [moves.sibling(s, d.at[:, half]) for s, d in zip(mo_source, (b.mo0, b.mo1))]
    ffn_loads = [
        moves.local(w.at[:, pl.ds(0, 2304)], d)
        for w, d in ((b.w0, b.gate), (b.w1, b.up), (b.w2, b.down))
    ]
    qw_loads = [
        moves.local(w.at[:, pl.ds(3072, 512)], b.qw.at[:, pl.ds(i * 512, 512)])
        for i, w in enumerate((b.w0, b.w1))
    ]
    norm_rows(b.x, b.gains[0:1], b.normed)
    for copy in ci_loads:
        copy.wait()

    def project(cols):
        b.p1[:, cols] = matmul(b.normed[...], b.ci[:, cols])

    by_columns(1536, project)
    moves.keep(b.p1, b.p1_out)
    ring.forward(0)

    def gated(rows):
        b.bx[rows] = low(b.p1[rows, :512] * b.p1[rows, 1024:]).astype(F32)

    by_rows(256, gated)
    for m in range(2):
        b.pad[m, 8:] = b.bx[m * 128 : m * 128 + 128]
    rim = moves.remote(b.pad.at[:, pl.ds(128, 8)], b.rim, {SQ: lax.rem(seq + 1, 8)})
    ring.finish(0)
    ring.start(1)
    rim.wait_recv()
    b.pad[:, :8] = jnp.where(seq > 0, b.rim[...], 0.0)
    moves.keep(b.pad, b.pad_out)

    def convolve(cols):
        taps = b.taps[:, cols]
        for m in range(2):
            conv = sum(taps[j : j + 1] * b.pad[m, 6 + j : 134 + j, cols] for j in range(3))
            rows = slice(m * 128, m * 128 + 128)
            gate = b.p1[rows, pl.ds(pl.multiple_of(cols.start + 512, 128), 128)]
            b.m1[rows, pl.ds(pl.multiple_of(core * 512 + cols.start, 128), 128)] = low(gate * conv)

    by_columns(512, convolve, 128)
    swap = moves.sibling(b.m1.at[:, half], b.m1.at[:, half])
    ring.forward(1)
    swap.wait_recv()
    moves.keep(b.m1, b.m1_out)
    for copy in mo_loads:
        copy.wait()
    for copy in mo_swaps:
        copy.wait_recv()

    def mix(cols):
        b.h1[:, cols] = b.x[:, cols].astype(F32) + matmul(b.m1[...], b.mo0[:, cols])

    by_columns(1024, mix)
    moves.keep(b.h1, b.h1_out)
    ring.finish(1)
    ring.start(2)
    norm_rows(b.h1, b.gains[1:2], b.normed)
    for copy in ffn_loads:
        copy.wait()

    def hidden(cols):
        g = matmul(b.normed[...], b.gate[:, cols])
        u = matmul(b.normed[...], b.up[:, cols])
        b.active[:, cols] = low(g / (1.0 + jnp.exp(-g)) * u)

    by_columns(2304, hidden)

    def contract(cols):
        b.f[:, cols] = times_transposed(b.active[...], b.down[cols, :])

    by_columns(1024, contract)
    swap = moves.sibling(b.f, b.f_other)
    ring.forward(2)
    swap.wait_recv()

    def passed(rows):
        b.z[rows] = low(b.h1[rows] + (b.f[rows] + b.f_other[rows]))

    by_rows(256, passed)
    moves.keep(b.z, b.z_out)

    norm_rows(b.z, b.gains[2:3], b.normed2)
    for copy in qw_loads:
        copy.wait()

    def project2(cols):
        b.p2[:, cols] = matmul(b.normed2[...], b.qw[:, cols])

    by_columns(1024, project2)
    moves.keep(b.p2, b.p2_out)
    for chunk in range(8):
        cols = slice(chunk * 128, chunk * 128 + 128)
        head, place = chunk % 4, pl.ds(chunk // 4 * 128, 128)
        for m in range(2):
            v = b.p2[m * 128 : m * 128 + 128, cols]
            y = v * lax.rsqrt(head_mean(v * v, b.ones[...]) + EPSILON) * b.qk[:, cols]
            y = y * b.cosine[...] + half_turn(y) * b.sine[...]
            if chunk >= 4:
                y = jnp.where(lanes() < 64, y, v)
            b.out[m * 4 + head, :, place] = low(y)
    arrived(moves.mates(lambda j: b.out.at[j], b.packed.at[seq]))
    moves.keep(b.packed, b.packed_out)
    for block in range(4):
        results = []
        for head in range(2):
            _, kv, probs = block_probs(b, block, head)
            results.append(matmul(low(probs), kv))
        joint = jnp.where(lanes() < 64, pltpu.roll(results[0], 64, 1), results[1])
        b.att_rows[2 * block : 2 * block + 2] = low(joint).reshape(2, 128, 128)
    rows = pl.ds(pl.multiple_of(seq // 4 * 128, 128), 128)
    cols = pl.ds(pl.multiple_of(core * 512 + seq % 4 * 128, 128), 128)
    arrived(moves.mates(lambda j: b.att_rows.at[j], b.att.at[rows, cols]))
    swap = moves.sibling(b.att.at[:, half], b.att.at[:, half])
    swap.wait_recv()
    moves.keep(b.att, b.att_out)

    def mix2(cols):
        b.h2[:, cols] = b.z[:, cols].astype(F32) + matmul(b.att[...], b.mo1[:, cols])

    by_columns(1024, mix2)
    moves.keep(b.h2, b.h2_out)
    moves.keep(b.mo0, b.mo0_out)
    moves.keep(b.mo1, b.mo1_out)
    ring.finish(2)
    ring.settle()
    moves.settle()


def dma(count):
    return pltpu.SemaphoreType.DMA((count,))


def bf(*shape):
    return pltpu.VMEM(shape, BF)


def forward(x, gains, qk, cosine, sine, ones, taps, wide, late):
    full = (4, 2, 4, 2, 16, 2304)
    return launch(
        forward_kernel,
        "forward",
        1,
        dict(
            x=(x, VM), gains=(gains, VM), qk=(qk, VM), cosine=(cosine, VM), sine=(sine, VM),
            ones=(ones, VM), taps=(taps, VM), w0=(wide[0], ANY), w1=(wide[1], ANY), w2=(wide[2], ANY),
            gs=(late[0], ANY), us=(late[1], ANY), ds=(late[2], ANY),
        ),
        dict(
            g1=(full, BF, ANY), u1=(full, BF, ANY), d1=(full, BF, ANY),
            p1_out=((256, 1536), F32, ANY), pad_out=((2, 136, 512), F32, ANY),
            m1_out=((256, 1024), BF, ANY), h1_out=((256, 1024), F32, ANY), z_out=((256, 1024), BF, ANY),
            p2_out=((256, 1024), F32, ANY), packed_out=((8, 128, 256), BF, ANY),
            att_out=((256, 1024), BF, ANY), h2_out=((256, 1024), F32, ANY),
            mo0_out=((1024, 1024), BF, ANY), mo1_out=((1024, 1024), BF, ANY),
        ),
        dict(
            ci=bf(1024, 1536), qw=bf(1024, 1024), mo0=bf(1024, 1024), mo1=bf(1024, 1024),
            gate=bf(1024, 2304), up=bf(1024, 2304), down=bf(1024, 2304),
            normed=bf(256, 1024), normed2=bf(256, 1024), p1=vm(256, 1536), bx=vm(256, 512), pad=vm(2, 136, 512),
            rim=vm(2, 8, 512), m1=bf(256, 1024), h1=vm(256, 1024), active=bf(256, 2304),
            f=vm(256, 1024), f_other=vm(256, 1024), z=bf(256, 1024), p2=vm(256, 1024),
            out=bf(8, 128, 256), packed=bf(8, 128, 256), att_rows=bf(8, 128, 128), att=bf(256, 1024),
            h2=vm(256, 1024), local=dma(32), send=dma(24), recv=dma(24), gsend=dma(54), grecv=dma(54),
        ),
    )


def ffn_scratch():
    return dict(
        wg=bf(2, 1024, 256), wu=bf(2, 1024, 256), wd=bf(2, 1024, 256),
        sg=bf(2, 1024, 256), su=bf(2, 1024, 256), sd=bf(2, 1024, 256),
        load=pltpu.SemaphoreType.DMA((2, 3)), store=pltpu.SemaphoreType.DMA((2, 3)),
    )


def ffn_loop(b, weights, grads, normed, normed_t, df, df_t, da, f=None):
    def columns(i):
        return pl.ds(pl.multiple_of(i * 256, 256), 256)

    def loads(i, slot):
        return [
            pltpu.make_async_copy(w.at[:, columns(i)], d.at[slot], b.load.at[slot, k])
            for k, (w, d) in enumerate(zip(weights, (b.wg, b.wu, b.wd)))
        ]

    def stores(i, slot):
        return [
            pltpu.make_async_copy(s.at[slot], g.at[:, columns(i)], b.store.at[slot, k])
            for k, (g, s) in enumerate(zip(grads, (b.sg, b.su, b.sd)))
        ]

    for copy in loads(0, 0):
        copy.start()
    da[...] = jnp.zeros_like(da)
    if f is not None:
        f[...] = jnp.zeros_like(f)

    def step(i, carry):
        slot = lax.rem(i, 2)
        for copy in loads(i, slot):
            copy.wait()

        @pl.when(i < 8)
        def _():
            for copy in loads(i + 1, 1 - slot):
                copy.start()

        gate, up, down = b.wg.at[slot], b.wu.at[slot], b.wd.at[slot]
        g = matmul(normed[...], gate[...])
        u = matmul(normed[...], up[...])
        ds = matmul(df[...], down[...])
        sig = 1.0 / (1.0 + jnp.exp(-g))
        silu = g * sig
        s = low(silu * u)
        dg = low(ds * u * (sig * (1.0 + g * (1.0 - sig))))
        du = low(ds * silu)
        if f is not None:
            f[...] += times_transposed(s, down[...])
        da[...] += times_transposed(dg, gate[...]) + times_transposed(du, up[...])

        @pl.when(i >= 2)
        def _():
            for copy in stores(i - 2, slot):
                copy.wait()

        b.sg[slot] = low(matmul(normed_t[...], dg))
        b.su[slot] = low(matmul(normed_t[...], du))
        b.sd[slot] = low(matmul(df_t[...], s))
        for copy in stores(i, slot):
            copy.start()
        return carry

    lax.fori_loop(0, 9, step, 0)
    for copy in stores(7, 1) + stores(8, 0):
        copy.wait()


def middle_kernel(b):
    greet([sibling_device()])
    moves = Moves(b.local, b.send, b.recv)
    norm_rows(b.h2, b.gains[3:4], b.normed)
    transpose_into(b.normed, b.normed_t)
    transpose_into(b.cot, b.cot_t)
    ffn_loop(
        b, (b.g1, b.u1, b.d1), (b.gg, b.gu, b.gd), b.normed, b.normed_t, b.cot, b.cot_t, b.da, b.f
    )
    half = core_columns(512)
    other = pl.ds(pl.multiple_of(512 - lax.axis_index(S) * 512, 512), 512)
    da_swap = moves.sibling(b.da, b.da_other)
    f_swap = moves.sibling(b.f.at[:, other], b.f_other)
    da_swap.wait_recv()
    norm_back_rows(b.h2, b.gains[3:4], (b.da, b.da_other), b.cot, b.dh2, b.d_ffn)
    f_swap.wait_recv()

    def finish(rows):
        b.result[rows] = low(b.h2[rows, half] + (b.f[rows, half] + b.f_other[rows]))

    by_rows(256, finish)
    moves.settle()


def middle(h2, cot, gains, w):
    grad = ((1024, 2304), BF, ANY)
    return launch(
        middle_kernel,
        "middle",
        2,
        dict(
            h2=(h2, VM), cot=(cot, VM), gains=(gains, VM),
            g1=(w.g1.reshape(1024, 2304), ANY), u1=(w.u1.reshape(1024, 2304), ANY),
            d1=(w.d1.reshape(1024, 2304), ANY),
        ),
        dict(
            gg=grad, gu=grad, gd=grad, dh2=((256, 1024), F32, VM), d_ffn=((8, 1024), F32, VM),
            result=((256, 512), BF, VM),
        ),
        dict(
            normed=bf(256, 1024), normed_t=bf(1024, 256), cot_t=bf(1024, 256), da=vm(256, 1024),
            da_other=vm(256, 1024), f=vm(256, 1024), f_other=vm(256, 512),
            local=dma(2), send=dma(2), recv=dma(2), **ffn_scratch(),
        ),
    )


def staged(moves, left_t, right, slots, dests):
    for k, (slot, dest) in enumerate(zip(slots, dests)):
        slot[...] = low(matmul(left_t[...], right(k)))
        moves.keep(slot, dest)


def backward_kernel(b):
    core, seq = lax.axis_index(S), lax.axis_index(SQ)
    greet(across_devices() + mate_devices() + [sibling_device()])
    moves = Moves(b.local, b.send, b.recv)
    ring = Scatter((b.rg, b.ru, b.rd), b.ring, (b.sum_g, b.sum_u, b.sum_d), b.ssend, b.srecv, b.sload)
    ring.start(0)
    half = core_columns(512)
    mo1_load = moves.local(b.mo1_in, b.mo)
    attn_loads = [
        moves.local(w.at[:, pl.ds(3072, 512)], b.proj.at[:, pl.ds(i * 512, 512)])
        for i, w in enumerate((b.w0, b.w1))
    ]
    packed_load = moves.local(b.packed_in, b.packed)
    p2_load = moves.local(b.p2_in, b.p2)
    p1_load = moves.local(b.p1_in, b.p1)

    def rounded(rows):
        b.do[rows] = low(b.dh2[rows])

    by_rows(256, rounded)
    mo1_load.wait()
    first_row = pl.multiple_of(core * 512, 512)
    for h in range(4):
        rows = pl.ds(pl.multiple_of(first_row + h * 128, 128), 128)
        d_att = low(times_transposed(b.do[...], b.mo[rows, :]))
        for m in range(2):
            b.out_att[m * 4 + h] = d_att[m * 128 : m * 128 + 128]
    exchange = moves.mates(lambda j: b.out_att.at[j], b.d_att.at[seq])
    transpose_into(b.att, b.turned)

    def own_do(k):
        return b.do[:, pl.ds(pl.multiple_of(core * 512 + k * 256, 256), 256)]

    def places(grad, start, count):
        return [grad.at[:, pl.ds(start + 256 * k, 256)] for k in range(count)]

    def slots(*stacks):
        return [stack.at[i] for stack in stacks for i in range(2)]

    staged(moves, b.turned, own_do, slots(b.sg), places(b.grad2, 2816, 2))
    mo0_load = moves.local(b.mo0_in, b.mo)
    packed_load.wait()
    arrived(exchange)
    b.dkv[...] = jnp.zeros_like(b.dkv)
    for block in range(4):
        count = 256 * (block + 1)
        results = []
        for head in range(2):
            q, kv, probs = block_probs(b, block, head)
            up = low(head_lanes(b.d_att[2 * block : 2 * block + 2].reshape(256, 128), head, 1))
            dp = times_transposed(up, kv)
            ds = low(probs * (dp - jnp.sum(dp * probs, -1, keepdims=True)))
            b.dkv[:count] += transposed_times(ds, low(q * 0.125)) + transposed_times(low(probs), up)
            results.append(matmul(ds, kv) * 0.125)
        joint = jnp.where(lanes() < 64, results[0], pltpu.roll(results[1], 64, 1))
        b.out[2 * block : 2 * block + 2, :, :128] = low(joint).reshape(2, 128, 128)
    for j in range(8):
        b.out[j, :, 128:] = low(b.dkv[j * 128 : j * 128 + 128])
    exchange = moves.mates(lambda j: b.out.at[j], b.d_packed.at[seq])
    norm_rows(b.z, b.gains[2:3], b.normed)
    transpose_into(b.normed, b.normed_t)
    p2_load.wait()
    arrived(exchange)
    for chunk in range(8):
        cols = slice(chunk * 128, chunk * 128 + 128)
        head, place = chunk % 4, slice(chunk // 4 * 128, chunk // 4 * 128 + 128)
        total = jnp.zeros((1, 128), F32)
        for m in range(2):
            v = b.p2[m * 128 : m * 128 + 128, cols]
            up = b.d_packed[m * 4 + head, :, place].astype(F32)
            r = lax.rsqrt(head_mean(v * v, b.ones[...]) + EPSILON)
            dy = up * b.cosine[...] + half_turn(up * b.sine[...])
            t = dy * b.qk[:, cols]
            dv = r * (t - v * (r * r * head_mean(t * v, b.ones[...])))
            total += jnp.sum(dy * (v * r), 0, keepdims=True)
            if chunk >= 4:
                dv = jnp.where(lanes() < 64, dv, up)
            b.dp2[m * 128 : m * 128 + 128, cols] = low(dv)
        b.d_qk[chunk : chunk + 1] = total
    for copy in attn_loads:
        copy.wait()

    def back2(cols):
        b.partial[:, cols] = times_transposed(b.dp2[...], b.proj[cols, :1024])

    by_columns(1024, back2)
    swap = moves.sibling(b.partial, b.other2)

    ci_loads = [
        moves.local(w.at[:, pl.ds(2304, 768)], b.proj.at[:, pl.ds(i * 768, 768)])
        for i, w in enumerate((b.w0, b.w1))
    ]
    staged(
        moves,
        b.normed_t,
        lambda k: b.dp2[:, k * 256 : k * 256 + 256],
        slots(b.su, b.sd),
        places(b.grad0, 3072, 2) + places(b.grad1, 3072, 2),
    )
    swap.wait_recv()
    norm_back_rows(b.z, b.gains[2:3], (b.partial, b.other2), b.dh2, b.dz, b.d_mix1)
    ring.forward(0)

    norm_rows(b.h1, b.gains[1:2], b.normed)
    transpose_into(b.normed, b.normed_t)
    transpose_into(b.dz, b.turned)
    moves.done(swap)
    moves.flush()
    ffn_loop(
        b,
        [w.at[:, pl.ds(0, 2304)] for w in (b.w0, b.w1, b.w2)],
        [w.at[:, pl.ds(0, 2304)] for w in (b.grad0, b.grad1, b.grad2)],
        b.normed, b.normed_t, b.dz, b.turned, b.partial,
    )
    swap = moves.sibling(b.partial, b.other0)
    ring.finish(0)
    ring.start(1)
    swap.wait_recv()
    norm_back_rows(b.h1, b.gains[1:2], (b.partial, b.other0), b.dz, b.dh1, b.d_ffn0)

    def rounded0(rows):
        b.do[rows] = low(b.dh1[rows])

    by_rows(256, rounded0)
    mo0_load.wait()
    p1_load.wait()

    def mixed(i, carry):
        rows = pl.ds(pl.multiple_of(core * 512 + i * 128, 128), 128)
        cols = pl.ds(pl.multiple_of(i * 128, 128), 128)
        middle_cols = pl.ds(pl.multiple_of(512 + i * 128, 128), 128)
        dm = times_transposed(b.do[...], b.mo[rows, :])
        taps = b.taps[:, cols]
        for m in range(2):
            part = slice(m * 128, m * 128 + 128)
            conv = sum(taps[j : j + 1] * b.pad[m, 6 + j : 134 + j, cols] for j in range(3))
            b.dp1[part, middle_cols] = low(dm[part] * conv)
            b.dconv[m, :128, cols] = dm[part] * b.p1[part, middle_cols]
        return carry

    lax.fori_loop(0, 4, mixed, 0)
    rim = moves.remote(b.dconv.at[:, pl.ds(0, 8)], b.rim, {SQ: lax.rem(seq + 7, 8)})
    transpose_into(b.m1, b.turned)
    staged(moves, b.turned, own_do, slots(b.sg), places(b.grad2, 2304, 2))
    norm_rows(b.x, b.gains[0:1], b.normed)
    transpose_into(b.normed, b.normed_t)
    ring.forward(1)
    rim.wait_recv()
    b.dconv[:, 128:] = jnp.where(seq < 7, b.rim[...], 0.0)
    b.d_taps[...] = jnp.zeros_like(b.d_taps)

    def conv_back(i, carry):
        cols = pl.ds(pl.multiple_of(i * 128, 128), 128)
        last_cols = pl.ds(pl.multiple_of(1024 + i * 128, 128), 128)
        taps = b.taps[:, cols]
        for m in range(2):
            part = slice(m * 128, m * 128 + 128)
            dconv = b.dconv[m, :128, cols]
            for j in range(3):
                b.d_taps[j : j + 1, cols] += jnp.sum(dconv * b.pad[m, 6 + j : 134 + j, cols], 0, keepdims=True)
            dbx = sum(taps[2 - j : 3 - j] * b.dconv[m, j : 128 + j, cols] for j in range(3))
            b.dp1[part, cols] = low(dbx * b.p1[part, last_cols])
            b.dp1[part, last_cols] = low(dbx * b.p1[part, cols])
        return carry

    lax.fori_loop(0, 4, conv_back, 0)
    for copy in ci_loads:
        copy.wait()
    moves.done(swap)

    def back1(cols):
        b.partial[:, cols] = times_transposed(b.dp1[...], b.proj[cols, :])

    by_columns(1024, back1)
    swap = moves.sibling(b.partial, b.other2)

    staged(
        moves,
        b.normed_t,
        lambda k: b.dp1[:, k * 256 : k * 256 + 256],
        slots(b.su, b.sd, b.wg),
        places(b.grad0, 2304, 3) + places(b.grad1, 2304, 3),
    )
    ring.finish(1)
    ring.start(2)
    swap.wait_recv()
    norm_back_rows(b.x, b.gains[0:1], (b.partial, b.other2), b.dh1, b.dx, b.d_mix0)
    ring.forward(2)
    ring.finish(2)
    ring.settle()
    moves.settle()


def backward(x, gains, qk, cosine, sine, ones, taps, wide, saved, mid):
    full = (4, 2, 4, 2, 16, 2304)
    partial_gain = ((8, 1024), F32, VM)
    widths = (2304,) * 3
    bufs = scatter_scratch(widths)
    ring = {chr(97 + i // 9) + str(i % 9): s for i, s in enumerate(bufs)}

    def body(b):
        b.ring = [getattr(b, name) for name in ring]
        backward_kernel(b)

    return launch(
        body,
        "backward",
        3,
        dict(
            x=(x, VM), gains=(gains, VM), qk=(qk, VM), cosine=(cosine, VM), sine=(sine, VM),
            ones=(ones, VM), taps=(taps, VM), dh2=(mid.dh2, VM), att=(saved.att_out, VM), z=(saved.z_out, VM),
            h1=(saved.h1_out, VM), m1=(saved.m1_out, VM), pad=(saved.pad_out, VM),
            w0=(wide[0], ANY), w1=(wide[1], ANY), w2=(wide[2], ANY),
            mo0_in=(saved.mo0_out, ANY), mo1_in=(saved.mo1_out, ANY), packed_in=(saved.packed_out, ANY),
            p2_in=(saved.p2_out, ANY), p1_in=(saved.p1_out, ANY),
            rg=(mid.gg.reshape(full), ANY), ru=(mid.gu.reshape(full), ANY), rd=(mid.gd.reshape(full), ANY),
        ),
        dict(
            grad0=((1024, 3584), BF, ANY), grad1=((1024, 3584), BF, ANY), grad2=((1024, 3328), BF, ANY),
            d_qk=((8, 128), F32, VM), d_mix1=partial_gain, d_ffn0=partial_gain, d_mix0=partial_gain,
            d_taps=((8, 512), F32, VM), dx=((256, 1024), BF, VM),
            sum_g=((16, 2304), F32, VM), sum_u=((16, 2304), F32, VM), sum_d=((16, 2304), F32, VM),
        ),
        dict(
            mo=bf(1024, 1024), proj=bf(1024, 1536),
            packed=bf(8, 128, 256), p2=vm(256, 1024), p1=vm(256, 1536), do=bf(256, 1024),
            out_att=bf(8, 128, 128), d_att=bf(8, 128, 128), turned=bf(1024, 256), dkv=vm(1024, 128), out=bf(8, 128, 256),
            d_packed=bf(8, 128, 256), normed=bf(256, 1024), normed_t=bf(1024, 256), dp2=bf(256, 1024),
            partial=vm(256, 1024), other2=vm(256, 1024), other0=vm(256, 1024),
            dz=bf(256, 1024), dh1=vm(256, 1024), dp1=bf(256, 1536), dconv=vm(2, 136, 512), rim=vm(2, 8, 512),
            local=dma(32), send=dma(24), recv=dma(24), ssend=dma(54), srecv=dma(54), sload=dma(27),
            **ffn_scratch(), **ring,
        ),
    )


def low(v):
    return v.astype(BF)


def matmul(left, right):
    return jnp.dot(left, right, preferred_element_type=F32)


def times_transposed(left, right):
    return lax.dot_general(left, right, (((1,), (1,)), ((), ())), preferred_element_type=F32)


def transposed_times(left, right):
    return lax.dot_general(left, right, (((0,), (0,)), ((), ())), preferred_element_type=F32)


def swapped(value):
    return lax.ppermute(value, S, [(0, 1), (1, 0)])


def core_half(value, which, axis=1):
    size = value.shape[axis] // 2
    return lax.dynamic_slice_in_dim(value, which * size, size, axis)


def row_homes(turn):
    pairs = []
    for s in range(2):
        for i in range(64):
            core = (i % 2) ^ turn
            pairs.append((s * 64 + i, core * 64 + s * 32 + i // 2))
    return pairs


def mixer_halves(conv_in, qkv):
    def half(core):
        b = conv_in.reshape(8, 3, 2, 512)
        b = lax.dynamic_index_in_dim(b, core, 2, False).reshape(8, 1536)
        q = core_half(qkv[:, :1024], core)
        k = core_half(qkv[:, 1024:1536], core).reshape(8, 4, 64)
        v = core_half(qkv[:, 1536:], core).reshape(8, 4, 64)
        return jnp.concatenate([b, q, jnp.concatenate([k, v], 2).reshape(8, 512)], 1)

    odd = lax.axis_index(SQ) % 2
    got = [
        lax.ppermute(half(jnp.bitwise_xor(odd, turn)), (S, DP, SQ), row_homes(turn))
        for turn in range(2)
    ]
    first = lax.axis_index(S) == 0
    return jnp.concatenate([jnp.where(first, got[0], got[1]), jnp.where(first, got[1], got[0])], 0)


def mixer_homes(grads):
    core = lax.axis_index(S)
    got = []
    for turn in range(2):
        parity = jnp.bitwise_xor(core, turn)
        rows = lax.dynamic_slice_in_dim(grads, parity * 8, 8, 0)
        got.append(lax.ppermute(rows, (S, DP, SQ), [(b, a) for a, b in row_homes(turn)]))
    even = lax.axis_index(SQ) % 2 == 0
    lower = jnp.where(even, got[0], got[1])
    upper = jnp.where(even, got[1], got[0])
    both = jnp.stack([lower, upper], 1)
    conv = both[:, :, :1536].reshape(8, 2, 3, 512).transpose(0, 2, 1, 3).reshape(8, 3072)

    kv = both[:, :, 2048:].reshape(8, 2, 4, 2, 64).transpose(0, 3, 1, 2, 4).reshape(8, 1024)
    return conv, jnp.concatenate([both[:, :, 1536:2048].reshape(8, 1024), kv], 1)


def rope_tables():
    positions = (lax.axis_index(SQ) * 128 + jnp.arange(128)).astype(F32)
    frequency = 1000000.0 ** (-jnp.arange(32).astype(F32) * 2.0 / 64)
    angles = positions[:, None] * frequency[None, :]
    cosine, sine = jnp.cos(angles), jnp.sin(angles)
    return jnp.concatenate([cosine] * 4, 1), jnp.concatenate([-sine, sine] * 2, 1)


def shards(
    inputs,
    cotangent,
    conv_in,
    conv_kernel,
    qkv_weight,
    qk_gain,
    mix_gain,
    ffn_gain,
    mix_out,
    w_gate,
    w_up,
    w_down,
):
    core = lax.axis_index(S)
    first = core == 0
    x = inputs.reshape(256, 1024)
    cot = cotangent.reshape(256, 1024)
    gains = lax.all_gather(jnp.concatenate([mix_gain, ffn_gain], 0), S).astype(F32)
    qk = qk_gain.astype(F32)

    own = [mix_out[0], w_gate[0], w_up[0], w_down[0].T]
    keep = jnp.concatenate([core_half(w, core) for w in own], 1)
    got = swapped(jnp.concatenate([core_half(w, 1 - core) for w in own], 1))
    block0, block1 = jnp.where(first, keep, got), jnp.where(first, got, keep)
    cuts = (512, 2816, 5120)
    mo0, g0, u0, d0 = jnp.split(block0, cuts, 1)
    mo1, g1, u1, d1 = jnp.split(block1, cuts, 1)
    mixers = mixer_halves(conv_in, qkv_weight)
    ci, qw = mixers[:, :1536], mixers[:, 1536:]
    taps = jnp.pad(conv_kernel, ((0, 13), (0, 120)))
    early = [
        jnp.concatenate([g0, ci[:, :768], qw[:, :512]], 1),
        jnp.concatenate([u0, ci[:, 768:], qw[:, 512:]], 1),
        jnp.concatenate([d0, mo0, mo1, taps], 1),
    ]
    wide = [b.reshape(1024, -1) for b in gathered(early, 0)]
    taps = wide[2][:, 3328:].reshape(64, 16, 128)[:, :3, :8].transpose(1, 0, 2).reshape(3, 512)
    taps = jnp.pad(taps.astype(F32), ((0, 5), (0, 0)))
    gains = jnp.pad(jnp.stack([gains[0, 0], gains[0, 1], gains[1, 0], gains[1, 1]]), ((0, 4), (0, 0)))
    kv_gain = jnp.concatenate([qk[1], jnp.ones((64,), F32)])
    qk_row = jnp.concatenate([jnp.tile(qk[0], 8), jnp.tile(kv_gain, 4)])[None]
    cosine, sine = rope_tables()
    lane = jnp.arange(128)
    ones = ((lane[:, None] // 64) == (lane[None, :] // 64)).astype(F32) / 64.0
    common = (x, gains, qk_row, cosine, sine, ones, taps, wide)
    saved = forward(*common, (g1, u1, d1))
    mid = middle(saved.h2_out, cot, gains, saved)
    back = backward(*common, saved, mid)

    taps_grad = jnp.pad(back.d_taps[:3].reshape(3, 64, 8).transpose(1, 0, 2), ((0, 0), (0, 13), (0, 120)))
    parts = [back.grad0, back.grad1, jnp.concatenate([back.grad2, low(taps_grad.reshape(1024, 128))], 1)]
    d_mix0, d_ffn0, d_mix1, d_ffn1 = [
        jnp.sum(g, 0) for g in (back.d_mix0, back.d_ffn0, back.d_mix1, mid.d_ffn)
    ]
    d_gains = jnp.stack([jnp.where(first, d_mix0, d_mix1), jnp.where(first, d_ffn0, d_ffn1)])
    d_q = jnp.sum(back.d_qk[:4].reshape(8, 64), 0)
    d_qk = jnp.concatenate([d_q, jnp.sum(back.d_qk[4:, :64], 0)])[None]
    small = jnp.concatenate([d_gains.reshape(16, 128), jnp.pad(d_qk, ((0, 7), (0, 0)))], 0)
    *sums, small = scattered(parts, 4, small)

    block0 = [sums[2][:, 2304:2816], sums[0][:, :2304], sums[1][:, :2304], sums[2][:, :2304]]
    block1 = [sums[2][:, 2816:3328]] + [back.sum_g, back.sum_u, back.sum_d]
    block0, block1 = jnp.concatenate(block0, 1), jnp.concatenate(block1, 1)
    mine = jnp.where(first, block0, block1)
    theirs = swapped(jnp.where(first, block1, block0))
    lower = jnp.split(jnp.where(first, mine, theirs), cuts, 1)
    upper = jnp.split(jnp.where(first, theirs, mine), cuts, 1)
    mo_grad, g_grad, u_grad, d_grad = [jnp.concatenate(p, 1) for p in zip(lower, upper)]
    mixers = jnp.concatenate([sums[0][:, 2304:3072], sums[1][:, 2304:3072], sums[0][:, 3072:], sums[1][:, 3072:]], 1)
    conv_in_grad, qkv_grad = mixer_homes(mixers)
    return (
        mid.result.reshape(2, 1, 128, 512),
        core_half(back.dx, core).reshape(2, 1, 128, 512),
        conv_in_grad,
        sums[2][:3, 3328:3336],
        qkv_grad,
        small[16].reshape(2, 64),
        small[:8].reshape(1, 1024),
        small[8:16].reshape(1, 1024),
        mo_grad[None],
        g_grad[None],
        u_grad[None],
        d_grad.T[None],
    )


def solution(mesh):
    every = (S, DP, SQ)
    weight = P(S, (DP, SQ), None)
    tokens = P(None, DP, SQ, None)
    in_specs = (
        tokens,
        tokens,
        P(every, None),
        P(None, every),
        P(every, None),
        P(),
        P(S, None),
        P(S, None),
        weight,
        weight,
        weight,
        P(S, None, (DP, SQ)),
    )
    tokens = P(None, DP, SQ, S)
    out_specs = (
        tokens,
        tokens,
        P(every, None),
        P(None, every),
        P(every, None),
        P(),
        P(S, None),
        P(S, None),
        weight,
        weight,
        weight,
        P(S, None, (DP, SQ)),
    )
    return jax.shard_map(shards, mesh=mesh, in_specs=in_specs, out_specs=out_specs, check_vma=False)
```

```python
import functools

import jax
import jax.numpy as jnp
from jax import lax
from jax.experimental import pallas as pl
from jax.experimental.pallas import tpu as pltpu
from jax.sharding import PartitionSpec as P

EPSILON = 1e-05
S, DP, SQ = "section", "dp", "seq"
MESH = pl.DeviceIdType.MESH
ANY = pl.BlockSpec(memory_space=pl.ANY)
BF, F32 = jnp.bfloat16, jnp.float32
ORDERS = ((0, 1, 2), (1, 2, 0), (2, 0, 1))
MIB = 2**20


def chip():
    dp, sq = lax.axis_index(DP), lax.axis_index(SQ)
    return (dp // 2, 2 * (sq % 2) + dp % 2, sq // 2)


def device_at(place):
    x, y, z = place
    return {DP: x * 2 + y % 2, SQ: z * 2 + y // 2}


def moved(place, axis, by):
    return tuple((v + by) % 4 if i == axis else v for i, v in enumerate(place))


def spot(place, kept=(0, 1, 2)):
    x, y, z = place

    def one(axis, value, take):
        if axis not in kept:
            return 0
        return slice(None) if value is None else take(value)

    return (
        one(0, x, lambda v: v),
        one(1, y, lambda v: v % 2),
        one(2, z, lambda v: v),
        one(1, y, lambda v: v // 2),
    )


def halves(width):
    first = (width // 256) * 128
    return (pl.ds(0, first), pl.ds(first, width - first))


def greet(devices):
    barrier = pltpu.get_barrier_semaphore()
    for device in devices:
        pl.semaphore_signal(barrier, inc=1, device_id=device, device_id_type=MESH)
    pl.semaphore_wait(barrier, len(devices))


def neighbours():
    here = chip()
    return [device_at(moved(here, axis, by)) for axis in range(3) for by in (1, -1)]


class Gather:
    def __init__(self, bufs, send, recv):
        self.bufs, self.send, self.recv = bufs, send, recv
        self.here = chip()

    def copy(self, colour, phase, kind):
        order = ORDERS[colour]
        axis, done = order[phase], order[:phase]
        buf = self.bufs[colour]
        half = halves(buf.shape[-1])
        step, part, to = ((0, 0, 1), (0, 1, 1), (0, 1, -1), (0, 0, -1), (-1, 0, 1), (1, 1, -1))[kind]
        source = moved(self.here, axis, step)
        block = tuple(None if i in done else v for i, v in enumerate(source))
        ref = buf.at[spot(block) + (slice(None), half[part])]
        slot = (colour * 3 + phase) * 6 + kind
        return pltpu.make_async_remote_copy(
            src_ref=ref,
            dst_ref=ref,
            send_sem=self.send.at[slot],
            recv_sem=self.recv.at[slot],
            device_id=device_at(moved(self.here, axis, to)),
            device_id_type=MESH,
        )

    def start(self, phase):
        for pair in ((0, 2), (1, 3)):
            for kind in pair:
                for colour in range(3):
                    self.copy(colour, phase, kind).start()

    def forward(self, phase):
        for got, then in ((0, 4), (2, 5)):
            for colour in range(3):
                self.copy(colour, phase, got).wait_recv()
                self.copy(colour, phase, then).start()

    def finish(self, phase):
        for kind in (1, 3, 4, 5):
            for colour in range(3):
                self.copy(colour, phase, kind).wait_recv()

    def settle(self):
        for phase in range(3):
            for kind in range(6):
                for colour in range(3):
                    self.copy(colour, phase, kind).wait_send()


def lead(kept):
    return (4 if 0 in kept else 1, 2 if 1 in kept else 1, 4 if 2 in kept else 1, 2 if 1 in kept else 1)


def one_block(place, axis):
    x, y, z = place
    every = slice(None)
    return (
        pl.ds(x, 1) if axis == 0 else every,
        pl.ds(y % 2, 1) if axis == 1 else every,
        pl.ds(z, 1) if axis == 2 else every,
        pl.ds(y // 2, 1) if axis == 1 else every,
        every,
    )


def scatter_scratch(widths):
    shapes = []
    for colour, width in enumerate(widths):
        for phase in range(3):
            rows = lead(ORDERS[colour][phase + 1 :]) + (16,)
            pair = [rows + (h.size,) for h in halves(width)]
            shapes += [rows + (width,)] + pair + pair + [rows + (width,)] * 2
    return [pltpu.VMEM(s, BF) for s in shapes]


class Scatter:
    def __init__(self, parts, bufs, results, send, recv, load):
        self.parts, self.results = parts, results
        self.bufs = [[bufs[(c * 3 + p) * 7 :][:7] for p in range(3)] for c in range(3)]
        self.send, self.recv, self.load = send, recv, load
        self.here = chip()

    def source(self, colour, phase, by, half=None):
        axis = ORDERS[colour][phase]
        ref = self.parts[colour] if phase == 0 else self.bufs[colour][phase - 1][0]
        half = slice(None) if half is None else half
        return ref.at[one_block(moved(self.here, axis, by), axis) + (half,)]

    def loads(self, colour, phase):
        half = halves(self.parts[colour].shape[-1])
        own, ahead0, ahead1 = self.bufs[colour][phase][:3]
        pairs = (
            (self.source(colour, phase, 1, half[0]), ahead0),
            (self.source(colour, phase, -1, half[1]), ahead1),
            (self.source(colour, phase, 0), own),
        )
        return [
            functools.partial(pltpu.make_async_copy, a, b, self.load.at[(colour * 3 + phase) * 3 + i])
            for i, (a, b) in enumerate(pairs)
        ]

    def copy(self, colour, phase, kind):
        half = halves(self.parts[colour].shape[-1])
        own, ahead0, ahead1, first0, first1, last0, last1 = self.bufs[colour][phase]
        side = kind % 2
        to = (1, -1)[side]
        last = (last0, last1)[side]
        if kind < 2:
            src, dst = self.source(colour, phase, 2, half[side]), (first0, first1)[side]
        elif kind < 4:
            src, dst = self.source(colour, phase, to, half[1 - side]), last.at[..., half[1 - side]]
        else:
            src, dst = (ahead0, ahead1)[side], last.at[..., half[side]]
        slot = (colour * 3 + phase) * 6 + kind
        return pltpu.make_async_remote_copy(
            src_ref=src,
            dst_ref=dst,
            send_sem=self.send.at[slot],
            recv_sem=self.recv.at[slot],
            device_id=device_at(moved(self.here, ORDERS[colour][phase], to)),
            device_id_type=MESH,
        )

    def start(self, phase):
        for kind in range(4):
            for colour in range(3):
                self.copy(colour, phase, kind).start()
        for colour in range(3):
            for load in self.loads(colour, phase):
                load().start()

    def forward(self, phase):
        for side in range(2):
            for colour in range(3):
                self.loads(colour, phase)[side]().wait()
                self.copy(colour, phase, side).wait_recv()
                bufs = self.bufs[colour][phase]
                added(bufs[1 + side], (bufs[3 + side],), bufs[1 + side])
                self.copy(colour, phase, 4 + side).start()

    def finish(self, phase):
        for colour in range(3):
            self.loads(colour, phase)[2]().wait()
            for kind in range(2, 6):
                self.copy(colour, phase, kind).wait_recv()
            bufs = self.bufs[colour][phase]
            if phase < 2:
                added(bufs[0], (bufs[5], bufs[6]), bufs[0])
            else:
                added(bufs[0], (bufs[5], bufs[6]), self.results[colour])

    def settle(self):
        for phase in range(3):
            for kind in range(6):
                for colour in range(3):
                    self.copy(colour, phase, kind).wait_send()


def added(base, others, out):
    sizes = base.shape[:4]
    _, b, c, d = sizes

    def step(i, carry):
        at = (i // (b * c * d), (i // (c * d)) % b, (i // d) % c, i % d)
        total = base[at].astype(F32)
        for other in others:
            total = total + other[at].astype(F32)
        if len(out.shape) == 2:
            out[...] = total.astype(out.dtype)
        else:
            out[at] = total.astype(out.dtype)
        return carry

    lax.fori_loop(0, sizes[0] * b * c * d, step, 0)


class Small:
    def __init__(self, sums, other, slots, send, recv):
        self.sums, self.other, self.slots = sums, other, slots
        self.send, self.recv = send, recv
        self.here = chip()

    def sibling(self, source):
        return pltpu.make_async_remote_copy(
            src_ref=source,
            dst_ref=self.other,
            send_sem=self.send.at[9],
            recv_sem=self.recv.at[9],
            device_id={S: 1 - lax.axis_index(S)},
            device_id_type=MESH,
        )

    def copy(self, phase, by):
        slot = phase * 3 + by - 1
        return pltpu.make_async_remote_copy(
            src_ref=self.sums.at[phase],
            dst_ref=self.slots.at[slot],
            send_sem=self.send.at[slot],
            recv_sem=self.recv.at[slot],
            device_id=device_at(moved(self.here, phase, by)),
            device_id_type=MESH,
        )

    def start(self, phase):
        for by in (1, 2, 3):
            self.copy(phase, by).start()

    def finish(self, phase):
        for by in (1, 2, 3):
            self.copy(phase, by).wait_recv()
        one, two, three = [self.slots[phase * 3 + i] for i in range(3)]
        self.sums[phase + 1] = (self.sums[phase] + two) + (one + three)

    def settle(self):
        for phase in range(3):
            for by in (1, 2, 3):
                self.copy(phase, by).wait_send()


class Bag:
    def __init__(self, **items):
        self.__dict__.update(items)


def launch(body, name, cid, ins, outs, scratch):
    def kernel(*refs):
        body(Bag(**dict(zip([*ins, *outs, *scratch], refs))))

    got = pl.pallas_call(
        kernel,
        name=name,
        out_shape=[jax.ShapeDtypeStruct(shape, dtype) for shape, dtype, _ in outs.values()],
        in_specs=[where for _, where in ins.values()],
        out_specs=[where for _, _, where in outs.values()],
        scratch_shapes=list(scratch.values()),
        compiler_params=pltpu.CompilerParams(
            collective_id=cid, has_side_effects=True, vmem_limit_bytes=60 * MIB
        ),
    )(*[value for value, _ in ins.values()])
    return Bag(**dict(zip(outs, got)))


VM = pl.BlockSpec(memory_space=pltpu.VMEM)


def vm(*shape, dtype=F32):
    return pltpu.VMEM(shape, dtype)


class Moves:
    def __init__(self, local, send, recv):
        self.sems = local, send, recv
        self.kept, self.sent = [], []
        self.locals = self.remotes = 0

    def local(self, src, dst):
        copy = pltpu.make_async_copy(src, dst, self.sems[0].at[self.locals])
        self.locals += 1
        copy.start()
        return copy

    def keep(self, src, dst):
        self.kept.append(self.local(src, dst))

    def remote(self, src, dst, device):
        slot = self.remotes
        self.remotes += 1
        copy = pltpu.make_async_remote_copy(
            src_ref=src,
            dst_ref=dst,
            send_sem=self.sems[1].at[slot],
            recv_sem=self.sems[2].at[slot],
            device_id=device,
            device_id_type=MESH,
        )
        copy.start()
        self.sent.append(copy)
        return copy

    def sibling(self, src, dst):
        return self.remote(src, dst, {S: 1 - lax.axis_index(S)})

    def mates(self, src, dst):
        me = lax.axis_index(SQ)
        copies = [self.remote(src(lax.rem(me + j, 8)), dst, {SQ: lax.rem(me + j, 8)}) for j in range(1, 8)]
        return [self.local(src(me), dst)], copies

    def done(self, copy):
        copy.wait_send()
        self.sent = [c for c in self.sent if c is not copy]

    def flush(self):
        for copy in self.kept:
            copy.wait()
        self.kept = []

    def settle(self):
        self.flush()
        for copy in self.sent:
            copy.wait_send()


def arrived(moves):
    own, copies = moves
    for copy in own:
        copy.wait()
    for copy in copies:
        copy.wait_recv()


def mate_devices():
    me = lax.axis_index(SQ)
    return [{SQ: lax.rem(me + j, 8)} for j in range(1, 8)]


def across_devices():
    here = chip()
    return [device_at(moved(here, axis, by)) for axis in range(2) for by in (1, -1)]


def sibling_device():
    return {S: 1 - lax.axis_index(S)}


def by_rows(rows, step, size=32):
    def body(i, carry):
        step(pl.ds(pl.multiple_of(i * size, size), size))
        return carry

    lax.fori_loop(0, rows // size, body, 0)


def by_columns(width, step, size=256):
    def body(i, carry):
        step(pl.ds(pl.multiple_of(i * size, size), size))
        return carry

    lax.fori_loop(0, width // size, body, 0)


def core_columns(size):
    return pl.ds(pl.multiple_of(lax.axis_index(S) * size, size), size)


def inverse_norm(v):
    return lax.rsqrt(jnp.mean(v * v, axis=-1, keepdims=True) + EPSILON)


def norm_rows(src, gain, dst):
    def step(rows):
        v = src[rows].astype(F32)
        dst[rows] = low(v * inverse_norm(v) * gain[...])

    by_rows(256, step)


def norm_back_rows(src, gain, upstreams, residual, out, d_gain):
    d_gain[...] = jnp.zeros_like(d_gain)

    def step(rows):
        v = src[rows].astype(F32)
        up = sum(u[rows] for u in upstreams)
        r = inverse_norm(v)
        t = up * gain[...]
        dv = r * (t - v * (r * r * jnp.mean(t * v, axis=-1, keepdims=True)))
        out[rows] = (residual[rows].astype(F32) + dv).astype(out.dtype)
        scaled = up * (v * r)
        d_gain[...] += scaled[:8] + scaled[8:16] + scaled[16:24] + scaled[24:]

    by_rows(256, step)


def transpose_into(src, dst):
    def step(cols):
        dst[cols, :] = src[:, cols].astype(F32).T.astype(BF)

    by_columns(1024, step, 128)


def lanes(width=128):
    return lax.broadcasted_iota(jnp.int32, (1, width), 1)


def head_mean(v, ones):
    return jnp.dot(v, ones, precision=lax.Precision.HIGHEST, preferred_element_type=F32)


def half_turn(v):
    return jnp.where(lanes() % 64 < 32, pltpu.roll(v, 96, 1), pltpu.roll(v, 32, 1))


def head_lanes(v, head, upper):
    v = v.astype(F32)
    if head != upper:
        v = pltpu.roll(v, 64, 1)
    return jnp.where(lanes() >= 64 if upper else lanes() < 64, v, 0.0)


def block_probs(b, block, head):
    count = 256 * (block + 1)
    q = head_lanes(b.packed[2 * block : 2 * block + 2, :, :128].reshape(256, 128), head, 0)
    kv = b.packed[: 2 * block + 2, :, 128:].reshape(count, 128)
    scores = times_transposed(low(q), kv) * 0.125
    row = lax.broadcasted_iota(jnp.int32, (256, count), 0) + 256 * block
    col = lax.broadcasted_iota(jnp.int32, (256, count), 1)
    e = jnp.exp(jnp.where(row >= col, scores, -1e9))
    return q, kv, e * (1.0 / jnp.sum(e, -1, keepdims=True))


def flat(value):
    return value.reshape(-1, value.shape[-1])


def ring_shape(width):
    return (4, 2, 4, 2, 16, width)


def forward_kernel(b):
    core, seq = lax.axis_index(S), lax.axis_index(SQ)
    greet(across_devices() + mate_devices() + [sibling_device()])
    moves = Moves(b.local, b.send, b.recv)
    here = spot(chip())
    half, other_half = core_columns(512), pl.ds(pl.multiple_of(512 - core * 512, 512), 512)

    mine = pl.ds(pl.multiple_of(core * 8, 8), 8)
    waits = [
        moves.local(b.mix_in.at[core], b.mix.at[mine]),
        moves.local(b.gains_in, b.gains.at[core]),
        moves.local(b.taps_in, b.mt.at[here + (slice(None), pl.ds(512, 128))]),
    ]
    swaps = [
        moves.sibling(b.mix_in.at[1 - core], b.mix.at[mine]),
        moves.sibling(b.gains_in, b.gains.at[core]),
    ]
    shards = (
        (b.wg, 2304, (b.gate0, b.gate1)),
        (b.wu, 2304, (b.up0, b.up1)),
        (b.wd, 2304, (b.down0, b.down1)),
        (b.mo, 512, (b.mt, b.mo1)),
    )

    def trade(k, block):
        w, n, homes = shards[k]
        home = homes[block].at[here + (slice(None), pl.ds(0, n))]
        keep = pltpu.make_async_copy(w.at[:, pl.ds(block * n, n)], home, b.trade.at[k])
        give = pltpu.make_async_remote_copy(
            src_ref=w.at[:, pl.ds((1 - block) * n, n)],
            dst_ref=home,
            send_sem=b.trade.at[4 + k],
            recv_sem=b.trade.at[8 + k],
            device_id=sibling_device(),
            device_id_type=MESH,
        )
        return keep, give

    for block in range(2):

        @pl.when(core == block)
        def _():
            for k in (3, 0, 1, 2):
                for copy in trade(k, block):
                    copy.start()

    perm_load = moves.local(b.perm_in, b.perm)
    for copy in waits:
        copy.wait()
    for copy in swaps:
        copy.wait_recv()
    b.ci0[here] = low(b.mix[:, :768])
    b.ci1[here] = low(b.mix[:, 768:1536])
    b.qw0[here] = low(b.mix[:, 1536:2048])
    b.qw1[here] = low(b.mix[:, 2048:])
    for k in (3, 0, 1, 2):
        keep, give = trade(k, 0)
        keep.wait()
        give.wait_recv()
    moves.keep(b.gains, b.gains_out)

    rings = [
        Gather(bufs, b.gsend.at[i], b.grecv.at[i])
        for i, bufs in enumerate(
            (
                (b.ci0, b.ci1, b.mt),
                (b.gate0, b.up0, b.down0),
                (b.qw0, b.qw1, b.mo1),
                (b.gate1, b.up1, b.down1),
            )
        )
    ]
    ring_a, ring_b, ring_c, ring_d = rings
    for ring in rings:
        ring.start(0)
    norm_rows(b.x, b.gains.at[0, 0:1], b.normed)
    perm_load.wait()
    permuted(b.normed, b.perm, b.turned)
    for ring in rings:
        ring.forward(0)
    ring_a.finish(0)
    ring_a.start(1)
    ring_b.finish(0)
    ring_b.start(1)
    ring_a.forward(1)
    ring_a.finish(1)
    ring_a.start(2)
    ring_b.forward(1)
    ring_c.finish(0)
    ring_c.start(1)
    ring_a.forward(2)
    ring_b.finish(1)
    ring_b.start(2)
    ring_a.finish(2)

    def other_mo(source, target):
        return moves.sibling(source.at[..., pl.ds(0, 512)], target)

    mo0_swap = other_mo(b.mt, b.mo0_other)
    ring_d.finish(0)
    ring_d.start(1)
    for x in range(4):
        rows = flat(b.mt[x, :, :, :, :, 512:]).reshape(16, 16, 128)
        b.taps[:, x * 128 : x * 128 + 128] = jnp.sum(rows.astype(F32), 0)[:8]
    for i, ci in enumerate((b.ci0, b.ci1)):
        for j in range(3):
            cols = slice(j * 256, j * 256 + 256)
            b.p1[:, i * 768 + j * 256 : i * 768 + j * 256 + 256] = matmul(b.turned[...], flat(ci[..., cols]))
    moves.keep(b.p1, b.p1_out)
    ring_c.forward(1)

    def gated(rows):
        b.bx[rows] = low(b.p1[rows, :512] * b.p1[rows, 1024:]).astype(F32)

    by_rows(256, gated)
    for m in range(2):
        b.pad[m, 8:] = b.bx[m * 128 : m * 128 + 128]
    rim = moves.remote(b.pad.at[:, pl.ds(128, 8)], b.rim, {SQ: lax.rem(seq + 1, 8)})
    ring_c.finish(1)
    ring_c.start(2)
    ring_d.forward(1)
    rim.wait_recv()
    b.pad[:, :8] = jnp.where(seq > 0, b.rim[...], 0.0)
    moves.keep(b.pad, b.pad_out)

    def convolve(cols):
        taps = b.taps[:, cols]
        for m in range(2):
            conv = sum(taps[j : j + 1] * b.pad[m, 6 + j : 134 + j, cols] for j in range(3))
            rows = slice(m * 128, m * 128 + 128)
            gate = b.p1[rows, pl.ds(pl.multiple_of(cols.start + 512, 128), 128)]
            b.m1[rows, pl.ds(pl.multiple_of(core * 512 + cols.start, 128), 128)] = low(gate * conv)

    by_columns(512, convolve, 128)
    swap = moves.sibling(b.m1.at[:, half], b.m1.at[:, half])
    ring_b.forward(2)
    ring_d.finish(1)
    swap.wait_recv()
    moves.keep(b.m1, b.m1_out)
    moves.keep(b.taps, b.taps_out)
    mo0_swap.wait_recv()
    b.h1[:, half] = b.x[:, half].astype(F32) + matmul(b.m1[...], flat(b.mt[..., :512]))
    b.h1[:, other_half] = b.x[:, other_half].astype(F32) + matmul(b.m1[...], flat(b.mo0_other[...]))
    moves.keep(b.h1, b.h1_out)
    norm_rows(b.h1, b.gains.at[0, 1:2], b.normed)
    ring_b.finish(2)
    ring_d.start(2)
    ring_c.forward(2)

    def hidden(cols):
        g = matmul(b.normed[...], flat(b.gate0[..., cols]))
        u = matmul(b.normed[...], flat(b.up0[..., cols]))
        b.active[:, cols] = low(g / (1.0 + jnp.exp(-g)) * u)

    by_columns(2304, hidden)

    def contract(x, carry):
        cols = pl.ds(pl.multiple_of(x * 256, 256), 256)
        b.f[:, cols] = times_transposed(b.active[...], flat(b.down0[x]))
        return carry

    lax.fori_loop(0, 4, contract, 0)
    swap = moves.sibling(b.f, b.f_other)
    ring_c.finish(2)
    mo1_swap = other_mo(b.mo1, b.mo1_other)
    swap.wait_recv()

    def passed(rows):
        b.z[rows] = low(b.h1[rows] + (b.f[rows] + b.f_other[rows]))

    by_rows(256, passed)
    moves.keep(b.z, b.z_out)

    norm_rows(b.z, b.gains.at[1, 0:1], b.normed)
    permuted(b.normed, b.perm, b.turned)
    for i, qw in enumerate((b.qw0, b.qw1)):
        for j in range(2):
            cols = slice(j * 256, j * 256 + 256)
            b.p2[:, i * 512 + j * 256 : i * 512 + j * 256 + 256] = matmul(b.turned[...], flat(qw[..., cols]))
    moves.keep(b.p2, b.p2_out)
    for chunk in range(8):
        cols = slice(chunk * 128, chunk * 128 + 128)
        head, place = chunk % 4, pl.ds(chunk // 4 * 128, 128)
        for m in range(2):
            v = b.p2[m * 128 : m * 128 + 128, cols]
            y = v * lax.rsqrt(head_mean(v * v, b.ones[...]) + EPSILON) * b.qk[:, cols]
            y = y * b.cosine[...] + half_turn(y) * b.sine[...]
            if chunk >= 4:
                y = jnp.where(lanes() < 64, y, v)
            b.out[m * 4 + head, :, place] = low(y)
    exchange = moves.mates(lambda j: b.out.at[j], b.packed.at[seq])
    for ring_out, ref in (
        (b.ci0_out, b.ci0), (b.ci1_out, b.ci1), (b.gate0_out, b.gate0), (b.up0_out, b.up0),
        (b.down0_out, b.down0), (b.qw0_out, b.qw0), (b.qw1_out, b.qw1),
    ):
        moves.keep(ref, ring_out)
    arrived(exchange)
    moves.keep(b.packed, b.packed_out)
    ring_d.forward(2)
    for block in range(4):
        results = []
        for head in range(2):
            _, kv, probs = block_probs(b, block, head)
            results.append(matmul(low(probs), kv))
        joint = jnp.where(lanes() < 64, pltpu.roll(results[0], 64, 1), results[1])
        b.att_rows[2 * block : 2 * block + 2] = low(joint).reshape(2, 128, 128)
    rows = pl.ds(pl.multiple_of(seq // 4 * 128, 128), 128)
    cols = pl.ds(pl.multiple_of(core * 512 + seq % 4 * 128, 128), 128)
    exchange = moves.mates(lambda j: b.att_rows.at[j], b.att.at[rows, cols])
    mo1_swap.wait_recv()
    for out, own, other in ((b.mo0_out, b.mt, b.mo0_other), (b.mo1_out, b.mo1, b.mo1_other)):
        moves.keep(own.at[..., pl.ds(0, 512)], out.at[..., half])
        moves.keep(other, out.at[..., other_half])
    arrived(exchange)
    swap = moves.sibling(b.att.at[:, half], b.att.at[:, half])
    swap.wait_recv()
    moves.keep(b.att, b.att_out)
    b.h2[:, half] = b.z[:, half].astype(F32) + matmul(b.att[...], flat(b.mo1[...]))
    b.h2[:, other_half] = b.z[:, other_half].astype(F32) + matmul(b.att[...], flat(b.mo1_other[...]))
    moves.keep(b.h2, b.h2_out)
    ring_d.finish(2)
    for ring in rings:
        ring.settle()
    for k in range(4):
        trade(k, 0)[1].wait_send()
    moves.settle()


def permuted(src, perm, dst):
    def step(cols):
        dst[:, cols] = low(matmul(src[...], perm[:, cols]))

    by_columns(1024, step)


def dma(*count):
    return pltpu.SemaphoreType.DMA(count)


def bf(*shape):
    return pltpu.VMEM(shape, BF)


def forward(x, gains_in, qk, cosine, sine, ones, perm, taps, mix_in, weights):
    def saved(*shape, dtype=BF):
        return (shape, dtype, ANY)

    wide, thin = ring_shape(2304), ring_shape(512)
    wg, wu, wd, mo = weights
    return launch(
        forward_kernel,
        "forward",
        1,
        dict(
            x=(x, VM), gains_in=(gains_in, VM), qk=(qk, VM), cosine=(cosine, VM), sine=(sine, VM), ones=(ones, VM),
            perm_in=(perm, ANY), taps_in=(taps, VM), mix_in=(mix_in, VM),
            wg=(wg, ANY), wu=(wu, ANY), wd=(wd, ANY), mo=(mo, ANY),
        ),
        dict(
            gate1=saved(*wide), up1=saved(*wide), down1=saved(*wide), ci0_out=saved(*ring_shape(768)),
            ci1_out=saved(*ring_shape(768)), gate0_out=saved(*wide), up0_out=saved(*wide),
            down0_out=saved(*wide), qw0_out=saved(*thin), qw1_out=saved(*thin),
            mo0_out=saved(*ring_shape(1024)), mo1_out=saved(*ring_shape(1024)),
            gains_out=saved(2, 8, 1024, dtype=F32), taps_out=saved(8, 512, dtype=F32),
            p1_out=saved(256, 1536, dtype=F32), pad_out=saved(2, 136, 512, dtype=F32),
            m1_out=saved(256, 1024), h1_out=saved(256, 1024, dtype=F32), z_out=saved(256, 1024),
            p2_out=saved(256, 1024, dtype=F32), packed_out=saved(8, 128, 256),
            att_out=saved(256, 1024), h2_out=saved(256, 1024, dtype=F32),
        ),
        dict(
            mix=vm(16, 2560), gains=vm(2, 8, 1024), taps=vm(8, 512), perm=bf(1024, 1024),
            ci0=bf(*ring_shape(768)), ci1=bf(*ring_shape(768)), mt=bf(*ring_shape(640)),
            gate0=bf(*wide), up0=bf(*wide), down0=bf(*wide), qw0=bf(*thin), qw1=bf(*thin), mo1=bf(*thin),
            mo0_other=bf(*thin), mo1_other=bf(*thin),
            normed=bf(256, 1024), turned=bf(256, 1024), p1=vm(256, 1536), bx=vm(256, 512), pad=vm(2, 136, 512),
            rim=vm(2, 8, 512), m1=bf(256, 1024), h1=vm(256, 1024), active=bf(256, 2304),
            f=vm(256, 1024), f_other=vm(256, 1024), z=bf(256, 1024), p2=vm(256, 1024),
            out=bf(8, 128, 256), packed=bf(8, 128, 256), att_rows=bf(8, 128, 128), att=bf(256, 1024),
            h2=vm(256, 1024), local=dma(40), send=dma(28), recv=dma(28), trade=dma(12),
            gsend=dma(4, 54), grecv=dma(4, 54),
        ),
    )


def ffn_scratch():
    return dict(
        wg=bf(2, 1024, 256), wu=bf(2, 1024, 256), wd=bf(2, 1024, 256),
        sg=bf(2, 1024, 256), su=bf(2, 1024, 256), sd=bf(2, 1024, 256),
        load=pltpu.SemaphoreType.DMA((2, 3)), store=pltpu.SemaphoreType.DMA((2, 3)),
    )


def ffn_loop(b, weights, grads, normed, normed_t, df, df_t, da, f=None):
    def columns(i):
        return pl.ds(pl.multiple_of(i * 256, 256), 256)

    def loads(i, slot):
        return [
            pltpu.make_async_copy(w.at[:, columns(i)], d.at[slot], b.load.at[slot, k])
            for k, (w, d) in enumerate(zip(weights, (b.wg, b.wu, b.wd)))
        ]

    def stores(i, slot):
        return [
            pltpu.make_async_copy(s.at[slot], g.at[:, columns(i)], b.store.at[slot, k])
            for k, (g, s) in enumerate(zip(grads, (b.sg, b.su, b.sd)))
        ]

    for copy in loads(0, 0):
        copy.start()
    da[...] = jnp.zeros_like(da)
    if f is not None:
        f[...] = jnp.zeros_like(f)

    def step(i, carry):
        slot = lax.rem(i, 2)
        for copy in loads(i, slot):
            copy.wait()

        @pl.when(i < 8)
        def _():
            for copy in loads(i + 1, 1 - slot):
                copy.start()

        gate, up, down = b.wg.at[slot], b.wu.at[slot], b.wd.at[slot]
        g = matmul(normed[...], gate[...])
        u = matmul(normed[...], up[...])
        ds = matmul(df[...], down[...])
        sig = 1.0 / (1.0 + jnp.exp(-g))
        silu = g * sig
        s = low(silu * u)
        dg = low(ds * u * (sig * (1.0 + g * (1.0 - sig))))
        du = low(ds * silu)
        if f is not None:
            f[...] += times_transposed(s, down[...])
        da[...] += times_transposed(dg, gate[...]) + times_transposed(du, up[...])

        @pl.when(i >= 2)
        def _():
            for copy in stores(i - 2, slot):
                copy.wait()

        b.sg[slot] = low(matmul(normed_t[...], dg))
        b.su[slot] = low(matmul(normed_t[...], du))
        b.sd[slot] = low(matmul(df_t[...], s))
        for copy in stores(i, slot):
            copy.start()
        return carry

    lax.fori_loop(0, 9, step, 0)
    for copy in stores(7, 1) + stores(8, 0):
        copy.wait()


def middle_kernel(b):
    greet([sibling_device()])
    moves = Moves(b.local, b.send, b.recv)
    norm_rows(b.h2, b.gains.at[1, 1:2], b.normed)
    transpose_into(b.normed, b.normed_t)
    transpose_into(b.cot, b.cot_t)
    ffn_loop(
        b, (b.g1, b.u1, b.d1), (b.gg, b.gu, b.gd), b.normed, b.normed_t, b.cot, b.cot_t, b.da, b.f
    )
    half = core_columns(512)
    other = pl.ds(pl.multiple_of(512 - lax.axis_index(S) * 512, 512), 512)
    da_swap = moves.sibling(b.da, b.da_other)
    f_swap = moves.sibling(b.f.at[:, other], b.f_other)
    da_swap.wait_recv()
    norm_back_rows(b.h2, b.gains.at[1, 1:2], (b.da, b.da_other), b.cot, b.dh2, b.d_ffn)
    f_swap.wait_recv()

    def finish(rows):
        b.result[rows] = low(b.h2[rows, half] + (b.f[rows, half] + b.f_other[rows]))

    by_rows(256, finish)
    moves.settle()


def middle(cot, w):
    grad = ((1024, 2304), BF, ANY)
    return launch(
        middle_kernel,
        "middle",
        2,
        dict(
            h2=(w.h2_out, VM), cot=(cot, VM), gains=(w.gains_out, VM),
            g1=(flat(w.gate1), ANY), u1=(flat(w.up1), ANY), d1=(flat(w.down1), ANY),
        ),
        dict(
            gg=grad, gu=grad, gd=grad, dh2=((256, 1024), F32, VM), d_ffn=((8, 1024), F32, VM),
            result=((256, 512), BF, VM),
        ),
        dict(
            normed=bf(256, 1024), normed_t=bf(1024, 256), cot_t=bf(1024, 256), da=vm(256, 1024),
            da_other=vm(256, 1024), f=vm(256, 1024), f_other=vm(256, 512),
            local=dma(2), send=dma(2), recv=dma(2), **ffn_scratch(),
        ),
    )


def staged(moves, left_t, right, slots, dests):
    for k, (slot, dest) in enumerate(zip(slots, dests)):
        slot[...] = low(matmul(left_t[...], right(k)))
        moves.keep(slot, dest)


def slots(*stacks):
    return [stack.at[i] for stack in stacks for i in range(2)]


def places(grad, count):
    return [grad.at[:, pl.ds(256 * k, 256)] for k in range(count)]


def unpermuted(b, mine, theirs, out):
    def step(cols):
        total = mine[:, cols] + theirs[:, cols]
        high = low(total)
        b.high[:, cols] = high
        b.rest[:, cols] = low(total - high.astype(F32))

    by_columns(1024, step)

    def turn(cols):
        out[:, cols] = times_transposed(b.high[...], b.perm[cols, :]) + times_transposed(b.rest[...], b.perm[cols, :])

    by_columns(1024, turn)


def backward_kernel(b):
    core, seq = lax.axis_index(S), lax.axis_index(SQ)
    greet(across_devices() + mate_devices() + [sibling_device()])
    moves = Moves(b.local, b.send, b.recv)
    ring = Scatter((b.rg, b.ru, b.rd), b.ring, (b.sum_g, b.sum_u, b.sum_d), b.ssend.at[0], b.srecv.at[0], b.sload.at[0])
    blocks = [g.reshape(ring_shape(512)) for g in (b.qw0_grad, b.qw1_grad, b.mo1_grad)]
    ring2 = Scatter(blocks, b.ring2, (b.sum_q0, b.sum_q1, b.sum_mo), b.ssend.at[1], b.srecv.at[1], b.sload.at[1])
    ring.start(0)
    mo1_load = moves.local(b.mo1_in, b.mo)
    packed_load = moves.local(b.packed_in, b.packed)
    attn_loads = [
        moves.local(w, b.proj.at[:, pl.ds(i * 512, 512)]) for i, w in enumerate((b.qw0, b.qw1))
    ]
    p2_load = moves.local(b.p2_in, b.p2)
    perm_load = moves.local(b.perm_in, b.perm)

    def rounded(rows):
        b.do[rows] = low(b.dh2[rows])

    by_rows(256, rounded)
    mo1_load.wait()
    for h in range(4):
        rows = pl.ds(pl.multiple_of(core * 512 + h * 128, 128), 128)
        d_att = low(times_transposed(b.do[...], b.mo[rows, :]))
        for m in range(2):
            b.out_att[m * 4 + h] = d_att[m * 128 : m * 128 + 128]
    exchange = moves.mates(lambda j: b.out_att.at[j], b.d_att.at[seq])
    transpose_into(b.att, b.turned)
    staged(moves, b.turned, lambda k: own_columns(b.do, k), slots(b.sg), places(b.mo1_grad, 2))
    packed_load.wait()
    norm_rows(b.z, b.gains.at[1, 0:1], b.normed)
    perm_load.wait()
    permuted(b.normed, b.perm, b.high)
    transpose_into(b.high, b.normed_t)
    arrived(exchange)
    b.dkv[...] = jnp.zeros_like(b.dkv)
    for block in range(4):
        count = 256 * (block + 1)
        results = []
        for head in range(2):
            q, kv, probs = block_probs(b, block, head)
            up = low(head_lanes(b.d_att[2 * block : 2 * block + 2].reshape(256, 128), head, 1))
            dp = times_transposed(up, kv)
            ds = low(probs * (dp - jnp.sum(dp * probs, -1, keepdims=True)))
            b.dkv[:count] += transposed_times(ds, low(q * 0.125)) + transposed_times(low(probs), up)
            results.append(matmul(ds, kv) * 0.125)
        joint = jnp.where(lanes() < 64, results[0], pltpu.roll(results[1], 64, 1))
        b.out[2 * block : 2 * block + 2, :, :128] = low(joint).reshape(2, 128, 128)
    for j in range(8):
        b.out[j, :, 128:] = low(b.dkv[j * 128 : j * 128 + 128])
    exchange = moves.mates(lambda j: b.out.at[j], b.d_packed.at[seq])
    ring.forward(0)
    p2_load.wait()
    arrived(exchange)
    b.d_qk[...] = jnp.zeros_like(b.d_qk)
    for chunk in range(8):
        cols = slice(chunk * 128, chunk * 128 + 128)
        head, place = chunk % 4, slice(chunk // 4 * 128, chunk // 4 * 128 + 128)
        for m in range(2):
            v = b.p2[m * 128 : m * 128 + 128, cols]
            up = b.d_packed[m * 4 + head, :, place].astype(F32)
            r = lax.rsqrt(head_mean(v * v, b.ones[...]) + EPSILON)
            dy = up * b.cosine[...] + half_turn(up * b.sine[...])
            t = dy * b.qk[:, cols]
            dv = r * (t - v * (r * r * head_mean(t * v, b.ones[...])))
            b.d_qk[chunk // 4 : chunk // 4 + 1] += jnp.sum(dy * (v * r), 0, keepdims=True)
            if chunk >= 4:
                dv = jnp.where(lanes() < 64, dv, up)
            b.dp2[m * 128 : m * 128 + 128, cols] = low(dv)
    for copy in attn_loads:
        copy.wait()

    def back2(cols):
        b.partial[:, cols] = times_transposed(b.dp2[...], b.proj[cols, :])

    by_columns(1024, back2)
    swap = moves.sibling(b.partial, b.other)
    staged(
        moves,
        b.normed_t,
        lambda k: b.dp2[:, k * 256 : k * 256 + 256],
        slots(b.su, b.sd),
        places(b.qw0_grad, 2) + places(b.qw1_grad, 2),
    )
    swap.wait_recv()
    unpermuted(b, b.partial, b.other, b.dn)
    moves.flush()
    ring2.start(0)
    norm_back_rows(b.z, b.gains.at[1, 0:1], (b.dn,), b.dh2, b.dz, b.d_mix1)

    norm_rows(b.h1, b.gains.at[0, 1:2], b.normed)
    transpose_into(b.normed, b.normed_t)
    transpose_into(b.dz, b.turned)
    moves.done(swap)
    ring.finish(0)
    ring.start(1)
    ffn_loop(
        b, (b.gate0, b.up0, b.down0), (b.gate_grad, b.up_grad, b.down_grad),
        b.normed, b.normed_t, b.dz, b.turned, b.partial,
    )
    swap = moves.sibling(b.partial, b.other0)
    ring.forward(1)
    ring2.forward(0)
    ring.finish(1)
    ring.start(2)
    ring2.finish(0)
    ring2.start(1)
    swap.wait_recv()
    norm_back_rows(b.h1, b.gains.at[0, 1:2], (b.partial, b.other0), b.dz, b.dh1, b.d_ffn0)
    ring.forward(2)
    ring2.forward(1)
    ring.finish(2)
    ring2.finish(1)
    ring2.start(2)
    ring2.forward(2)
    ring2.finish(2)
    ring.settle()
    ring2.settle()
    moves.settle()


def own_columns(ref, k):
    return ref[:, pl.ds(pl.multiple_of(lax.axis_index(S) * 512 + k * 256, 256), 256)]


def ring_scratch(first, widths):
    return {first + str(i): s for i, s in enumerate(scatter_scratch(widths))}


def backward(qk, cosine, sine, ones, perm, w, mid):
    partial_gain = ((8, 1024), F32, VM)
    wide, thin = ((1024, 2304), BF, ANY), ((1024, 512), BF, ANY)
    rings = ring_scratch(chr(97), (2304,) * 3), ring_scratch(chr(98), (512,) * 3)

    def body(b):
        b.ring, b.ring2 = [[getattr(b, name) for name in ring] for ring in rings]
        backward_kernel(b)

    def sums(width):
        return ((16, width), F32, VM)

    return launch(
        body,
        "backward",
        3,
        dict(
            gains=(w.gains_out, VM), qk=(qk, VM), cosine=(cosine, VM), sine=(sine, VM), ones=(ones, VM),
            dh2=(mid.dh2, VM), att=(w.att_out, VM), z=(w.z_out, VM), h1=(w.h1_out, VM), perm_in=(perm, ANY),
            gate0=(flat(w.gate0_out), ANY), up0=(flat(w.up0_out), ANY), down0=(flat(w.down0_out), ANY),
            qw0=(flat(w.qw0_out), ANY), qw1=(flat(w.qw1_out), ANY), mo1_in=(flat(w.mo1_out), ANY),
            packed_in=(w.packed_out, ANY), p2_in=(w.p2_out, ANY),
            rg=(mid.gg.reshape(ring_shape(2304)), ANY), ru=(mid.gu.reshape(ring_shape(2304)), ANY),
            rd=(mid.gd.reshape(ring_shape(2304)), ANY),
        ),
        dict(
            gate_grad=wide, up_grad=wide, down_grad=wide, qw0_grad=thin, qw1_grad=thin, mo1_grad=thin,
            d_qk=((8, 128), F32, VM), d_mix1=partial_gain, d_ffn0=partial_gain, dh1=((256, 1024), F32, VM),
            sum_g=sums(2304), sum_u=sums(2304), sum_d=sums(2304), sum_q0=sums(512), sum_q1=sums(512), sum_mo=sums(512),
        ),
        dict(
            mo=bf(1024, 1024), proj=bf(1024, 1024), perm=bf(1024, 1024),
            packed=bf(8, 128, 256), p2=vm(256, 1024), do=bf(256, 1024),
            out_att=bf(8, 128, 128), d_att=bf(8, 128, 128), turned=bf(1024, 256), dkv=vm(1024, 128), out=bf(8, 128, 256),
            d_packed=bf(8, 128, 256), normed=bf(256, 1024), normed_t=bf(1024, 256), dp2=bf(256, 1024),
            high=bf(256, 1024), rest=bf(256, 1024), dn=vm(256, 1024),
            partial=vm(256, 1024), other=vm(256, 1024), other0=vm(256, 1024), dz=bf(256, 1024),
            local=dma(32), send=dma(24), recv=dma(24), ssend=dma(2, 54), srecv=dma(2, 54), sload=dma(2, 27),
            **ffn_scratch(), **rings[0], **rings[1],
        ),
    )


def last_kernel(b):
    core, seq = lax.axis_index(S), lax.axis_index(SQ)
    here = chip()
    around = [device_at(moved(here, axis, by)) for axis in range(3) for by in (1, 2, 3)]
    greet(around + [sibling_device(), {SQ: lax.rem(seq + 1, 8)}, {SQ: lax.rem(seq + 7, 8)}])
    moves = Moves(b.local, b.send, b.recv)
    ring = Scatter((b.rg, b.ru, b.rd), b.ring, (b.sum_g, b.sum_u, b.sum_d), b.ssend.at[0], b.srecv.at[0], b.sload.at[0])
    ring2 = Scatter(
        (b.ci0_grad, b.ci1_grad, b.mt_grad), b.ring2, (b.sum_c0, b.sum_c1, b.sum_mt), b.ssend.at[1], b.srecv.at[1], b.sload.at[1]
    )
    ring.start(0)
    mo0_load = moves.local(b.mo0_in, b.mo)
    p1_load = moves.local(b.p1_in, b.p1)
    perm_load = moves.local(b.perm_in, b.perm)
    ci_loads = [moves.local(w, b.ci.at[:, pl.ds(i * 768, 768)]) for i, w in enumerate((b.ci0, b.ci1))]

    def rounded(rows):
        b.do[rows] = low(b.dh1[rows])

    by_rows(256, rounded)
    mo0_load.wait()
    p1_load.wait()

    def mixed(i, carry):
        rows = pl.ds(pl.multiple_of(core * 512 + i * 128, 128), 128)
        cols = pl.ds(pl.multiple_of(i * 128, 128), 128)
        middle_cols = pl.ds(pl.multiple_of(512 + i * 128, 128), 128)
        dm = times_transposed(b.do[...], b.mo[rows, :])
        taps = b.taps[:, cols]
        for m in range(2):
            part = slice(m * 128, m * 128 + 128)
            conv = sum(taps[j : j + 1] * b.pad[m, 6 + j : 134 + j, cols] for j in range(3))
            b.dp1[part, middle_cols] = low(dm[part] * conv)
            b.dconv[m, :128, cols] = dm[part] * b.p1[part, middle_cols]
        return carry

    lax.fori_loop(0, 4, mixed, 0)
    rim = moves.remote(b.dconv.at[:, pl.ds(0, 8)], b.rim, {SQ: lax.rem(seq + 7, 8)})
    transpose_into(b.m1, b.turned)
    for k in range(2):
        cols = slice(k * 256, k * 256 + 256)
        grad = low(matmul(b.turned[...], own_columns(b.do, k)))
        b.mt_grad[..., cols] = grad.reshape(ring_shape(256))
    norm_rows(b.x, b.gains.at[0, 0:1], b.normed)
    perm_load.wait()
    permuted(b.normed, b.perm, b.high)
    transpose_into(b.high, b.normed_t)
    rim.wait_recv()
    b.dconv[:, 128:] = jnp.where(seq < 7, b.rim[...], 0.0)
    b.d_taps[...] = jnp.zeros_like(b.d_taps)

    def conv_back(i, carry):
        cols = pl.ds(pl.multiple_of(i * 128, 128), 128)
        last_cols = pl.ds(pl.multiple_of(1024 + i * 128, 128), 128)
        taps = b.taps[:, cols]
        for m in range(2):
            part = slice(m * 128, m * 128 + 128)
            dconv = b.dconv[m, :128, cols]
            for j in range(3):
                b.d_taps[j : j + 1, cols] += jnp.sum(dconv * b.pad[m, 6 + j : 134 + j, cols], 0, keepdims=True)
            dbx = sum(taps[2 - j : 3 - j] * b.dconv[m, j : 128 + j, cols] for j in range(3))
            b.dp1[part, cols] = low(dbx * b.p1[part, last_cols])
            b.dp1[part, last_cols] = low(dbx * b.p1[part, cols])
        return carry

    lax.fori_loop(0, 4, conv_back, 0)
    for x in range(4):
        tile = low(b.d_taps[:, x * 128 : x * 128 + 128])
        b.mt_grad[x, :, :, :, :, 512:] = jnp.broadcast_to(jnp.concatenate([tile, tile], 0), (2, 4, 2, 16, 128))
    for i, grad in enumerate((b.ci0_grad, b.ci1_grad)):
        for j in range(3):
            cols = slice(i * 768 + j * 256, i * 768 + j * 256 + 256)
            value = low(matmul(b.normed_t[...], b.dp1[:, cols]))
            grad[..., j * 256 : j * 256 + 256] = value.reshape(ring_shape(256))
    ring2.start(0)
    ring.forward(0)
    for copy in ci_loads:
        copy.wait()

    def back1(cols):
        b.partial[:, cols] = times_transposed(b.dp1[...], b.ci[cols, :])

    by_columns(1024, back1)
    swap = moves.sibling(b.partial, b.other)
    swap.wait_recv()
    unpermuted(b, b.partial, b.other, b.dn)
    norm_back_rows(b.x, b.gains.at[0, 0:1], (b.dn,), b.dh1, b.dx, b.d_mix0)

    first = core == 0
    small = Small(b.sums, b.qk_other, b.arrivals, b.small_send, b.small_recv)
    b.sums[0] = jnp.zeros((8, 1024), F32)
    b.sums[0, 0:1] = jnp.sum(jnp.where(first, b.d_mix0[...], b.d_mix1[...]), 0, keepdims=True)
    b.sums[0, 1:2] = jnp.sum(jnp.where(first, b.d_ffn0[...], b.d_ffn1[...]), 0, keepdims=True)
    small.sibling(b.d_qk).start()
    small.sibling(b.d_qk).wait_recv()
    b.sums[0, 2:4, :128] = b.d_qk[0:2] + b.qk_other[0:2]
    small.start(0)
    ring.finish(0)
    ring.start(1)
    ring2.forward(0)
    small.finish(0)
    small.start(1)
    ring.forward(1)
    ring2.finish(0)
    ring2.start(1)
    small.finish(1)
    small.start(2)
    ring.finish(1)
    ring.start(2)
    ring2.forward(1)
    small.finish(2)
    b.small[...] = b.sums[3]
    ring.forward(2)
    ring2.finish(1)
    ring2.start(2)
    ring.finish(2)
    ring2.forward(2)
    ring2.finish(2)

    mine = (pl.ds(pl.multiple_of(core * 8, 8), 8), pl.ds(pl.multiple_of(8 - core * 8, 8), 8))
    column = 0
    for ref in (b.sum_c0, b.sum_c1, b.sum_q0, b.sum_q1):
        width = ref.shape[1]
        home = b.mix_grad.at[core, :, pl.ds(column, width)]
        moves.keep(ref.at[mine[0]], home)
        moves.sibling(ref.at[mine[1]], home)
        column += width
    pairs = (
        (b.gate_grad, 2304, (b.sum_g, b.sum_g1)),
        (b.up_grad, 2304, (b.sum_u, b.sum_u1)),
        (b.down_grad, 2304, (b.sum_d, b.sum_d1)),
        (b.mo_grad, 512, (b.sum_mt, b.sum_mo1)),
    )

    def trade(k, block):
        out, n, sources = pairs[k]
        home = out.at[:, pl.ds(block * n, n)]
        keep = pltpu.make_async_copy(sources[block].at[:, pl.ds(0, n)], home, b.trade.at[k])
        give = pltpu.make_async_remote_copy(
            src_ref=sources[1 - block].at[:, pl.ds(0, n)],
            dst_ref=home,
            send_sem=b.trade.at[4 + k],
            recv_sem=b.trade.at[8 + k],
            device_id=sibling_device(),
            device_id_type=MESH,
        )
        return keep, give

    for block in range(2):

        @pl.when(core == block)
        def _():
            for k in range(4):
                for copy in trade(k, block):
                    copy.start()

    for k in range(4):
        keep, give = trade(k, 0)
        keep.wait()
        give.wait()
    ring.settle()
    ring2.settle()
    small.settle()
    small.sibling(b.d_qk).wait_send()
    for copy in moves.sent[-4:]:
        copy.wait_recv()
    moves.settle()


def last(x, perm, w, mid, back):
    rings = ring_scratch(chr(97), (2304,) * 3), ring_scratch(chr(98), (768, 768, 640))

    def body(b):
        b.ring, b.ring2 = [[getattr(b, name) for name in ring] for ring in rings]
        last_kernel(b)

    def out(*shape, where=ANY):
        return (shape, F32, where)

    def sums(width):
        return vm(16, width)

    return launch(
        body,
        "last",
        4,
        dict(
            x=(x, VM), gains=(w.gains_out, VM), taps=(w.taps_out, VM), dh1=(back.dh1, VM), m1=(w.m1_out, VM),
            pad=(w.pad_out, VM), d_qk=(back.d_qk, VM), d_mix1=(back.d_mix1, VM), d_ffn0=(back.d_ffn0, VM),
            d_ffn1=(mid.d_ffn, VM), mo0_in=(flat(w.mo0_out), ANY), p1_in=(w.p1_out, ANY), perm_in=(perm, ANY),
            ci0=(flat(w.ci0_out), ANY), ci1=(flat(w.ci1_out), ANY),
            rg=(back.gate_grad.reshape(ring_shape(2304)), ANY), ru=(back.up_grad.reshape(ring_shape(2304)), ANY),
            rd=(back.down_grad.reshape(ring_shape(2304)), ANY),
            sum_g1=(back.sum_g, VM), sum_u1=(back.sum_u, VM), sum_d1=(back.sum_d, VM),
            sum_q0=(back.sum_q0, VM), sum_q1=(back.sum_q1, VM), sum_mo1=(back.sum_mo, VM),
        ),
        dict(
            dx=((256, 1024), BF, VM), small=out(8, 1024, where=VM), mix_grad=out(2, 8, 2560),
            gate_grad=out(16, 4608), up_grad=out(16, 4608), down_grad=out(16, 4608), mo_grad=out(16, 1024),
            sum_mt=out(16, 640, where=VM),
        ),
        dict(
            mo=bf(1024, 1024), ci=bf(1024, 1536), perm=bf(1024, 1024), p1=vm(256, 1536), do=bf(256, 1024),
            turned=bf(1024, 256), normed=bf(256, 1024), normed_t=bf(1024, 256), high=bf(256, 1024),
            rest=bf(256, 1024), dn=vm(256, 1024), partial=vm(256, 1024), other=vm(256, 1024),
            dp1=bf(256, 1536), dconv=vm(2, 136, 512), rim=vm(2, 8, 512), d_taps=vm(8, 512), d_mix0=vm(8, 1024),
            ci0_grad=bf(*ring_shape(768)), ci1_grad=bf(*ring_shape(768)), mt_grad=bf(*ring_shape(640)),
            sum_g=sums(2304), sum_u=sums(2304), sum_d=sums(2304), sum_c0=sums(768), sum_c1=sums(768),
            sums=vm(4, 8, 1024), qk_other=vm(8, 128), arrivals=vm(9, 8, 1024), small_send=dma(10), small_recv=dma(10),
            local=dma(16), send=dma(12), recv=dma(12), trade=dma(12),
            ssend=dma(2, 54), srecv=dma(2, 54), sload=dma(2, 27), **rings[0], **rings[1],
        ),
    )


def low(v):
    return v.astype(BF)


def matmul(left, right):
    return jnp.dot(left, right, preferred_element_type=F32)


def times_transposed(left, right):
    return lax.dot_general(left, right, (((1,), (1,)), ((), ())), preferred_element_type=F32)


def transposed_times(left, right):
    return lax.dot_general(left, right, (((0,), (0,)), ((), ())), preferred_element_type=F32)


def both_halves(conv_in, qkv):
    b = conv_in.reshape(8, 3, 2, 512).transpose(2, 0, 1, 3).reshape(2, 8, 1536)
    q = qkv[:, :1024].reshape(8, 2, 512).transpose(1, 0, 2)
    kv = qkv[:, 1024:].reshape(8, 2, 2, 4, 64).transpose(2, 0, 3, 1, 4).reshape(2, 8, 512)
    return jnp.concatenate([b, q, kv], 2)


def from_halves(grads):
    conv = grads[:, :, :1536].reshape(2, 8, 3, 512).transpose(1, 2, 0, 3).reshape(8, 3072)
    q = grads[:, :, 1536:2048].transpose(1, 0, 2).reshape(8, 1024)
    kv = grads[:, :, 2048:].reshape(2, 8, 4, 2, 64).transpose(1, 3, 0, 2, 4).reshape(8, 1024)
    return conv, jnp.concatenate([q, kv], 1)


def rope_tables():
    positions = (lax.axis_index(SQ) * 128 + jnp.arange(128)).astype(F32)
    frequency = 1000000.0 ** (-jnp.arange(32).astype(F32) * 2.0 / 64)
    angles = positions[:, None] * frequency[None, :]
    cosine, sine = jnp.cos(angles), jnp.sin(angles)
    return jnp.concatenate([cosine] * 4, 1), jnp.concatenate([-sine, sine] * 2, 1)


def shards(
    inputs,
    cotangent,
    conv_in,
    conv_kernel,
    qkv_weight,
    qk_gain,
    mix_gain,
    ffn_gain,
    mix_out,
    w_gate,
    w_up,
    w_down,
):
    core = lax.axis_index(S)
    place = lax.axis_index((DP, SQ)) % 16 * 8
    x = inputs.reshape(256, 1024)
    cot = cotangent.reshape(256, 1024)
    gains = jnp.pad(jnp.concatenate([mix_gain, ffn_gain], 0).astype(F32), ((0, 6), (0, 0)))
    qk = qk_gain.astype(F32)
    kv_gain = jnp.concatenate([qk[1], jnp.ones((64,), F32)])
    qk_row = jnp.concatenate([jnp.tile(qk[0], 8), jnp.tile(kv_gain, 4)])[None]
    cosine, sine = rope_tables()
    lane = jnp.arange(128)
    ones = ((lane[:, None] // 64) == (lane[None, :] // 64)).astype(F32) / 64.0
    row = jnp.arange(1024)
    natural = row % 16 // 8 * 512 + row // 16 * 8 + row % 8
    perm = (row[:, None] == natural[None, :]).astype(BF)
    taps = lax.dynamic_update_slice(jnp.zeros((16, 128), BF), conv_kernel, (0, place))
    mix = both_halves(conv_in, qkv_weight).astype(F32)
    common = (qk_row, cosine, sine, ones, perm)
    saved = forward(x, gains, *common, taps, mix, (w_gate[0], w_up[0], w_down[0].T, mix_out[0]))
    mid = middle(cot, saved)
    back = backward(*common, saved, mid)
    end = last(x, perm, saved, mid, back)
    conv_in_grad, qkv_grad = from_halves(end.mix_grad)
    half = lax.dynamic_slice_in_dim(end.dx, core * 512, 512, 1)
    q_sum, k_sum = end.small[2, :128], end.small[3, :64]
    return (
        mid.result.reshape(2, 1, 128, 512),
        half.reshape(2, 1, 128, 512),
        conv_in_grad,
        lax.dynamic_slice(end.sum_mt, (0, 512 + place), (3, 8)),
        qkv_grad,
        jnp.stack([q_sum[:64] + q_sum[64:], k_sum]),
        end.small[0:1],
        end.small[1:2],
        end.mo_grad[None],
        end.gate_grad[None],
        end.up_grad[None],
        end.down_grad.T[None],
    )


def solution(mesh):
    every = (S, DP, SQ)
    weight = P(S, (DP, SQ), None)
    tokens = P(None, DP, SQ, None)
    in_specs = (
        tokens,
        tokens,
        P(every, None),
        P(None, every),
        P(every, None),
        P(),
        P(S, None),
        P(S, None),
        weight,
        weight,
        weight,
        P(S, None, (DP, SQ)),
    )
    tokens = P(None, DP, SQ, S)
    out_specs = (
        tokens,
        tokens,
        P(every, None),
        P(None, every),
        P(every, None),
        P(),
        P(S, None),
        P(S, None),
        weight,
        weight,
        weight,
        P(S, None, (DP, SQ)),
    )
    return jax.shard_map(shards, mesh=mesh, in_specs=in_specs, out_specs=out_specs, check_vma=False)
```

```python
import functools

import jax
import jax.numpy as jnp
from jax import lax
from jax.experimental import pallas as pl
from jax.experimental.pallas import tpu as pltpu
from jax.sharding import PartitionSpec as P

EPSILON = 1e-05
S, DP, SQ = "section", "dp", "seq"
MESH = pl.DeviceIdType.MESH
ANY = pl.BlockSpec(memory_space=pl.ANY)
BF, F32 = jnp.bfloat16, jnp.float32
ORDERS = ((0, 1, 2), (1, 2, 0), (2, 0, 1))
MIB = 2**20


def chip():
    dp, sq = lax.axis_index(DP), lax.axis_index(SQ)
    return (dp // 2, 2 * (sq % 2) + dp % 2, sq // 2)


def device_at(place):
    x, y, z = place
    return {DP: x * 2 + y % 2, SQ: z * 2 + y // 2}


def moved(place, axis, by):
    return tuple((v + by) % 4 if i == axis else v for i, v in enumerate(place))


def spot(place, kept=(0, 1, 2)):
    x, y, z = place

    def one(axis, value, take):
        if axis not in kept:
            return 0
        return slice(None) if value is None else take(value)

    return (
        one(0, x, lambda v: v),
        one(1, y, lambda v: v % 2),
        one(2, z, lambda v: v),
        one(1, y, lambda v: v // 2),
    )


def halves(width):
    first = (width // 256) * 128
    return (pl.ds(0, first), pl.ds(first, width - first))


def greet(devices):
    barrier = pltpu.get_barrier_semaphore()
    for device in devices:
        pl.semaphore_signal(barrier, inc=1, device_id=device, device_id_type=MESH)
    pl.semaphore_wait(barrier, len(devices))


class Gather:
    def __init__(self, bufs, send, recv, turn=0):
        self.bufs, self.send, self.recv, self.turn = bufs, send, recv, turn
        self.here = chip()

    def copy(self, colour, phase, kind):
        order = ORDERS[colour]
        axis, done = order[phase], order[:phase]
        buf = self.bufs[colour]
        half = halves(buf.shape[-1])
        step, part, to = ((0, 0, 1), (0, 1, 1), (0, 1, -1), (0, 0, -1), (-1, 0, 1), (1, 1, -1))[kind]
        source = moved(self.here, axis, step)
        block = tuple(None if i in done else v for i, v in enumerate(source))
        ref = buf.at[spot(block) + (slice(None), half[part])]
        slot = (colour * 3 + (phase + self.turn) % 3) * 6 + kind
        return pltpu.make_async_remote_copy(
            src_ref=ref,
            dst_ref=ref,
            send_sem=self.send.at[slot],
            recv_sem=self.recv.at[slot],
            device_id=device_at(moved(self.here, axis, to)),
            device_id_type=MESH,
        )

    def start(self, phase):
        for pair in ((0, 2), (1, 3)):
            for kind in pair:
                for colour in range(3):
                    self.copy(colour, phase, kind).start()

    def forward(self, phase):
        for got, then in ((0, 4), (2, 5)):
            for colour in range(3):
                self.copy(colour, phase, got).wait_recv()
                self.copy(colour, phase, then).start()

    def finish(self, phase):
        for kind in (1, 3, 4, 5):
            for colour in range(3):
                self.copy(colour, phase, kind).wait_recv()

    def settle(self, phases=range(3)):
        for phase in phases:
            for kind in range(6):
                for colour in range(3):
                    self.copy(colour, phase, kind).wait_send()


def lead(kept):
    return (4 if 0 in kept else 1, 2 if 1 in kept else 1, 4 if 2 in kept else 1, 2 if 1 in kept else 1)


def one_block(place, axis):
    x, y, z = place
    every = slice(None)
    return (
        pl.ds(x, 1) if axis == 0 else every,
        pl.ds(y % 2, 1) if axis == 1 else every,
        pl.ds(z, 1) if axis == 2 else every,
        pl.ds(y // 2, 1) if axis == 1 else every,
        every,
    )


def scatter_scratch(widths):
    shapes = []
    for colour, width in enumerate(widths):
        for phase in range(3):
            rows = lead(ORDERS[colour][phase + 1 :]) + (16,)
            pair = [rows + (h.size,) for h in halves(width)]
            shapes += pair + pair + [rows + (width,)] * 2
    return [pltpu.VMEM(s, BF) for s in shapes]


class Scatter:
    def __init__(self, parts, bufs, results, send, recv, load):
        self.parts, self.results = parts, results
        self.halves = [halves(p.shape[-1]) for p in parts]
        self.bufs = []
        for c, half in enumerate(self.halves):
            sizes = [h.size for h in half] * 2 + [parts[c].shape[-1]] * 2
            of_colour = [bufs[(c * 3 + p) * 6 :][:6] for p in range(3)]
            self.bufs.append([[b.at[..., pl.ds(0, n)] for b, n in zip(bs, sizes)] for bs in of_colour])
        self.send, self.recv, self.load = send, recv, load
        self.here = chip()

    def source(self, colour, phase, by, side):
        axis = ORDERS[colour][phase]
        block = one_block(moved(self.here, axis, by), axis)
        if phase == 0:
            return self.parts[colour].at[block + (self.halves[colour][side],)]
        return self.bufs[colour][phase - 1][2 + side].at[block + (slice(None),)]

    def loads(self, colour, phase, which):
        side = which % 2
        by = 0 if which >= 2 else (1, -1)[side]
        target = self.bufs[colour][phase][which]
        slot = (colour * 3 + phase) * 4 + which
        return pltpu.make_async_copy(self.source(colour, phase, by, side), target, self.load.at[slot])

    def copy(self, colour, phase, kind):
        half = self.halves[colour]
        bufs = self.bufs[colour][phase]
        side = kind % 2
        to = (1, -1)[side]
        last = bufs[4 + side]
        if kind < 2:
            src, dst = self.source(colour, phase, 2, side), bufs[2 + side]
        elif kind < 4:
            src, dst = self.source(colour, phase, to, 1 - side), last.at[..., half[1 - side]]
        else:
            src, dst = bufs[side], last.at[..., half[side]]
        slot = (colour * 3 + phase) * 6 + kind
        return pltpu.make_async_remote_copy(
            src_ref=src,
            dst_ref=dst,
            send_sem=self.send.at[slot],
            recv_sem=self.recv.at[slot],
            device_id=device_at(moved(self.here, ORDERS[colour][phase], to)),
            device_id_type=MESH,
        )

    def start(self, phase, colours=(0, 1, 2)):
        for colour in colours:
            for which in range(2):
                self.loads(colour, phase, which).start()
        for kind in range(4):
            for colour in colours:
                self.copy(colour, phase, kind).start()

    def forward(self, phase):
        for side in range(2):
            for colour in range(3):
                self.loads(colour, phase, side).wait()
                self.copy(colour, phase, side).wait_recv()
                bufs = self.bufs[colour][phase]
                added(bufs[side], (bufs[2 + side],), bufs[side])
                self.copy(colour, phase, 4 + side).start()
                self.loads(colour, phase, 2 + side).start()

    def advance(self, phase):
        for colour in range(3):
            self.finish(phase, (colour,))
            self.start(phase + 1, (colour,))

    def finish(self, phase, colours=(0, 1, 2)):
        for colour in colours:
            for which in (2, 3):
                self.loads(colour, phase, which).wait()
            for kind in range(2, 6):
                self.copy(colour, phase, kind).wait_recv()
            bufs = self.bufs[colour][phase]
            for side, half in enumerate(self.halves[colour]):
                last = [bufs[4 + i].at[..., half] for i in range(2)]
                out = bufs[2 + side] if phase < 2 else self.results[colour].at[:, half]
                added(bufs[2 + side], last, out)

    def settle(self):
        for phase in range(3):
            for kind in range(6):
                for colour in range(3):
                    self.copy(colour, phase, kind).wait_send()


def added(base, others, out):
    sizes = base.shape[:4]
    _, b, c, d = sizes

    def step(i, carry):
        at = (i // (b * c * d), (i // (c * d)) % b, (i // d) % c, i % d)
        total = base[at].astype(F32)
        for other in others:
            total = total + other[at].astype(F32)
        if len(out.shape) == 2:
            out[...] = total.astype(out.dtype)
        else:
            out[at] = total.astype(out.dtype)
        return carry

    lax.fori_loop(0, sizes[0] * b * c * d, step, 0)


class Small:
    def __init__(self, sums, other, slots, send, recv):
        self.sums, self.other, self.slots = sums, other, slots
        self.send, self.recv = send, recv
        self.here = chip()

    def sibling(self, source):
        return pltpu.make_async_remote_copy(
            src_ref=source,
            dst_ref=self.other,
            send_sem=self.send.at[9],
            recv_sem=self.recv.at[9],
            device_id={S: 1 - lax.axis_index(S)},
            device_id_type=MESH,
        )

    def copy(self, phase, by):
        slot = phase * 3 + by - 1
        return pltpu.make_async_remote_copy(
            src_ref=self.sums.at[phase],
            dst_ref=self.slots.at[slot],
            send_sem=self.send.at[slot],
            recv_sem=self.recv.at[slot],
            device_id=device_at(moved(self.here, phase, by)),
            device_id_type=MESH,
        )

    def start(self, phase):
        for by in (1, 2, 3):
            self.copy(phase, by).start()

    def finish(self, phase):
        for by in (1, 2, 3):
            self.copy(phase, by).wait_recv()
        one, two, three = [self.slots[phase * 3 + i] for i in range(3)]
        self.sums[phase + 1] = (self.sums[phase] + two) + (one + three)

    def settle(self):
        for phase in range(3):
            for by in (1, 2, 3):
                self.copy(phase, by).wait_send()


class Bag:
    def __init__(self, **items):
        self.__dict__.update(items)


def launch(body, name, cid, ins, outs, scratch):
    def kernel(*refs):
        body(Bag(**dict(zip([*ins, *outs, *scratch], refs))))

    got = pl.pallas_call(
        kernel,
        name=name,
        out_shape=[jax.ShapeDtypeStruct(shape, dtype) for shape, dtype, _ in outs.values()],
        in_specs=[where for _, where in ins.values()],
        out_specs=[where for _, _, where in outs.values()],
        scratch_shapes=list(scratch.values()),
        compiler_params=pltpu.CompilerParams(
            collective_id=cid, has_side_effects=True, vmem_limit_bytes=60 * MIB
        ),
    )(*[value for value, _ in ins.values()])
    return Bag(**dict(zip(outs, got)))


VM = pl.BlockSpec(memory_space=pltpu.VMEM)


def vm(*shape, dtype=F32):
    return pltpu.VMEM(shape, dtype)


class Moves:
    def __init__(self, local, send, recv):
        self.sems = local, send, recv
        self.kept, self.sent = [], []
        self.locals = self.remotes = 0

    def local(self, src, dst):
        copy = pltpu.make_async_copy(src, dst, self.sems[0].at[self.locals])
        self.locals += 1
        copy.start()
        return copy

    def keep(self, src, dst):
        self.kept.append(self.local(src, dst))

    def remote(self, src, dst, device):
        slot = self.remotes
        self.remotes += 1
        copy = pltpu.make_async_remote_copy(
            src_ref=src,
            dst_ref=dst,
            send_sem=self.sems[1].at[slot],
            recv_sem=self.sems[2].at[slot],
            device_id=device,
            device_id_type=MESH,
        )
        copy.start()
        self.sent.append(copy)
        return copy

    def sibling(self, src, dst):
        return self.remote(src, dst, {S: 1 - lax.axis_index(S)})

    def mates(self, src, dst):
        me = lax.axis_index(SQ)
        copies = [self.remote(src(lax.rem(me + j, 8)), dst, {SQ: lax.rem(me + j, 8)}) for j in range(1, 8)]
        return [self.local(src(me), dst)], copies

    def done(self, copy):
        copy.wait_send()
        self.sent = [c for c in self.sent if c is not copy]

    def flush(self):
        for copy in self.kept:
            copy.wait()
        self.kept = []

    def settle(self):
        self.flush()
        for copy in self.sent:
            copy.wait_send()


def arrived(moves):
    own, copies = moves
    for copy in own:
        copy.wait()
    for copy in copies:
        copy.wait_recv()


def mate_devices():
    me = lax.axis_index(SQ)
    return [{SQ: lax.rem(me + j, 8)} for j in range(1, 8)]


def across_devices():
    here = chip()
    return [device_at(moved(here, axis, by)) for axis in range(2) for by in (1, -1)]


def sibling_device():
    return {S: 1 - lax.axis_index(S)}


def by_rows(rows, step, size=32):
    def body(i, carry):
        step(pl.ds(pl.multiple_of(i * size, size), size))
        return carry

    lax.fori_loop(0, rows // size, body, 0)


def by_columns(width, step, size=256):
    def body(i, carry):
        step(pl.ds(pl.multiple_of(i * size, size), size))
        return carry

    lax.fori_loop(0, width // size, body, 0)


def core_columns(size):
    return pl.ds(pl.multiple_of(lax.axis_index(S) * size, size), size)


def inverse_norm(v):
    return lax.rsqrt(jnp.mean(v * v, axis=-1, keepdims=True) + EPSILON)


def norm_rows(src, gain, dst):
    def step(rows):
        v = src[rows].astype(F32)
        dst[rows] = low(v * inverse_norm(v) * gain[...])

    by_rows(256, step)


def norm_back_rows(src, gain, upstreams, residual, out, d_gain):
    d_gain[...] = jnp.zeros_like(d_gain)

    def step(rows):
        v = src[rows].astype(F32)
        up = sum(u[rows] for u in upstreams)
        r = inverse_norm(v)
        t = up * gain[...]
        dv = r * (t - v * (r * r * jnp.mean(t * v, axis=-1, keepdims=True)))
        out[rows] = (residual[rows].astype(F32) + dv).astype(out.dtype)
        scaled = up * (v * r)
        d_gain[...] += scaled[:8] + scaled[8:16] + scaled[16:24] + scaled[24:]

    by_rows(256, step)


def transpose_into(src, dst):
    def step(cols):
        dst[cols, :] = src[:, cols].astype(F32).T.astype(BF)

    by_columns(1024, step, 128)


def lanes(width=128):
    return lax.broadcasted_iota(jnp.int32, (1, width), 1)


def head_mean(v, ones):
    return jnp.dot(v, ones, precision=lax.Precision.HIGHEST, preferred_element_type=F32)


def qk_gain(b, chunk):
    return b.qk[chunk // 4 : chunk // 4 + 1]


def half_turn(v):
    return jnp.where(lanes() % 64 < 32, pltpu.roll(v, 96, 1), pltpu.roll(v, 32, 1))


def head_lanes(v, head, upper):
    v = v.astype(F32)
    if head != upper:
        v = pltpu.roll(v, 64, 1)
    return jnp.where(lanes() >= 64 if upper else lanes() < 64, v, 0.0)


def block_probs(b, block, head):
    count = 256 * (block + 1)
    q = head_lanes(b.packed[2 * block : 2 * block + 2, :, :128].reshape(256, 128), head, 0)
    kv = b.packed[: 2 * block + 2, :, 128:].reshape(count, 128)
    scores = times_transposed(low(q), kv) * 0.125
    row = lax.broadcasted_iota(jnp.int32, (256, count), 0) + 256 * block
    col = lax.broadcasted_iota(jnp.int32, (256, count), 1)
    e = jnp.exp(jnp.where(row >= col, scores, -1e9))
    return q, kv, e * (1.0 / jnp.sum(e, -1, keepdims=True))


def flat(value):
    return value.reshape(-1, value.shape[-1])


def ring_shape(width):
    return (4, 2, 4, 2, 16, width)


def fill_perm(perm):
    def step(cols):
        p = lax.broadcasted_iota(jnp.int32, (1024, 256), 1) + cols.start
        row = lax.broadcasted_iota(jnp.int32, (1024, 256), 0)
        natural = (p & 8) * 64 + (p >> 4) * 8 + (p & 7)
        perm[:, cols] = jnp.where(row == natural, 1.0, 0.0).astype(BF)

    by_columns(1024, step)


def fill_ones(ones):
    row = lax.broadcasted_iota(jnp.int32, (128, 128), 0)
    col = lax.broadcasted_iota(jnp.int32, (128, 128), 1)
    ones[...] = jnp.where(row // 64 == col // 64, 1.0 / 64.0, 0.0)


def forward_kernel(b):
    core, seq = lax.axis_index(S), lax.axis_index(SQ)
    greet(across_devices() + mate_devices() + [sibling_device()])
    moves = Moves(b.local, b.send, b.recv)
    here = spot(chip())
    half, other_half = core_columns(512), pl.ds(pl.multiple_of(512 - core * 512, 512), 512)

    mine = pl.ds(pl.multiple_of(core * 8, 8), 8)
    waits = [
        moves.local(b.mix_in.at[core], b.mix.at[mine]),
        moves.local(b.gains_in, b.gains.at[core]),
        moves.local(b.taps_in, b.mt.at[here + (slice(None), pl.ds(512, 128))]),
    ]
    swaps = [
        moves.sibling(b.mix_in.at[1 - core], b.mix.at[mine]),
        moves.sibling(b.gains_in, b.gains.at[core]),
    ]
    shards = (
        (b.gate_in, 2304, (b.gate0, b.gate1)),
        (b.up_in, 2304, (b.up0, b.up1)),
        (b.down_in, 2304, (b.down0, b.down1)),
        (b.mo, 512, (b.mt, b.mo1)),
    )

    def trade(k, block):
        w, n, homes = shards[k]
        home = homes[block].at[here + (slice(None), pl.ds(0, n))]
        keep = pltpu.make_async_copy(w.at[:, pl.ds(block * n, n)], home, b.trade.at[k])
        give = pltpu.make_async_remote_copy(
            src_ref=w.at[:, pl.ds((1 - block) * n, n)],
            dst_ref=home,
            send_sem=b.trade.at[4 + k],
            recv_sem=b.trade.at[8 + k],
            device_id=sibling_device(),
            device_id_type=MESH,
        )
        return keep, give

    for block in range(2):

        @pl.when(core == block)
        def _():
            for k in (3, 0, 1, 2):
                for copy in trade(k, block):
                    copy.start()

    for copy in waits:
        copy.wait()
    for copy in swaps:
        copy.wait_recv()
    b.ci0[here] = low(b.mix[:, :768])
    b.ci1[here] = low(b.mix[:, 768:1536])
    b.qw0[here] = low(b.mix[:, 1536:2048])
    b.qw1[here] = low(b.mix[:, 2048:])
    for k in (3, 0, 1, 2):
        keep, give = trade(k, 0)
        keep.wait()
        give.wait_recv()
    moves.keep(b.gains, b.gains_out)

    rings = [
        Gather(bufs, b.gsend.at[i], b.grecv.at[i])
        for i, bufs in enumerate(
            (
                (b.ci0, b.ci1, b.mt),
                (b.gate0, b.up0, b.down0),
                (b.qw0, b.qw1, b.mo1),
                (b.gate1, b.up1, b.down1),
            )
        )
    ]
    ring_a, ring_b, ring_c, ring_d = rings
    lasts = [
        Gather([w.at[..., pl.ds(768 * i, 768)] for w in (b.gate1, b.up1, b.down1)], b.gsend.at[j], b.grecv.at[j], turn)
        for i, (j, turn) in enumerate(((3, 0), (4, 0), (4, 1)))
    ]
    for ring in rings:
        ring.start(0)
    norm_rows(b.x, b.gains.at[0, 0:1], b.normed)
    fill_perm(b.perm)
    fill_ones(b.ones)
    permuted(b.normed, b.perm, b.turned)
    for ring in rings:
        ring.forward(0)
    ring_a.finish(0)
    ring_a.start(1)
    ring_b.finish(0)
    ring_b.start(1)
    ring_a.forward(1)
    ring_a.finish(1)
    ring_a.start(2)
    ring_b.forward(1)
    ring_c.finish(0)
    ring_c.start(1)
    ring_a.forward(2)
    ring_b.finish(1)
    ring_b.start(2)
    ring_a.finish(2)

    def other_mo(source, target):
        return moves.sibling(source.at[..., pl.ds(0, 512)], target)

    mo0_swap = other_mo(b.mt, b.mo0_other)
    ring_d.finish(0)
    for x in range(4):
        rows = flat(b.mt[x, :, :, :, :, 512:]).reshape(16, 16, 128)
        b.taps[:, x * 128 : x * 128 + 128] = jnp.sum(rows.astype(F32), 0)[:8]
    for i, ci in enumerate((b.ci0, b.ci1)):
        for j in range(3):
            cols = slice(j * 256, j * 256 + 256)
            b.p1[:, i * 768 + j * 256 : i * 768 + j * 256 + 256] = matmul(b.turned[...], flat(ci[..., cols]))
    moves.keep(b.p1, b.p1_out)
    ring_c.forward(1)

    def gated(rows):
        b.bx[rows] = low(b.p1[rows, :512] * b.p1[rows, 1024:]).astype(F32)

    by_rows(256, gated)
    for m in range(2):
        b.pad[m, 8:] = b.bx[m * 128 : m * 128 + 128]
    rim = moves.remote(b.pad.at[:, pl.ds(128, 8)], b.rim, {SQ: lax.rem(seq + 1, 8)})
    ring_c.finish(1)
    rim.wait_recv()
    b.pad[:, :8] = jnp.where(seq > 0, b.rim[...], 0.0)
    moves.keep(b.pad, b.pad_out)

    def convolve(cols):
        taps = b.taps[:, cols]
        for m in range(2):
            conv = sum(taps[j : j + 1] * b.pad[m, 6 + j : 134 + j, cols] for j in range(3))
            rows = slice(m * 128, m * 128 + 128)
            gate = b.p1[rows, pl.ds(pl.multiple_of(cols.start + 512, 128), 128)]
            b.m1[rows, pl.ds(pl.multiple_of(core * 512 + cols.start, 128), 128)] = low(gate * conv)

    by_columns(512, convolve, 128)
    swap = moves.sibling(b.m1.at[:, half], b.m1.at[:, half])
    ring_b.forward(2)
    swap.wait_recv()
    moves.keep(b.m1, b.m1_out)
    moves.keep(b.taps, b.taps_out)
    mo0_swap.wait_recv()
    b.h1[:, half] = b.x[:, half].astype(F32) + matmul(b.m1[...], flat(b.mt[..., :512]))
    b.h1[:, other_half] = b.x[:, other_half].astype(F32) + matmul(b.m1[...], flat(b.mo0_other[...]))
    moves.keep(b.h1, b.h1_out)
    norm_rows(b.h1, b.gains.at[0, 1:2], b.normed)
    ring_c.start(2)
    ring_d.start(1)
    ring_b.finish(2)

    def hidden(cols):
        g = matmul(b.normed[...], flat(b.gate0[..., cols]))
        u = matmul(b.normed[...], flat(b.up0[..., cols]))
        b.active[:, cols] = low(g / (1.0 + jnp.exp(-g)) * u)

    by_columns(2304, hidden)
    ring_d.forward(1)
    ring_c.forward(2)

    def contract(cols):
        b.f[:, cols] = times_transposed(b.active[...], flat(b.down0[cols.start // 256]))

    swaps = swapped_columns(moves, contract, b.f, b.f_other)
    ring_d.finish(1)
    lasts[0].start(2)
    ring_c.finish(2)
    mo1_swap = other_mo(b.mo1, b.mo1_other)
    for swap in swaps:
        swap.wait_recv()

    def passed(rows):
        b.z[rows] = low(b.h1[rows] + (b.f[rows] + b.f_other[rows]))

    by_rows(256, passed)
    for swap in swaps:
        moves.done(swap)
    moves.keep(b.z, b.z_out)

    norm_rows(b.z, b.gains.at[1, 0:1], b.normed)
    permuted(b.normed, b.perm, b.turned)
    lasts[0].forward(2)
    lasts[1].start(2)
    for i, qw in enumerate((b.qw0, b.qw1)):
        for j in range(2):
            cols = slice(j * 256, j * 256 + 256)
            b.p2[:, i * 512 + j * 256 : i * 512 + j * 256 + 256] = matmul(b.turned[...], flat(qw[..., cols]))
    moves.keep(b.p2, b.p2_out)
    for chunk in range(8):
        cols = slice(chunk * 128, chunk * 128 + 128)
        head, place = chunk % 4, pl.ds(chunk // 4 * 128, 128)
        for m in range(2):
            v = b.p2[m * 128 : m * 128 + 128, cols]
            y = v * lax.rsqrt(head_mean(v * v, b.ones[...]) + EPSILON) * qk_gain(b, chunk)
            y = y * b.cosine[...] + half_turn(y) * b.sine[...]
            if chunk >= 4:
                y = jnp.where(lanes() < 64, y, v)
            b.out[m * 4 + head, :, place] = low(y)
    exchange = moves.mates(lambda j: b.out.at[j], b.packed.at[seq])
    for ring_out, ref in (
        (b.ci0_out, b.ci0), (b.ci1_out, b.ci1), (b.gate0_out, b.gate0), (b.up0_out, b.up0),
        (b.down0_out, b.down0), (b.qw0_out, b.qw0), (b.qw1_out, b.qw1),
    ):
        moves.keep(ref, ring_out)
    lasts[1].forward(2)
    transpose_into(b.cot, b.cot_t)
    arrived(exchange)
    lasts[2].start(2)
    moves.keep(b.packed, b.packed_out)
    for block in range(4):
        results = []
        for head in range(2):
            _, kv, probs = block_probs(b, block, head)
            results.append(matmul(low(probs), kv))
        joint = jnp.where(lanes() < 64, pltpu.roll(results[0], 64, 1), results[1])
        b.att_rows[2 * block : 2 * block + 2] = low(joint).reshape(2, 128, 128)
    rows = pl.ds(pl.multiple_of(seq // 4 * 128, 128), 128)
    cols = pl.ds(pl.multiple_of(core * 512 + seq % 4 * 128, 128), 128)
    exchange = moves.mates(lambda j: b.att_rows.at[j], b.att.at[rows, cols])
    mo1_swap.wait_recv()
    for out, own, other in ((b.mo0_out, b.mt, b.mo0_other), (b.mo1_out, b.mo1, b.mo1_other)):
        moves.keep(own.at[..., pl.ds(0, 512)], out.at[..., half])
        moves.keep(other, out.at[..., other_half])
    arrived(exchange)
    lasts[2].forward(2)
    swap = moves.sibling(b.att.at[:, half], b.att.at[:, half])
    swap.wait_recv()
    moves.keep(b.att, b.att_out)
    b.h2[:, half] = b.z[:, half].astype(F32) + matmul(b.att[...], flat(b.mo1[...]))
    b.h2[:, other_half] = b.z[:, other_half].astype(F32) + matmul(b.att[...], flat(b.mo1_other[...]))

    norm_rows(b.h2, b.gains.at[1, 1:2], b.normed)
    transpose_into(b.normed, b.normed_t)
    ffn_loop(
        b, [flat_ref(w) for w in (b.gate1, b.up1, b.down1)], (b.gate_grad, b.up_grad, b.down_grad),
        b.normed, b.normed_t, b.cot, b.cot_t, b.f, b.f1,
        {3 * i: functools.partial(ring.finish, 2) for i, ring in enumerate(lasts)}, True,
    )
    da_swap = moves.sibling(b.f, b.da_other)
    f_swap = moves.sibling(b.f1.at[:, other_half], b.f1_other)
    da_swap.wait_recv()
    norm_back_rows(b.h2, b.gains.at[1, 1:2], (b.f, b.da_other), b.cot, b.dh2, b.d_ffn)
    f_swap.wait_recv()

    def finish(rows):
        b.result[rows] = low(b.h2[rows, half] + (b.f1[rows, half] + b.f1_other[rows]))

    by_rows(256, finish)
    for ring in rings[:3]:
        ring.settle()
    ring_d.settle(range(2))
    for ring in lasts:
        ring.settle(range(2, 3))
    for k in range(4):
        trade(k, 0)[1].wait_send()
    moves.settle()


def flat_ref(ref):
    return ref.reshape(1024, ref.shape[-1])


def swapped_columns(moves, step, ref, target):
    swaps = []
    for i in range(4):
        cols = pl.ds(256 * i, 256)
        step(cols)
        swaps.append(moves.sibling(ref.at[:, cols], target.at[:, cols]))
    return swaps


def permuted(src, perm, dst):
    def step(cols):
        dst[:, cols] = low(matmul(src[...], perm[:, cols]))

    by_columns(1024, step)


def dma(*count):
    return pltpu.SemaphoreType.DMA(count)


def bf(*shape):
    return pltpu.VMEM(shape, BF)


def forward(x, cot, gains_in, qk, cosine, sine, taps, mix_in, weights):
    def saved(*shape, dtype=BF):
        return (shape, dtype, ANY)

    wide, thin = ring_shape(2304), ring_shape(512)
    wg, wu, wd, mo = weights
    return launch(
        forward_kernel,
        "forward",
        1,
        dict(
            x=(x, VM), cot=(cot, VM), gains_in=(gains_in, VM), qk=(qk, VM), cosine=(cosine, VM), sine=(sine, VM),
            taps_in=(taps, VM), mix_in=(mix_in, VM),
            gate_in=(wg, ANY), up_in=(wu, ANY), down_in=(wd, ANY), mo=(mo, ANY),
        ),
        dict(
            gate1=saved(*wide), up1=saved(*wide), down1=saved(*wide), ci0_out=saved(*ring_shape(768)),
            ci1_out=saved(*ring_shape(768)), gate0_out=saved(*wide), up0_out=saved(*wide),
            down0_out=saved(*wide), qw0_out=saved(*thin), qw1_out=saved(*thin),
            mo0_out=saved(*ring_shape(1024)), mo1_out=saved(*ring_shape(1024)),
            gains_out=saved(2, 8, 1024, dtype=F32), taps_out=saved(8, 512, dtype=F32),
            p1_out=saved(256, 1536, dtype=F32), pad_out=saved(2, 136, 512, dtype=F32),
            m1_out=saved(256, 1024), h1_out=saved(256, 1024, dtype=F32), z_out=saved(256, 1024),
            p2_out=saved(256, 1024, dtype=F32), packed_out=saved(8, 128, 256),
            att_out=saved(256, 1024), gate_grad=saved(1024, 2304), up_grad=saved(1024, 2304), down_grad=saved(1024, 2304),
            dh2=((256, 1024), F32, VM), d_ffn=((8, 1024), F32, VM), result=((256, 512), BF, VM),
        ),
        dict(
            mix=vm(16, 2560), gains=vm(2, 8, 1024), taps=vm(8, 512), perm=bf(1024, 1024),
            ci0=bf(*ring_shape(768)), ci1=bf(*ring_shape(768)), mt=bf(*ring_shape(640)),
            gate0=bf(*wide), up0=bf(*wide), down0=bf(*wide), qw0=bf(*thin), qw1=bf(*thin), mo1=bf(*thin),
            mo0_other=bf(*thin), mo1_other=bf(*thin),
            normed=bf(256, 1024), turned=bf(256, 1024), p1=vm(256, 1536), bx=vm(256, 512), pad=vm(2, 136, 512),
            rim=vm(2, 8, 512), m1=bf(256, 1024), h1=vm(256, 1024), active=bf(256, 2304),
            f=vm(256, 1024), f_other=vm(256, 1024), z=bf(256, 1024), p2=vm(256, 1024),
            out=bf(8, 128, 256), packed=bf(8, 128, 256), att_rows=bf(8, 128, 128), att=bf(256, 1024),
            h2=vm(256, 1024), ones=vm(128, 128), normed_t=bf(1024, 256), cot_t=bf(1024, 256), f1=vm(256, 1024),
            f1_other=vm(256, 512), da_other=vm(256, 1024), local=dma(40), send=dma(32), recv=dma(32), trade=dma(12),
            gsend=dma(5, 54), grecv=dma(5, 54), **ffn_scratch(),
        ),
    )


def ffn_scratch():
    return dict(
        wg=bf(2, 1024, 256), wu=bf(2, 1024, 256), wd=bf(2, 1024, 256),
        sg=bf(2, 1024, 256), su=bf(2, 1024, 256), sd=bf(2, 1024, 256),
        load=pltpu.SemaphoreType.DMA((2, 3)), store=pltpu.SemaphoreType.DMA((2, 3)),
    )


def ffn_loop(b, weights, grads, normed, normed_t, df, df_t, da, f=None, ticks=None, gated=False, stored=None):
    ticks = ticks or {}
    bounds = sorted({0, 9, *ticks})

    def columns(i):
        return pl.ds(pl.multiple_of(i * 256, 256), 256)

    def loads(i, slot):
        return [
            pltpu.make_async_copy(w.at[:, columns(i)], d.at[slot], b.load.at[slot, k])
            for k, (w, d) in enumerate(zip(weights, (b.wg, b.wu, b.wd)))
        ]

    def stores(i, slot):
        return [
            pltpu.make_async_copy(s.at[slot], g.at[:, columns(i)], b.store.at[slot, k])
            for k, (g, s) in enumerate(zip(grads, (b.sg, b.su, b.sd)))
        ]

    da[...] = jnp.zeros_like(da)
    if f is not None:
        f[...] = jnp.zeros_like(f)

    def step(begin, end, i, carry):
        slot = lax.rem(i, 2)
        for copy in loads(i, slot):
            copy.wait()

        @pl.when(i + 1 < end)
        def _():
            for copy in loads(i + 1, 1 - slot):
                copy.start()

        gate, up, down = b.wg.at[slot], b.wu.at[slot], b.wd.at[slot]
        g = matmul(normed[...], gate[...])
        u = matmul(normed[...], up[...])
        ds = matmul(df[...], down[...])
        sig = 1.0 / (1.0 + jnp.exp(-g))
        silu = g * sig
        s = low(silu * u)
        dg = low(ds * u * (sig * (1.0 + g * (1.0 - sig))))
        du = low(ds * silu)
        if f is not None:
            f[...] += times_transposed(s, down[...])
        da[...] += times_transposed(dg, gate[...]) + times_transposed(du, up[...])

        @pl.when(i >= stored + 2 if stored and begin == stored else i >= 2)
        def _():
            for copy in stores(i - 2, slot):
                copy.wait()

        b.sg[slot] = low(matmul(normed_t[...], dg))
        b.su[slot] = low(matmul(normed_t[...], du))
        b.sd[slot] = low(matmul(df_t[...], s))
        for copy in stores(i, slot):
            copy.start()
        return carry

    for start, end in zip(bounds, bounds[1:]):
        if stored and start == stored:
            for copy in stores(start - 2, start % 2) + stores(start - 1, 1 - start % 2):
                copy.wait()
        if start in ticks:
            ticks[start]()
        if gated or start == 0:
            for copy in loads(start, start % 2):
                copy.start()
        lax.fori_loop(start, end, functools.partial(step, start, end if gated else 9), 0)
    for copy in stores(7, 1) + stores(8, 0):
        copy.wait()


def staged(moves, left_t, right, slots, dests):
    for k, (slot, dest) in enumerate(zip(slots, dests)):
        slot[...] = low(matmul(left_t[...], right(k)))
        moves.keep(slot, dest)


def slots(*stacks):
    return [stack.at[i] for stack in stacks for i in range(2)]


def places(grad, count):
    return [grad.at[:, pl.ds(256 * k, 256)] for k in range(count)]


def unpermuted(b, mine, theirs, out):
    def step(cols):
        total = mine[:, cols] + theirs[:, cols]
        high = low(total)
        b.high[:, cols] = high
        b.rest[:, cols] = low(total - high.astype(F32))

    by_columns(1024, step)

    def turn(cols):
        out[:, cols] = times_transposed(b.high[...], b.perm[cols, :]) + times_transposed(b.rest[...], b.perm[cols, :])

    by_columns(1024, turn)


def backward_kernel(b):
    core, seq = lax.axis_index(S), lax.axis_index(SQ)
    greet(across_devices() + mate_devices() + [sibling_device()])
    moves = Moves(b.local, b.send, b.recv)
    ring, ring1 = ffn_rings(b, (b.rg, b.ru, b.rd), (b.sum_g, b.sum_u, b.sum_d))
    ring.start(0)
    mo1_load = moves.local(b.mo1_in, b.mo)
    packed_load = moves.local(b.packed_in, b.packed)
    attn_loads = [
        moves.local(w, b.proj.at[:, pl.ds(i * 512, 512)]) for i, w in enumerate((b.qw0, b.qw1))
    ]
    p2_load = moves.local(b.p2_in, b.p2)
    fill_perm(b.perm)
    fill_ones(b.ones)

    def rounded(rows):
        b.do[rows] = low(b.dh2[rows])

    by_rows(256, rounded)
    mo1_load.wait()
    for h in range(4):
        rows = pl.ds(pl.multiple_of(core * 512 + h * 128, 128), 128)
        d_att = low(times_transposed(b.do[...], b.mo[rows, :]))
        for m in range(2):
            b.out_att[m * 4 + h] = d_att[m * 128 : m * 128 + 128]
    exchange = moves.mates(lambda j: b.out_att.at[j], b.d_att.at[seq])
    transpose_into(b.att, b.turned)
    staged(moves, b.turned, lambda k: own_columns(b.do, k), slots(b.sg), places(b.mo1_grad, 2))
    packed_load.wait()
    norm_rows(b.z, b.gains.at[1, 0:1], b.normed)
    permuted(b.normed, b.perm, b.high)
    transpose_into(b.high, b.normed_t)
    arrived(exchange)
    ring.forward(0)
    ring1.start(0)
    b.dkv[...] = jnp.zeros_like(b.dkv)
    for block in range(4):
        count = 256 * (block + 1)
        results = []
        for head in range(2):
            q, kv, probs = block_probs(b, block, head)
            up = low(head_lanes(b.d_att[2 * block : 2 * block + 2].reshape(256, 128), head, 1))
            dp = times_transposed(up, kv)
            ds = low(probs * (dp - jnp.sum(dp * probs, -1, keepdims=True)))
            b.dkv[:count] += transposed_times(ds, low(q * 0.125)) + transposed_times(low(probs), up)
            results.append(matmul(ds, kv) * 0.125)
        joint = jnp.where(lanes() < 64, results[0], pltpu.roll(results[1], 64, 1))
        b.out[2 * block : 2 * block + 2, :, :128] = low(joint).reshape(2, 128, 128)
    for j in range(8):
        b.out[j, :, 128:] = low(b.dkv[j * 128 : j * 128 + 128])
    exchange = moves.mates(lambda j: b.out.at[j], b.d_packed.at[seq])
    ring.advance(0)
    p2_load.wait()
    arrived(exchange)
    ring1.forward(0)
    ring.forward(1)
    b.d_qk[...] = jnp.zeros_like(b.d_qk)
    for chunk in range(8):
        cols = slice(chunk * 128, chunk * 128 + 128)
        head, place = chunk % 4, slice(chunk // 4 * 128, chunk // 4 * 128 + 128)
        for m in range(2):
            v = b.p2[m * 128 : m * 128 + 128, cols]
            up = b.d_packed[m * 4 + head, :, place].astype(F32)
            r = lax.rsqrt(head_mean(v * v, b.ones[...]) + EPSILON)
            dy = up * b.cosine[...] + half_turn(up * b.sine[...])
            t = dy * qk_gain(b, chunk)
            dv = r * (t - v * (r * r * head_mean(t * v, b.ones[...])))
            b.d_qk[chunk // 4 : chunk // 4 + 1] += jnp.sum(dy * (v * r), 0, keepdims=True)
            if chunk >= 4:
                dv = jnp.where(lanes() < 64, dv, up)
            b.dp2[m * 128 : m * 128 + 128, cols] = low(dv)
    for copy in attn_loads:
        copy.wait()

    def back2(cols):
        b.partial[:, cols] = times_transposed(b.dp2[...], b.proj[cols, :])

    swaps = swapped_columns(moves, back2, b.partial, b.other)
    staged(
        moves,
        b.normed_t,
        lambda k: b.dp2[:, k * 256 : k * 256 + 256],
        slots(b.su, b.sd),
        places(b.qw0_grad, 2) + places(b.qw1_grad, 2),
    )
    ring.advance(1)
    for swap in swaps:
        swap.wait_recv()
        moves.done(swap)
    unpermuted(b, b.partial, b.other, b.partial)
    ring1.advance(0)
    ring.forward(2)
    norm_back_rows(b.z, b.gains.at[1, 0:1], (b.partial,), b.dh2, b.dz, b.d_mix1)
    ring.finish(2)
    ring1.forward(1)
    ring1.advance(1)
    ring1.forward(2)
    ring1.finish(2)
    ring.settle()
    ring1.settle()
    moves.settle()


def ffn_rings(b, grads, sums):
    cols = (pl.ds(0, 1280), pl.ds(1280, 1024))
    grads = [g.reshape(ring_shape(2304)) for g in grads]
    return [
        Scatter(
            [g.at[..., cols[i]] for g in grads], bufs, [s.at[:, cols[i]] for s in sums],
            b.ssend.at[i], b.srecv.at[i], b.sload.at[i],
        )
        for i, bufs in enumerate((b.ring, b.ring1))
    ]


def last_kernel(b):
    core, seq = lax.axis_index(S), lax.axis_index(SQ)
    here = chip()
    greet(
        [device_at(moved(here, axis, by)) for axis in range(3) for by in (1, 2, 3)]
        + [sibling_device(), {SQ: lax.rem(seq + 1, 8)}, {SQ: lax.rem(seq + 7, 8)}]
    )
    moves = Moves(b.local, b.send, b.recv)

    def mixer_rings(i, grads, bufs, sums):
        parts = [g.reshape(ring_shape(g.shape[-1])) for g in grads]
        return Scatter(parts, bufs, sums, b.ssend.at[i], b.srecv.at[i], b.sload.at[i])

    ring, ring1 = ffn_rings(b, (b.gate_grad, b.up_grad, b.down_grad), (b.sum_g, b.sum_u, b.sum_d))
    ring2 = mixer_rings(2, (b.qw0_grad, b.qw1_grad, b.mo1_grad), b.ring2, (b.sum_q0, b.sum_q1, b.sum_mo1))
    ring3 = mixer_rings(3, (b.ci0_grad, b.ci1_grad, b.mt_grad), b.ring3, (b.sum_c0, b.sum_c1, b.sum_mt))
    ring2.start(0)
    norm_rows(b.h1, b.gains.at[0, 1:2], b.normed)
    transpose_into(b.normed, b.normed_t)
    transpose_into(b.dz_in, b.turned)
    mo0_load = moves.local(b.mo0_in, b.mo)
    p1_load = moves.local(b.p1_in, b.p1)
    ci_loads = [moves.local(w, b.proj.at[:, pl.ds(i * 768, 768)]) for i, w in enumerate((b.ci0, b.ci1))]
    fill_perm(b.perm)

    def tick3():
        ring2.forward(0)

    def tick5():
        ring.start(0)
        ring2.advance(0)

    def tick7():
        ring2.forward(1)

    ffn_loop(
        b, (b.gate0, b.up0, b.down0), (b.gate_grad, b.up_grad, b.down_grad),
        b.normed, b.normed_t, b.dz_in, b.turned, b.partial, None, {3: tick3, 5: tick5, 7: tick7}, False, 5,
    )
    ring1.start(0)
    swap = moves.sibling(b.partial, b.other0)
    ring.forward(0)
    ring2.advance(1)
    swap.wait_recv()
    moves.done(swap)
    norm_back_rows(b.h1, b.gains.at[0, 1:2], (b.partial, b.other0), b.dz_in, b.dh1, b.d_ffn0)

    def rounded0(rows):
        b.do[rows] = low(b.dh1[rows])

    by_rows(256, rounded0)
    mo0_load.wait()
    p1_load.wait()

    def mixed(i, carry):
        rows = pl.ds(pl.multiple_of(core * 512 + i * 128, 128), 128)
        cols = pl.ds(pl.multiple_of(i * 128, 128), 128)
        middle_cols = pl.ds(pl.multiple_of(512 + i * 128, 128), 128)
        dm = times_transposed(b.do[...], b.mo[rows, :])
        taps = b.taps[:, cols]
        for m in range(2):
            part = slice(m * 128, m * 128 + 128)
            conv = sum(taps[j : j + 1] * b.pad[m, 6 + j : 134 + j, cols] for j in range(3))
            b.dp1[part, middle_cols] = low(dm[part] * conv)
            b.dconv[m, :128, cols] = dm[part] * b.p1[part, middle_cols]
        return carry

    lax.fori_loop(0, 4, mixed, 0)
    rim = moves.remote(b.dconv.at[:, pl.ds(0, 8)], b.rim, {SQ: lax.rem(seq + 7, 8)})
    transpose_into(b.m1, b.turned)
    staged(moves, b.turned, lambda k: own_columns(b.do, k), slots(b.sg), places(b.mt_grad, 2))
    ring2.forward(2)
    ring1.forward(0)
    norm_rows(b.x, b.gains.at[0, 0:1], b.normed)
    permuted(b.normed, b.perm, b.high)
    transpose_into(b.high, b.normed_t)
    rim.wait_recv()
    b.dconv[:, 128:] = jnp.where(seq < 7, b.rim[...], 0.0)
    b.d_taps[...] = jnp.zeros_like(b.d_taps)

    def conv_back(i, carry):
        cols = pl.ds(pl.multiple_of(i * 128, 128), 128)
        last_cols = pl.ds(pl.multiple_of(1024 + i * 128, 128), 128)
        taps = b.taps[:, cols]
        for m in range(2):
            part = slice(m * 128, m * 128 + 128)
            dconv = b.dconv[m, :128, cols]
            for j in range(3):
                b.d_taps[j : j + 1, cols] += jnp.sum(dconv * b.pad[m, 6 + j : 134 + j, cols], 0, keepdims=True)
            dbx = sum(taps[2 - j : 3 - j] * b.dconv[m, j : 128 + j, cols] for j in range(3))
            b.dp1[part, cols] = low(dbx * b.p1[part, last_cols])
            b.dp1[part, last_cols] = low(dbx * b.p1[part, cols])
        return carry

    lax.fori_loop(0, 4, conv_back, 0)
    for x in range(4):
        tile = low(b.d_taps[:, x * 128 : x * 128 + 128])
        tile = jnp.broadcast_to(jnp.concatenate([tile, tile], 0), (16, 16, 128))
        b.wu[0, x * 256 : x * 256 + 256, :128] = tile.reshape(256, 128)
    moves.keep(b.wu.at[0, :, pl.ds(0, 128)], b.mt_grad.at[:, pl.ds(512, 128)])
    staged(
        moves,
        b.normed_t,
        lambda k: b.dp1[:, k * 256 : k * 256 + 256],
        slots(b.su, b.sd, b.wg),
        places(b.ci0_grad, 3) + places(b.ci1_grad, 3),
    )
    moves.flush()
    ring3.start(0)
    ring2.finish(2)
    for copy in ci_loads:
        copy.wait()

    def back1(cols):
        b.partial[:, cols] = times_transposed(b.dp1[...], b.proj[cols, :])

    swaps = swapped_columns(moves, back1, b.partial, b.other)
    ring.advance(0)
    for swap in swaps:
        swap.wait_recv()
        moves.done(swap)
    unpermuted(b, b.partial, b.other, b.partial)
    norm_back_rows(b.x, b.gains.at[0, 0:1], (b.partial,), b.dh1, b.do, b.d_mix0)

    moves.keep(b.do.at[:, core_columns(512)], b.dx_out)

    first = core == 0
    small = Small(b.sums, b.qk_other, b.arrivals, b.small_send, b.small_recv)
    b.sums[0] = jnp.zeros((8, 1024), F32)
    b.sums[0, 0:1] = jnp.sum(jnp.where(first, b.d_mix0[...], b.d_mix1[...]), 0, keepdims=True)
    b.sums[0, 1:2] = jnp.sum(jnp.where(first, b.d_ffn0[...], b.d_ffn1[...]), 0, keepdims=True)
    small.sibling(b.d_qk).start()
    small.sibling(b.d_qk).wait_recv()
    b.sums[0, 2:4, :128] = b.d_qk[0:2] + b.qk_other[0:2]
    small.start(0)
    ring.forward(1)
    ring1.advance(0)
    ring3.forward(0)
    small.finish(0)
    small.start(1)
    ring.advance(1)
    ring1.forward(1)
    ring3.advance(0)
    small.finish(1)
    small.start(2)
    ring.forward(2)
    ring1.advance(1)
    ring3.forward(1)
    small.finish(2)
    b.small[...] = b.sums[3]
    ring.finish(2)
    ring1.forward(2)
    ring3.advance(1)
    ring1.finish(2)
    ring3.forward(2)
    ring3.finish(2)

    mine = (pl.ds(pl.multiple_of(core * 8, 8), 8), pl.ds(pl.multiple_of(8 - core * 8, 8), 8))
    column = 0
    for ref in (b.sum_c0, b.sum_c1, b.sum_q0, b.sum_q1):
        width = ref.shape[1]
        home = b.mix_out.at[core, :, pl.ds(column, width)]
        moves.keep(ref.at[mine[0]], home)
        moves.sibling(ref.at[mine[1]], home)
        column += width
    pairs = (
        (b.gate_out, 2304, (b.sum_g, b.sum_g1)),
        (b.up_out, 2304, (b.sum_u, b.sum_u1)),
        (b.down_out, 2304, (b.sum_d, b.sum_d1)),
        (b.mo_out, 512, (b.sum_mt, b.sum_mo1)),
    )

    def trade(k, block):
        out, n, sources = pairs[k]
        home = out.at[block]
        keep = pltpu.make_async_copy(sources[block].at[:, pl.ds(0, n)], home, b.trade.at[k])
        give = pltpu.make_async_remote_copy(
            src_ref=sources[1 - block].at[:, pl.ds(0, n)],
            dst_ref=home,
            send_sem=b.trade.at[4 + k],
            recv_sem=b.trade.at[8 + k],
            device_id=sibling_device(),
            device_id_type=MESH,
        )
        return keep, give

    for block in range(2):

        @pl.when(core == block)
        def _():
            for k in range(4):
                for copy in trade(k, block):
                    copy.start()

    for k in range(4):
        keep, give = trade(k, 0)
        keep.wait()
        give.wait()
    for each in (ring, ring1, ring2, ring3):
        each.settle()
    small.settle()
    small.sibling(b.d_qk).wait_send()
    for copy in moves.sent[-4:]:
        copy.wait_recv()
    moves.settle()


def own_columns(ref, k):
    return ref[:, pl.ds(pl.multiple_of(lax.axis_index(S) * 512 + k * 256, 256), 256)]


def ring_scratch(first, widths):
    return {first + str(i): s for i, s in enumerate(scatter_scratch(widths))}


def ring_names(*widths):
    return [ring_scratch(chr(97 + i), w) for i, w in enumerate(widths)]


def sums(width, where=None):
    return vm(16, width) if where is None else ((16, width), F32, where)


def backward(qk, cosine, sine, w):
    thin, partial_gain = ((1024, 512), BF, ANY), ((8, 1024), F32, VM)
    rings = ring_names((1280,) * 3, (1024,) * 3)

    def body(b):
        b.ring, b.ring1 = [[getattr(b, name) for name in ring] for ring in rings]
        backward_kernel(b)

    return launch(
        body,
        "backward",
        3,
        dict(
            gains=(w.gains_out, VM), qk=(qk, VM), cosine=(cosine, VM), sine=(sine, VM),
            dh2=(w.dh2, VM), att=(w.att_out, VM), z=(w.z_out, VM),
            qw0=(flat(w.qw0_out), ANY), qw1=(flat(w.qw1_out), ANY), mo1_in=(flat(w.mo1_out), ANY),
            packed_in=(w.packed_out, ANY), p2_in=(w.p2_out, ANY),
            rg=(w.gate_grad, ANY), ru=(w.up_grad, ANY), rd=(w.down_grad, ANY),
        ),
        dict(
            qw0_grad=thin, qw1_grad=thin, mo1_grad=thin, d_qk=((8, 128), F32, VM), d_mix1=partial_gain,
            dz=((256, 1024), BF, VM), sum_g=sums(2304, VM), sum_u=sums(2304, VM), sum_d=sums(2304, VM),
        ),
        dict(
            mo=bf(1024, 1024), proj=bf(1024, 1024), perm=bf(1024, 1024), ones=vm(128, 128),
            packed=bf(8, 128, 256), p2=vm(256, 1024), do=bf(256, 1024),
            out_att=bf(8, 128, 128), d_att=bf(8, 128, 128), turned=bf(1024, 256), dkv=vm(1024, 128), out=bf(8, 128, 256),
            d_packed=bf(8, 128, 256), normed=bf(256, 1024), normed_t=bf(1024, 256), dp2=bf(256, 1024),
            high=bf(256, 1024), rest=bf(256, 1024), partial=vm(256, 1024), other=vm(256, 1024),
            sg=bf(2, 1024, 256), su=bf(2, 1024, 256), sd=bf(2, 1024, 256),
            local=dma(24), send=dma(24), recv=dma(24),
            ssend=dma(2, 54), srecv=dma(2, 54), sload=dma(2, 36), **rings[0], **rings[1],
        ),
    )


def last(x, w, back):
    wide, mid = [((1024, n), BF, ANY) for n in (2304, 768)]
    rings = ring_names((1280,) * 3, (1024,) * 3, (512,) * 3, (768, 768, 640))

    def body(b):
        b.ring, b.ring1, b.ring2, b.ring3 = [[getattr(b, name) for name in ring] for ring in rings]
        last_kernel(b)

    def out(*shape, where=ANY):
        return (shape, F32, where)

    return launch(
        body,
        "last",
        4,
        dict(
            gains=(w.gains_out, VM), h1=(w.h1_out, VM), dz_in=(back.dz, VM), d_qk=(back.d_qk, VM), d_mix1=(back.d_mix1, VM),
            gate0=(flat(w.gate0_out), ANY), up0=(flat(w.up0_out), ANY), down0=(flat(w.down0_out), ANY),
            qw0_grad=(back.qw0_grad, ANY), qw1_grad=(back.qw1_grad, ANY), mo1_grad=(back.mo1_grad, ANY),
            x=(x, VM), taps=(w.taps_out, VM), m1=(w.m1_out, VM), pad=(w.pad_out, VM), d_ffn1=(w.d_ffn, VM),
            mo0_in=(flat(w.mo0_out), ANY), p1_in=(w.p1_out, ANY), ci0=(flat(w.ci0_out), ANY), ci1=(flat(w.ci1_out), ANY),
            sum_g1=(back.sum_g, VM), sum_u1=(back.sum_u, VM), sum_d1=(back.sum_d, VM),
        ),
        dict(
            gate_grad=wide, up_grad=wide, down_grad=wide, ci0_grad=mid, ci1_grad=mid, mt_grad=((1024, 640), BF, ANY),
            dx_out=((256, 512), BF, ANY), small=out(8, 1024, where=VM), mix_out=out(2, 8, 2560),
            gate_out=out(2, 16, 2304), up_out=out(2, 16, 2304), down_out=out(2, 16, 2304), mo_out=out(2, 16, 512),
            sum_mt=out(16, 640, where=VM),
        ),
        dict(
            mo=bf(1024, 1024), proj=bf(1024, 1536), perm=bf(1024, 1024), p1=vm(256, 1536), do=bf(256, 1024),
            turned=bf(1024, 256), normed=bf(256, 1024), normed_t=bf(1024, 256), high=bf(256, 1024), rest=bf(256, 1024),
            partial=vm(256, 1024), other=vm(256, 1024), other0=vm(256, 1024), dh1=vm(256, 1024),
            dp1=bf(256, 1536), dconv=vm(2, 136, 512), rim=vm(2, 8, 512), d_taps=vm(8, 512),
            d_ffn0=vm(8, 1024), d_mix0=vm(8, 1024), sum_q0=sums(512), sum_q1=sums(512),
            sum_mo1=sums(512), sum_g=sums(2304), sum_u=sums(2304), sum_d=sums(2304), sum_c0=sums(768), sum_c1=sums(768),
            sums=vm(4, 8, 1024), qk_other=vm(8, 128), arrivals=vm(9, 8, 1024), small_send=dma(10), small_recv=dma(10),
            local=dma(24), send=dma(20), recv=dma(20), trade=dma(12),
            ssend=dma(4, 54), srecv=dma(4, 54), sload=dma(4, 36), **ffn_scratch(),
            **rings[0], **rings[1], **rings[2], **rings[3],
        ),
    )


def low(v):
    return v.astype(BF)


def matmul(left, right):
    return jnp.dot(left, right, preferred_element_type=F32)


def times_transposed(left, right):
    return lax.dot_general(left, right, (((1,), (1,)), ((), ())), preferred_element_type=F32)


def transposed_times(left, right):
    return lax.dot_general(left, right, (((0,), (0,)), ((), ())), preferred_element_type=F32)


def both_halves(conv_in, qkv):
    b = conv_in.reshape(8, 3, 2, 512).transpose(2, 0, 1, 3).reshape(2, 8, 1536)
    q = qkv[:, :1024].reshape(8, 2, 512).transpose(1, 0, 2)
    kv = qkv[:, 1024:].reshape(8, 2, 2, 4, 64).transpose(2, 0, 3, 1, 4).reshape(2, 8, 512)
    return jnp.concatenate([b, q, kv], 2)


def from_halves(grads):
    conv = grads[:, :, :1536].reshape(2, 8, 3, 512).transpose(1, 2, 0, 3).reshape(8, 3072)
    q = grads[:, :, 1536:2048].transpose(1, 0, 2).reshape(8, 1024)
    kv = grads[:, :, 2048:].reshape(2, 8, 4, 2, 64).transpose(1, 3, 0, 2, 4).reshape(8, 1024)
    return conv, jnp.concatenate([q, kv], 1)


def rope_tables():
    positions = (lax.axis_index(SQ) * 128 + jnp.arange(128)).astype(F32)
    frequency = 1000000.0 ** (-jnp.arange(32).astype(F32) * 2.0 / 64)
    angles = positions[:, None] * frequency[None, :]
    cosine, sine = jnp.cos(angles), jnp.sin(angles)
    return jnp.concatenate([cosine] * 4, 1), jnp.concatenate([-sine, sine] * 2, 1)


def shards(
    inputs,
    cotangent,
    conv_in,
    conv_kernel,
    qkv_weight,
    qk_gain,
    mix_gain,
    ffn_gain,
    mix_out,
    w_gate,
    w_up,
    w_down,
):
    place = lax.axis_index((DP, SQ)) % 16 * 8
    x = inputs.reshape(256, 1024)
    cot = cotangent.reshape(256, 1024)
    gains = jnp.pad(jnp.concatenate([mix_gain, ffn_gain], 0).astype(F32), ((0, 6), (0, 0)))
    qk = qk_gain.astype(F32)
    qk = jnp.concatenate([qk, jnp.concatenate([qk[:1], jnp.ones((1, 64), F32)], 0)], 1)
    cosine, sine = rope_tables()
    taps = lax.dynamic_update_slice(jnp.zeros((16, 128), BF), conv_kernel, (0, place))
    mix = both_halves(conv_in, qkv_weight).astype(F32)
    saved = forward(x, cot, gains, qk, cosine, sine, taps, mix, (w_gate[0], w_up[0], w_down[0].T, mix_out[0]))
    end = last(x, saved, backward(qk, cosine, sine, saved))
    conv_in_grad, qkv_grad = from_halves(end.mix_out)
    q_sum, k_sum = end.small[2, :128], end.small[3, :64]

    def whole(halves, axis=1):
        return jnp.concatenate([halves[0], halves[1]], axis)[None]

    return (
        saved.result.reshape(2, 1, 128, 512),
        end.dx_out.reshape(2, 1, 128, 512),
        conv_in_grad,
        lax.dynamic_slice(end.sum_mt, (0, 512 + place), (3, 8)),
        qkv_grad,
        jnp.stack([q_sum[:64] + q_sum[64:], k_sum]),
        end.small[0:1],
        end.small[1:2],
        whole(end.mo_out),
        whole(end.gate_out),
        whole(end.up_out),
        whole(end.down_out.transpose(0, 2, 1), 0),
    )


def solution(mesh):
    every = (S, DP, SQ)
    weight = P(S, (DP, SQ), None)
    tokens = P(None, DP, SQ, None)
    in_specs = (
        tokens,
        tokens,
        P(every, None),
        P(None, every),
        P(every, None),
        P(),
        P(S, None),
        P(S, None),
        weight,
        weight,
        weight,
        P(S, None, (DP, SQ)),
    )
    tokens = P(None, DP, SQ, S)
    out_specs = (
        tokens,
        tokens,
        P(every, None),
        P(None, every),
        P(every, None),
        P(),
        P(S, None),
        P(S, None),
        weight,
        weight,
        weight,
        P(S, None, (DP, SQ)),
    )
    return jax.shard_map(shards, mesh=mesh, in_specs=in_specs, out_specs=out_specs, check_vma=False)
```

```python
import functools

import jax
import jax.numpy as jnp
from jax import lax
from jax.experimental import pallas as pl
from jax.experimental.pallas import tpu as pltpu
from jax.sharding import PartitionSpec as P

EPSILON = 1e-05
S, DP, SQ = "section", "dp", "seq"
MESH = pl.DeviceIdType.MESH
ANY = pl.BlockSpec(memory_space=pl.ANY)
BF, F32 = jnp.bfloat16, jnp.float32
ORDERS = ((0, 1, 2), (1, 2, 0), (2, 0, 1))
MIB = 2**20


def chip():
    dp, sq = lax.axis_index(DP), lax.axis_index(SQ)
    return (dp // 2, 2 * (sq % 2) + dp % 2, sq // 2)


def device_at(place):
    x, y, z = place
    return {DP: x * 2 + y % 2, SQ: z * 2 + y // 2}


def moved(place, axis, by):
    return tuple((v + by) % 4 if i == axis else v for i, v in enumerate(place))


def spot(place, kept=(0, 1, 2)):
    x, y, z = place

    def one(axis, value, take):
        if axis not in kept:
            return 0
        return slice(None) if value is None else take(value)

    return (
        one(0, x, lambda v: v),
        one(1, y, lambda v: v % 2),
        one(2, z, lambda v: v),
        one(1, y, lambda v: v // 2),
    )


def halves(width):
    first = (width // 256) * 128
    return (pl.ds(0, first), pl.ds(first, width - first))


def greet(devices):
    barrier = pltpu.get_barrier_semaphore()
    for device in devices:
        pl.semaphore_signal(barrier, inc=1, device_id=device, device_id_type=MESH)
    pl.semaphore_wait(barrier, len(devices))


class Gather:
    def __init__(self, bufs, send, recv, turn=0):
        self.bufs, self.send, self.recv, self.turn = bufs, send, recv, turn
        self.here = chip()

    def copy(self, colour, phase, kind):
        order = ORDERS[colour]
        axis, done = order[phase], order[:phase]
        buf = self.bufs[colour]
        half = halves(buf.shape[-1])
        step, part, to = ((0, 0, 1), (0, 1, 1), (0, 1, -1), (0, 0, -1), (-1, 0, 1), (1, 1, -1))[kind]
        source = moved(self.here, axis, step)
        block = tuple(None if i in done else v for i, v in enumerate(source))
        ref = buf.at[spot(block) + (slice(None), half[part])]
        slot = (colour * 3 + (phase + self.turn) % 3) * 6 + kind
        return pltpu.make_async_remote_copy(
            src_ref=ref,
            dst_ref=ref,
            send_sem=self.send.at[slot],
            recv_sem=self.recv.at[slot],
            device_id=device_at(moved(self.here, axis, to)),
            device_id_type=MESH,
        )

    def start(self, phase):
        for pair in ((0, 2), (1, 3)):
            for kind in pair:
                for colour in range(3):
                    self.copy(colour, phase, kind).start()

    def forward(self, phase):
        for got, then in ((0, 4), (2, 5)):
            for colour in range(3):
                self.copy(colour, phase, got).wait_recv()
                self.copy(colour, phase, then).start()

    def finish(self, phase):
        for kind in (1, 3, 4, 5):
            for colour in range(3):
                self.copy(colour, phase, kind).wait_recv()

    def settle(self, phases=range(3)):
        for phase in phases:
            for kind in range(6):
                for colour in range(3):
                    self.copy(colour, phase, kind).wait_send()


def lead(kept):
    return (4 if 0 in kept else 1, 2 if 1 in kept else 1, 4 if 2 in kept else 1, 2 if 1 in kept else 1)


def one_block(place, axis):
    x, y, z = place
    every = slice(None)
    return (
        pl.ds(x, 1) if axis == 0 else every,
        pl.ds(y % 2, 1) if axis == 1 else every,
        pl.ds(z, 1) if axis == 2 else every,
        pl.ds(y // 2, 1) if axis == 1 else every,
        every,
    )


def scatter_scratch(widths):
    shapes = []
    for colour, width in enumerate(widths):
        for phase in range(3):
            rows = lead(ORDERS[colour][phase + 1 :]) + (16,)
            pair = [rows + (h.size,) for h in halves(width)]
            shapes += pair + pair + [rows + (width,)] * 2
    return [pltpu.VMEM(s, BF) for s in shapes]


class Scatter:
    def __init__(self, parts, bufs, results, send, recv, load):
        self.parts, self.results = parts, results
        self.halves = [halves(p.shape[-1]) for p in parts]
        self.bufs = []
        for c, half in enumerate(self.halves):
            sizes = [h.size for h in half] * 2 + [parts[c].shape[-1]] * 2
            of_colour = [bufs[(c * 3 + p) * 6 :][:6] for p in range(3)]
            self.bufs.append([[b.at[..., pl.ds(0, n)] for b, n in zip(bs, sizes)] for bs in of_colour])
        self.send, self.recv, self.load = send, recv, load
        self.here = chip()

    def source(self, colour, phase, by, side):
        axis = ORDERS[colour][phase]
        block = one_block(moved(self.here, axis, by), axis)
        if phase == 0:
            return self.parts[colour].at[block + (self.halves[colour][side],)]
        return self.bufs[colour][phase - 1][2 + side].at[block + (slice(None),)]

    def loads(self, colour, phase, which):
        side = which % 2
        by = 0 if which >= 2 else (1, -1)[side]
        target = self.bufs[colour][phase][which]
        slot = (colour * 3 + phase) * 4 + which
        return pltpu.make_async_copy(self.source(colour, phase, by, side), target, self.load.at[slot])

    def copy(self, colour, phase, kind):
        half = self.halves[colour]
        bufs = self.bufs[colour][phase]
        side = kind % 2
        to = (1, -1)[side]
        last = bufs[4 + side]
        if kind < 2:
            src, dst = self.source(colour, phase, 2, side), bufs[2 + side]
        elif kind < 4:
            src, dst = self.source(colour, phase, to, 1 - side), last.at[..., half[1 - side]]
        else:
            src, dst = bufs[side], last.at[..., half[side]]
        slot = (colour * 3 + phase) * 6 + kind
        return pltpu.make_async_remote_copy(
            src_ref=src,
            dst_ref=dst,
            send_sem=self.send.at[slot],
            recv_sem=self.recv.at[slot],
            device_id=device_at(moved(self.here, ORDERS[colour][phase], to)),
            device_id_type=MESH,
        )

    def start(self, phase, colours=(0, 1, 2)):
        for colour in colours:
            for which in range(2):
                self.loads(colour, phase, which).start()
        for kind in range(4):
            for colour in colours:
                self.copy(colour, phase, kind).start()

    def forward(self, phase):
        for side in range(2):
            for colour in range(3):
                self.loads(colour, phase, side).wait()
                self.copy(colour, phase, side).wait_recv()
                bufs = self.bufs[colour][phase]
                added(bufs[side], (bufs[2 + side],), bufs[side])
                self.copy(colour, phase, 4 + side).start()
                self.loads(colour, phase, 2 + side).start()

    def advance(self, phase):
        for colour in range(3):
            self.finish(phase, (colour,))
            self.start(phase + 1, (colour,))

    def finish(self, phase, colours=(0, 1, 2)):
        for colour in colours:
            for which in (2, 3):
                self.loads(colour, phase, which).wait()
            for kind in range(2, 6):
                self.copy(colour, phase, kind).wait_recv()
            bufs = self.bufs[colour][phase]
            for side, half in enumerate(self.halves[colour]):
                last = [bufs[4 + i].at[..., half] for i in range(2)]
                out = bufs[2 + side] if phase < 2 else self.results[colour].at[:, half]
                added(bufs[2 + side], last, out)

    def settle(self):
        for phase in range(3):
            for kind in range(6):
                for colour in range(3):
                    self.copy(colour, phase, kind).wait_send()


def added(base, others, out):
    sizes = base.shape[:4]
    _, b, c, d = sizes

    def step(i, carry):
        at = (i // (b * c * d), (i // (c * d)) % b, (i // d) % c, i % d)
        total = base[at].astype(F32)
        for other in others:
            total = total + other[at].astype(F32)
        if len(out.shape) == 2:
            out[...] = total.astype(out.dtype)
        else:
            out[at] = total.astype(out.dtype)
        return carry

    lax.fori_loop(0, sizes[0] * b * c * d, step, 0)


class Small:
    def __init__(self, sums, other, slots, send, recv):
        self.sums, self.other, self.slots = sums, other, slots
        self.send, self.recv = send, recv
        self.here = chip()

    def sibling(self, source):
        return pltpu.make_async_remote_copy(
            src_ref=source,
            dst_ref=self.other,
            send_sem=self.send.at[9],
            recv_sem=self.recv.at[9],
            device_id={S: 1 - lax.axis_index(S)},
            device_id_type=MESH,
        )

    def copy(self, phase, by):
        slot = phase * 3 + by - 1
        return pltpu.make_async_remote_copy(
            src_ref=self.sums.at[phase],
            dst_ref=self.slots.at[slot],
            send_sem=self.send.at[slot],
            recv_sem=self.recv.at[slot],
            device_id=device_at(moved(self.here, phase, by)),
            device_id_type=MESH,
        )

    def start(self, phase):
        for by in (1, 2, 3):
            self.copy(phase, by).start()

    def finish(self, phase):
        for by in (1, 2, 3):
            self.copy(phase, by).wait_recv()
        one, two, three = [self.slots[phase * 3 + i] for i in range(3)]
        self.sums[phase + 1] = (self.sums[phase] + two) + (one + three)

    def settle(self):
        for phase in range(3):
            for by in (1, 2, 3):
                self.copy(phase, by).wait_send()


class Bag:
    def __init__(self, **items):
        self.__dict__.update(items)


def launch(body, name, cid, ins, outs, scratch):
    def kernel(*refs):
        body(Bag(**dict(zip([*ins, *outs, *scratch], refs))))

    got = pl.pallas_call(
        kernel,
        name=name,
        out_shape=[jax.ShapeDtypeStruct(shape, dtype) for shape, dtype, _ in outs.values()],
        in_specs=[where for _, where in ins.values()],
        out_specs=[where for _, _, where in outs.values()],
        scratch_shapes=list(scratch.values()),
        compiler_params=pltpu.CompilerParams(
            collective_id=cid, has_side_effects=True, vmem_limit_bytes=60 * MIB
        ),
    )(*[value for value, _ in ins.values()])
    return Bag(**dict(zip(outs, got)))


VM = pl.BlockSpec(memory_space=pltpu.VMEM)


def vm(*shape, dtype=F32):
    return pltpu.VMEM(shape, dtype)


class Moves:
    def __init__(self, local, send, recv):
        self.sems = local, send, recv
        self.kept, self.sent = [], []
        self.locals = self.remotes = 0

    def local(self, src, dst):
        copy = pltpu.make_async_copy(src, dst, self.sems[0].at[self.locals])
        self.locals += 1
        copy.start()
        return copy

    def keep(self, src, dst):
        self.kept.append(self.local(src, dst))

    def remote(self, src, dst, device):
        slot = self.remotes
        self.remotes += 1
        copy = pltpu.make_async_remote_copy(
            src_ref=src,
            dst_ref=dst,
            send_sem=self.sems[1].at[slot],
            recv_sem=self.sems[2].at[slot],
            device_id=device,
            device_id_type=MESH,
        )
        copy.start()
        self.sent.append(copy)
        return copy

    def sibling(self, src, dst):
        return self.remote(src, dst, {S: 1 - lax.axis_index(S)})

    def mates(self, src, dst):
        me = lax.axis_index(SQ)
        copies = [self.remote(src(lax.rem(me + j, 8)), dst, {SQ: lax.rem(me + j, 8)}) for j in range(1, 8)]
        return [self.local(src(me), dst)], copies

    def done(self, copy):
        copy.wait_send()
        self.sent = [c for c in self.sent if c is not copy]

    def flush(self):
        for copy in self.kept:
            copy.wait()
        self.kept = []

    def settle(self):
        self.flush()
        for copy in self.sent:
            copy.wait_send()


def arrived(moves):
    own, copies = moves
    for copy in own:
        copy.wait()
    for copy in copies:
        copy.wait_recv()


def mate_devices():
    me = lax.axis_index(SQ)
    return [{SQ: lax.rem(me + j, 8)} for j in range(1, 8)]


def across_devices():
    here = chip()
    return [device_at(moved(here, axis, by)) for axis in range(2) for by in (1, -1)]


def sibling_device():
    return {S: 1 - lax.axis_index(S)}


def by_rows(rows, step, size=32):
    def body(i, carry):
        step(pl.ds(pl.multiple_of(i * size, size), size))
        return carry

    lax.fori_loop(0, rows // size, body, 0)


def by_columns(width, step, size=256):
    def body(i, carry):
        step(pl.ds(pl.multiple_of(i * size, size), size))
        return carry

    lax.fori_loop(0, width // size, body, 0)


def core_columns(size):
    return pl.ds(pl.multiple_of(lax.axis_index(S) * size, size), size)


def inverse_norm(v):
    return lax.rsqrt(jnp.mean(v * v, axis=-1, keepdims=True) + EPSILON)


def norm_rows(src, gain, dst):
    def step(rows):
        v = src[rows].astype(F32)
        dst[rows] = low(v * inverse_norm(v) * gain[...])

    by_rows(256, step)


def norm_back_rows(src, gain, upstreams, residual, out, d_gain):
    d_gain[...] = jnp.zeros_like(d_gain)

    def step(rows):
        v = src[rows].astype(F32)
        up = sum(u[rows] for u in upstreams)
        r = inverse_norm(v)
        t = up * gain[...]
        dv = r * (t - v * (r * r * jnp.mean(t * v, axis=-1, keepdims=True)))
        out[rows] = (residual[rows].astype(F32) + dv).astype(out.dtype)
        scaled = up * (v * r)
        d_gain[...] += scaled[:8] + scaled[8:16] + scaled[16:24] + scaled[24:]

    by_rows(256, step)


def transpose_into(src, dst):
    def step(cols):
        dst[cols, :] = src[:, cols].astype(F32).T.astype(BF)

    by_columns(1024, step, 128)


def lanes(width=128):
    return lax.broadcasted_iota(jnp.int32, (1, width), 1)


def head_mean(v, ones):
    return jnp.dot(v, ones, precision=lax.Precision.HIGHEST, preferred_element_type=F32)


def qk_gain(b, chunk):
    return b.qk[chunk // 4 : chunk // 4 + 1]


def half_turn(v):
    return jnp.where(lanes() % 64 < 32, pltpu.roll(v, 96, 1), pltpu.roll(v, 32, 1))


def head_lanes(v, head, upper):
    v = v.astype(F32)
    if head != upper:
        v = pltpu.roll(v, 64, 1)
    return jnp.where(lanes() >= 64 if upper else lanes() < 64, v, 0.0)


def block_probs(b, block, head):
    count = 256 * (block + 1)
    q = head_lanes(b.packed[2 * block : 2 * block + 2, :, :128].reshape(256, 128), head, 0)
    kv = b.packed[: 2 * block + 2, :, 128:].reshape(count, 128)
    scores = times_transposed(low(q), kv) * 0.125
    row = lax.broadcasted_iota(jnp.int32, (256, count), 0) + 256 * block
    col = lax.broadcasted_iota(jnp.int32, (256, count), 1)
    e = jnp.exp(jnp.where(row >= col, scores, -1e9))
    return q, kv, e * (1.0 / jnp.sum(e, -1, keepdims=True))


def flat(value):
    return value.reshape(-1, value.shape[-1])


def ring_shape(width):
    return (4, 2, 4, 2, 16, width)


def fill_perm(perm):
    def step(cols):
        p = lax.broadcasted_iota(jnp.int32, (1024, 256), 1) + cols.start
        row = lax.broadcasted_iota(jnp.int32, (1024, 256), 0)
        natural = (p & 8) * 64 + (p >> 4) * 8 + (p & 7)
        perm[:, cols] = jnp.where(row == natural, 1.0, 0.0).astype(BF)

    by_columns(1024, step)


def fill_ones(ones):
    row = lax.broadcasted_iota(jnp.int32, (128, 128), 0)
    col = lax.broadcasted_iota(jnp.int32, (128, 128), 1)
    ones[...] = jnp.where(row // 64 == col // 64, 1.0 / 64.0, 0.0)


def forward_kernel(b):
    core, seq = lax.axis_index(S), lax.axis_index(SQ)
    greet(across_devices() + mate_devices() + [sibling_device()])
    moves = Moves(b.local, b.send, b.recv)
    here = spot(chip())
    half, other_half = core_columns(512), pl.ds(pl.multiple_of(512 - core * 512, 512), 512)

    mine = pl.ds(pl.multiple_of(core * 8, 8), 8)
    waits = [
        moves.local(b.mix_in.at[core], b.mix.at[mine]),
        moves.local(b.gains_in, b.gains.at[core]),
        moves.local(b.taps_in, b.mt.at[here + (slice(None), pl.ds(512, 128))]),
    ]
    swaps = [
        moves.sibling(b.mix_in.at[1 - core], b.mix.at[mine]),
        moves.sibling(b.gains_in, b.gains.at[core]),
    ]
    shards = (
        (b.gate_in, 2304, (b.gate0, b.gate1)),
        (b.up_in, 2304, (b.up0, b.up1)),
        (b.down_in, 2304, (b.down0, b.down1)),
        (b.mo, 512, (b.mt, b.mo1)),
    )

    def trade(k, block):
        w, n, homes = shards[k]
        home = homes[block].at[here + (slice(None), pl.ds(0, n))]
        keep = pltpu.make_async_copy(w.at[:, pl.ds(block * n, n)], home, b.trade.at[k])
        give = pltpu.make_async_remote_copy(
            src_ref=w.at[:, pl.ds((1 - block) * n, n)],
            dst_ref=home,
            send_sem=b.trade.at[4 + k],
            recv_sem=b.trade.at[8 + k],
            device_id=sibling_device(),
            device_id_type=MESH,
        )
        return keep, give

    for block in range(2):

        @pl.when(core == block)
        def _():
            for k in (3, 0, 1, 2):
                for copy in trade(k, block):
                    copy.start()

    for copy in waits:
        copy.wait()
    for copy in swaps:
        copy.wait_recv()
    b.ci0[here] = low(b.mix[:, :768])
    b.ci1[here] = low(b.mix[:, 768:1536])
    b.qw0[here] = low(b.mix[:, 1536:2048])
    b.qw1[here] = low(b.mix[:, 2048:])
    for k in (3, 0, 1, 2):
        keep, give = trade(k, 0)
        keep.wait()
        give.wait_recv()
    moves.keep(b.gains, b.gains_out)

    rings = [
        Gather(bufs, b.gsend.at[i], b.grecv.at[i])
        for i, bufs in enumerate(
            (
                (b.ci0, b.ci1, b.mt),
                (b.gate0, b.up0, b.down0),
                (b.qw0, b.qw1, b.mo1),
                (b.gate1, b.up1, b.down1),
            )
        )
    ]
    ring_a, ring_b, ring_c, ring_d = rings
    firsts = [
        Gather([w.at[..., cols] for w in (b.gate0, b.up0, b.down0)], b.gsend.at[j], b.grecv.at[j], turn)
        for cols, j, turn in ((pl.ds(0, 1280), 1, 0), (pl.ds(1280, 1024), 4, 2))
    ]
    lasts = [
        Gather([w.at[..., pl.ds(768 * i, 768)] for w in (b.gate1, b.up1, b.down1)], b.gsend.at[j], b.grecv.at[j], turn)
        for i, (j, turn) in enumerate(((3, 0), (4, 0), (4, 1)))
    ]
    for ring in rings:
        ring.start(0)
    norm_rows(b.x, b.gains.at[0, 0:1], b.normed)
    fill_perm(b.perm)
    fill_ones(b.ones)
    permuted(b.normed, b.perm, b.turned)
    for ring in rings:
        ring.forward(0)
    ring_a.finish(0)
    ring_a.start(1)
    ring_b.finish(0)
    ring_b.start(1)
    ring_a.forward(1)
    ring_a.finish(1)
    ring_a.start(2)
    ring_b.forward(1)
    ring_c.finish(0)
    ring_c.start(1)
    ring_a.forward(2)
    ring_b.finish(1)
    for ring in firsts:
        ring.start(2)
    ring_a.finish(2)

    def other_mo(source, target):
        return moves.sibling(source.at[..., pl.ds(0, 512)], target)

    mo0_swap = other_mo(b.mt, b.mo0_other)
    ring_d.finish(0)
    for x in range(4):
        rows = flat(b.mt[x, :, :, :, :, 512:]).reshape(16, 16, 128)
        b.taps[:, x * 128 : x * 128 + 128] = jnp.sum(rows.astype(F32), 0)[:8]
    for i, ci in enumerate((b.ci0, b.ci1)):
        for j in range(3):
            cols = slice(j * 256, j * 256 + 256)
            b.p1[:, i * 768 + j * 256 : i * 768 + j * 256 + 256] = matmul(b.turned[...], flat(ci[..., cols]))
    moves.keep(b.p1, b.p1_out)
    ring_c.forward(1)

    def gated(rows):
        b.bx[rows] = low(b.p1[rows, :512] * b.p1[rows, 1024:]).astype(F32)

    by_rows(256, gated)
    for m in range(2):
        b.pad[m, 8:] = b.bx[m * 128 : m * 128 + 128]
    rim = moves.remote(b.pad.at[:, pl.ds(128, 8)], b.rim, {SQ: lax.rem(seq + 1, 8)})
    for ring in firsts:
        ring.forward(2)
    rim.wait_recv()
    b.pad[:, :8] = jnp.where(seq > 0, b.rim[...], 0.0)
    moves.keep(b.pad, b.pad_out)

    def convolve(cols):
        taps = b.taps[:, cols]
        for m in range(2):
            conv = sum(taps[j : j + 1] * b.pad[m, 6 + j : 134 + j, cols] for j in range(3))
            rows = slice(m * 128, m * 128 + 128)
            gate = b.p1[rows, pl.ds(pl.multiple_of(cols.start + 512, 128), 128)]
            b.m1[rows, pl.ds(pl.multiple_of(core * 512 + cols.start, 128), 128)] = low(gate * conv)

    by_columns(512, convolve, 128)
    swap = moves.sibling(b.m1.at[:, half], b.m1.at[:, half])
    swap.wait_recv()
    moves.keep(b.m1, b.m1_out)
    moves.keep(b.taps, b.taps_out)
    mo0_swap.wait_recv()
    b.h1[:, half] = b.x[:, half].astype(F32) + matmul(b.m1[...], flat(b.mt[..., :512]))
    b.h1[:, other_half] = b.x[:, other_half].astype(F32) + matmul(b.m1[...], flat(b.mo0_other[...]))
    moves.keep(b.h1, b.h1_out)
    norm_rows(b.h1, b.gains.at[0, 1:2], b.normed)
    ring_c.finish(1)
    ring_c.start(2)
    ring_d.start(1)

    def hidden(cols):
        g = matmul(b.normed[...], flat(b.gate0[..., cols]))
        u = matmul(b.normed[...], flat(b.up0[..., cols]))
        b.active[:, cols] = low(g / (1.0 + jnp.exp(-g)) * u)

    firsts[0].finish(2)
    by_columns(1280, hidden)

    def contract_first(x, carry):
        cols = pl.ds(pl.multiple_of(x * 256, 256), 256)
        b.f[:, cols] = times_transposed(b.active[:, :1280], flat(b.down0[x, :, :, :, :, :1280]))
        return carry

    lax.fori_loop(0, 4, contract_first, 0)
    firsts[1].finish(2)
    by_columns(1024, lambda cols: hidden(pl.ds(pl.multiple_of(cols.start + 1280, 256), 256)))
    ring_d.forward(1)
    ring_c.forward(2)

    def contract(cols):
        down = flat(b.down0[cols.start // 256, :, :, :, :, 1280:])
        b.f[:, cols] += times_transposed(b.active[:, 1280:], down)

    swaps = swapped_columns(moves, contract, b.f, b.f_other)
    ring_d.finish(1)
    lasts[0].start(2)
    ring_c.finish(2)
    mo1_swap = other_mo(b.mo1, b.mo1_other)
    for swap in swaps:
        swap.wait_recv()

    def passed(rows):
        b.z[rows] = low(b.h1[rows] + (b.f[rows] + b.f_other[rows]))

    by_rows(256, passed)
    for swap in swaps:
        moves.done(swap)
    moves.keep(b.z, b.z_out)

    norm_rows(b.z, b.gains.at[1, 0:1], b.normed)
    permuted(b.normed, b.perm, b.turned)
    lasts[0].forward(2)
    for i, qw in enumerate((b.qw0, b.qw1)):
        for j in range(2):
            cols = slice(j * 256, j * 256 + 256)
            b.p2[:, i * 512 + j * 256 : i * 512 + j * 256 + 256] = matmul(b.turned[...], flat(qw[..., cols]))
    moves.keep(b.p2, b.p2_out)
    for chunk in range(8):
        cols = slice(chunk * 128, chunk * 128 + 128)
        head, place = chunk % 4, pl.ds(chunk // 4 * 128, 128)
        for m in range(2):
            v = b.p2[m * 128 : m * 128 + 128, cols]
            y = v * lax.rsqrt(head_mean(v * v, b.ones[...]) + EPSILON) * qk_gain(b, chunk)
            y = y * b.cosine[...] + half_turn(y) * b.sine[...]
            if chunk >= 4:
                y = jnp.where(lanes() < 64, y, v)
            b.out[m * 4 + head, :, place] = low(y)
    exchange = moves.mates(lambda j: b.out.at[j], b.packed.at[seq])
    lasts[1].start(2)
    for ring_out, ref in (
        (b.ci0_out, b.ci0), (b.ci1_out, b.ci1), (b.gate0_out, b.gate0), (b.up0_out, b.up0),
        (b.down0_out, b.down0), (b.qw0_out, b.qw0), (b.qw1_out, b.qw1),
    ):
        moves.keep(ref, ring_out)
    transpose_into(b.cot, b.cot_t)
    arrived(exchange)
    moves.keep(b.packed, b.packed_out)
    for block in range(4):
        results = []
        for head in range(2):
            _, kv, probs = block_probs(b, block, head)
            results.append(matmul(low(probs), kv))
        joint = jnp.where(lanes() < 64, pltpu.roll(results[0], 64, 1), results[1])
        b.att_rows[2 * block : 2 * block + 2] = low(joint).reshape(2, 128, 128)
    rows = pl.ds(pl.multiple_of(seq // 4 * 128, 128), 128)
    cols = pl.ds(pl.multiple_of(core * 512 + seq % 4 * 128, 128), 128)
    exchange = moves.mates(lambda j: b.att_rows.at[j], b.att.at[rows, cols])
    lasts[1].forward(2)
    lasts[2].start(2)
    mo1_swap.wait_recv()
    for out, own, other in ((b.mo0_out, b.mt, b.mo0_other), (b.mo1_out, b.mo1, b.mo1_other)):
        moves.keep(own.at[..., pl.ds(0, 512)], out.at[..., half])
        moves.keep(other, out.at[..., other_half])
    arrived(exchange)
    lasts[2].forward(2)
    swap = moves.sibling(b.att.at[:, half], b.att.at[:, half])
    swap.wait_recv()
    moves.keep(b.att, b.att_out)
    b.h2[:, half] = b.z[:, half].astype(F32) + matmul(b.att[...], flat(b.mo1[...]))
    b.h2[:, other_half] = b.z[:, other_half].astype(F32) + matmul(b.att[...], flat(b.mo1_other[...]))

    norm_rows(b.h2, b.gains.at[1, 1:2], b.normed)
    transpose_into(b.normed, b.normed_t)
    ffn_loop(
        b, [flat_ref(w) for w in (b.gate1, b.up1, b.down1)], (b.gate_grad, b.up_grad, b.down_grad),
        b.normed, b.normed_t, b.cot, b.cot_t, b.f, b.f1,
        {3 * i: functools.partial(ring.finish, 2) for i, ring in enumerate(lasts)}, True,
    )
    da_swap = moves.sibling(b.f, b.da_other)
    f_swap = moves.sibling(b.f1.at[:, other_half], b.f1_other)
    da_swap.wait_recv()
    norm_back_rows(b.h2, b.gains.at[1, 1:2], (b.f, b.da_other), b.cot, b.dh2, b.d_ffn)
    f_swap.wait_recv()

    def finish(rows):
        b.result[rows] = low(b.h2[rows, half] + (b.f1[rows, half] + b.f1_other[rows]))

    by_rows(256, finish)
    ring_a.settle()
    ring_c.settle()
    ring_b.settle(range(2))
    ring_d.settle(range(2))
    for ring in firsts + lasts:
        ring.settle(range(2, 3))
    for k in range(4):
        trade(k, 0)[1].wait_send()
    moves.settle()


def flat_ref(ref):
    return ref.reshape(1024, ref.shape[-1])


def swapped_columns(moves, step, ref, target):
    swaps = []
    for i in range(4):
        cols = pl.ds(256 * i, 256)
        step(cols)
        swaps.append(moves.sibling(ref.at[:, cols], target.at[:, cols]))
    return swaps


def permuted(src, perm, dst):
    def step(cols):
        dst[:, cols] = low(matmul(src[...], perm[:, cols]))

    by_columns(1024, step)


def dma(*count):
    return pltpu.SemaphoreType.DMA(count)


def bf(*shape):
    return pltpu.VMEM(shape, BF)


def forward(x, cot, gains_in, qk, cosine, sine, taps, mix_in, weights):
    def saved(*shape, dtype=BF):
        return (shape, dtype, ANY)

    wide, thin = ring_shape(2304), ring_shape(512)
    wg, wu, wd, mo = weights
    return launch(
        forward_kernel,
        "forward",
        1,
        dict(
            x=(x, VM), cot=(cot, VM), gains_in=(gains_in, VM), qk=(qk, VM), cosine=(cosine, VM), sine=(sine, VM),
            taps_in=(taps, VM), mix_in=(mix_in, VM),
            gate_in=(wg, ANY), up_in=(wu, ANY), down_in=(wd, ANY), mo=(mo, ANY),
        ),
        dict(
            gate1=saved(*wide), up1=saved(*wide), down1=saved(*wide), ci0_out=saved(*ring_shape(768)),
            ci1_out=saved(*ring_shape(768)), gate0_out=saved(*wide), up0_out=saved(*wide),
            down0_out=saved(*wide), qw0_out=saved(*thin), qw1_out=saved(*thin),
            mo0_out=saved(*ring_shape(1024)), mo1_out=saved(*ring_shape(1024)),
            gains_out=saved(2, 8, 1024, dtype=F32), taps_out=saved(8, 512, dtype=F32),
            p1_out=saved(256, 1536, dtype=F32), pad_out=saved(2, 136, 512, dtype=F32),
            m1_out=saved(256, 1024), h1_out=saved(256, 1024, dtype=F32), z_out=saved(256, 1024),
            p2_out=saved(256, 1024, dtype=F32), packed_out=saved(8, 128, 256),
            att_out=saved(256, 1024), gate_grad=saved(1024, 2304), up_grad=saved(1024, 2304), down_grad=saved(1024, 2304),
            dh2=((256, 1024), F32, VM), d_ffn=((8, 1024), F32, VM), result=((256, 512), BF, VM),
        ),
        dict(
            mix=vm(16, 2560), gains=vm(2, 8, 1024), taps=vm(8, 512), perm=bf(1024, 1024),
            ci0=bf(*ring_shape(768)), ci1=bf(*ring_shape(768)), mt=bf(*ring_shape(640)),
            gate0=bf(*wide), up0=bf(*wide), down0=bf(*wide), qw0=bf(*thin), qw1=bf(*thin), mo1=bf(*thin),
            mo0_other=bf(*thin), mo1_other=bf(*thin),
            normed=bf(256, 1024), turned=bf(256, 1024), p1=vm(256, 1536), bx=vm(256, 512), pad=vm(2, 136, 512),
            rim=vm(2, 8, 512), m1=bf(256, 1024), h1=vm(256, 1024), active=bf(256, 2304),
            f=vm(256, 1024), f_other=vm(256, 1024), z=bf(256, 1024), p2=vm(256, 1024),
            out=bf(8, 128, 256), packed=bf(8, 128, 256), att_rows=bf(8, 128, 128), att=bf(256, 1024),
            h2=vm(256, 1024), ones=vm(128, 128), normed_t=bf(1024, 256), cot_t=bf(1024, 256), f1=vm(256, 1024),
            f1_other=vm(256, 512), da_other=vm(256, 1024), local=dma(40), send=dma(32), recv=dma(32), trade=dma(12),
            gsend=dma(5, 54), grecv=dma(5, 54), **ffn_scratch(),
        ),
    )


def ffn_scratch():
    return dict(
        wg=bf(2, 1024, 256), wu=bf(2, 1024, 256), wd=bf(2, 1024, 256),
        sg=bf(2, 1024, 256), su=bf(2, 1024, 256), sd=bf(2, 1024, 256),
        load=pltpu.SemaphoreType.DMA((2, 3)), store=pltpu.SemaphoreType.DMA((2, 3)),
    )


def ffn_loop(b, weights, grads, normed, normed_t, df, df_t, da, f=None, ticks=None, gated=False, stored=()):
    ticks = ticks or {}
    bounds = sorted({0, 9, *ticks})

    def columns(i):
        return pl.ds(pl.multiple_of(i * 256, 256), 256)

    def loads(i, slot):
        return [
            pltpu.make_async_copy(w.at[:, columns(i)], d.at[slot], b.load.at[slot, k])
            for k, (w, d) in enumerate(zip(weights, (b.wg, b.wu, b.wd)))
        ]

    def stores(i, slot):
        return [
            pltpu.make_async_copy(s.at[slot], g.at[:, columns(i)], b.store.at[slot, k])
            for k, (g, s) in enumerate(zip(grads, (b.sg, b.su, b.sd)))
        ]

    da[...] = jnp.zeros_like(da)
    if f is not None:
        f[...] = jnp.zeros_like(f)

    def last_stored(begin):
        return max((s for s in stored if s <= begin), default=0)

    def step(begin, end, i, carry):
        slot = lax.rem(i, 2)
        for copy in loads(i, slot):
            copy.wait()

        @pl.when(i + 1 < end)
        def _():
            for copy in loads(i + 1, 1 - slot):
                copy.start()

        gate, up, down = b.wg.at[slot], b.wu.at[slot], b.wd.at[slot]
        g = matmul(normed[...], gate[...])
        u = matmul(normed[...], up[...])
        ds = matmul(df[...], down[...])
        sig = 1.0 / (1.0 + jnp.exp(-g))
        silu = g * sig
        s = low(silu * u)
        dg = low(ds * u * (sig * (1.0 + g * (1.0 - sig))))
        du = low(ds * silu)
        if f is not None:
            f[...] += times_transposed(s, down[...])
        da[...] += times_transposed(dg, gate[...]) + times_transposed(du, up[...])

        @pl.when(i >= last_stored(begin) + 2)
        def _():
            for copy in stores(i - 2, slot):
                copy.wait()

        b.sg[slot] = low(matmul(normed_t[...], dg))
        b.su[slot] = low(matmul(normed_t[...], du))
        b.sd[slot] = low(matmul(df_t[...], s))
        for copy in stores(i, slot):
            copy.start()
        return carry

    for start, end in zip(bounds, bounds[1:]):
        if start in stored:
            for copy in stores(start - 2, start % 2) + stores(start - 1, 1 - start % 2):
                copy.wait()
        if start in ticks:
            ticks[start]()
        if gated or start == 0:
            for copy in loads(start, start % 2):
                copy.start()
        lax.fori_loop(start, end, functools.partial(step, start, end if gated else 9), 0)
    for copy in stores(7, 1) + stores(8, 0):
        copy.wait()


def staged(moves, left_t, right, slots, dests):
    for k, (slot, dest) in enumerate(zip(slots, dests)):
        slot[...] = low(matmul(left_t[...], right(k)))
        moves.keep(slot, dest)


def slots(*stacks):
    return [stack.at[i] for stack in stacks for i in range(2)]


def places(grad, count):
    return [grad.at[:, pl.ds(256 * k, 256)] for k in range(count)]


def unpermuted(b, mine, theirs, out):
    def step(cols):
        total = mine[:, cols] + theirs[:, cols]
        high = low(total)
        b.high[:, cols] = high
        b.rest[:, cols] = low(total - high.astype(F32))

    by_columns(1024, step)

    def turn(cols):
        out[:, cols] = times_transposed(b.high[...], b.perm[cols, :]) + times_transposed(b.rest[...], b.perm[cols, :])

    by_columns(1024, turn)


def backward_kernel(b):
    core, seq = lax.axis_index(S), lax.axis_index(SQ)
    greet(across_devices() + mate_devices() + [sibling_device()])
    moves = Moves(b.local, b.send, b.recv)
    r0, r1, r2, r3 = ffn_rings(b, (b.rg, b.ru, b.rd), (b.sum_g, b.sum_u, b.sum_d))
    r0.start(0)
    mo1_load = moves.local(b.mo1_in, b.mo)
    packed_load = moves.local(b.packed_in, b.packed)
    attn_loads = [
        moves.local(w, b.proj.at[:, pl.ds(i * 512, 512)]) for i, w in enumerate((b.qw0, b.qw1))
    ]
    p2_load = moves.local(b.p2_in, b.p2)
    fill_perm(b.perm)
    fill_ones(b.ones)

    def rounded(rows):
        b.do[rows] = low(b.dh2[rows])

    by_rows(256, rounded)
    mo1_load.wait()
    for h in range(4):
        rows = pl.ds(pl.multiple_of(core * 512 + h * 128, 128), 128)
        d_att = low(times_transposed(b.do[...], b.mo[rows, :]))
        for m in range(2):
            b.out_att[m * 4 + h] = d_att[m * 128 : m * 128 + 128]
    exchange = moves.mates(lambda j: b.out_att.at[j], b.d_att.at[seq])
    r1.start(0)
    r2.start(0)
    transpose_into(b.att, b.turned)
    staged(moves, b.turned, lambda k: own_columns(b.do, k), slots(b.sg), places(b.mo1_grad, 2))
    packed_load.wait()
    norm_rows(b.z, b.gains.at[1, 0:1], b.normed)
    permuted(b.normed, b.perm, b.high)
    transpose_into(b.high, b.normed_t)
    arrived(exchange)
    r3.start(0)
    b.dkv[...] = jnp.zeros_like(b.dkv)
    for block in range(4):
        count = 256 * (block + 1)
        results = []
        for head in range(2):
            q, kv, probs = block_probs(b, block, head)
            up = low(head_lanes(b.d_att[2 * block : 2 * block + 2].reshape(256, 128), head, 1))
            dp = times_transposed(up, kv)
            ds = low(probs * (dp - jnp.sum(dp * probs, -1, keepdims=True)))
            b.dkv[:count] += transposed_times(ds, low(q * 0.125)) + transposed_times(low(probs), up)
            results.append(matmul(ds, kv) * 0.125)
        joint = jnp.where(lanes() < 64, results[0], pltpu.roll(results[1], 64, 1))
        b.out[2 * block : 2 * block + 2, :, :128] = low(joint).reshape(2, 128, 128)
    for j in range(8):
        b.out[j, :, 128:] = low(b.dkv[j * 128 : j * 128 + 128])
    exchange = moves.mates(lambda j: b.out.at[j], b.d_packed.at[seq])
    rings = (r0, r1, r2, r3)
    for each in rings:
        each.forward(0)
    p2_load.wait()
    arrived(exchange)
    b.d_qk[...] = jnp.zeros_like(b.d_qk)
    for chunk in range(8):
        cols = slice(chunk * 128, chunk * 128 + 128)
        head, place = chunk % 4, slice(chunk // 4 * 128, chunk // 4 * 128 + 128)
        for m in range(2):
            v = b.p2[m * 128 : m * 128 + 128, cols]
            up = b.d_packed[m * 4 + head, :, place].astype(F32)
            r = lax.rsqrt(head_mean(v * v, b.ones[...]) + EPSILON)
            dy = up * b.cosine[...] + half_turn(up * b.sine[...])
            t = dy * qk_gain(b, chunk)
            dv = r * (t - v * (r * r * head_mean(t * v, b.ones[...])))
            b.d_qk[chunk // 4 : chunk // 4 + 1] += jnp.sum(dy * (v * r), 0, keepdims=True)
            if chunk >= 4:
                dv = jnp.where(lanes() < 64, dv, up)
            b.dp2[m * 128 : m * 128 + 128, cols] = low(dv)
    for copy in attn_loads:
        copy.wait()

    def back2(cols):
        b.partial[:, cols] = times_transposed(b.dp2[...], b.proj[cols, :])

    for each in rings:
        each.advance(0)
    swaps = swapped_columns(moves, back2, b.partial, b.other)
    staged(
        moves,
        b.normed_t,
        lambda k: b.dp2[:, k * 256 : k * 256 + 256],
        slots(b.su, b.sd),
        places(b.qw0_grad, 2) + places(b.qw1_grad, 2),
    )
    for each in rings:
        each.forward(1)
    for swap in swaps:
        swap.wait_recv()
        moves.done(swap)
    unpermuted(b, b.partial, b.other, b.partial)
    for each in rings:
        each.advance(1)
    norm_back_rows(b.z, b.gains.at[1, 0:1], (b.partial,), b.dh2, b.dz, b.d_mix1)
    for each in rings:
        each.forward(2)
    for each in rings:
        each.finish(2)
        each.settle()
    moves.settle()


def ffn_rings(b, grads, sums):
    widths = [bufs[-1].shape[-1] for bufs in b.rings]
    cols = [pl.ds(sum(widths[:i]), w) for i, w in enumerate(widths)]
    grads = [g.reshape(ring_shape(2304)) for g in grads]
    return [
        Scatter(
            [g.at[..., cols[i]] for g in grads], bufs, [s.at[:, cols[i]] for s in sums],
            b.ssend.at[i], b.srecv.at[i], b.sload.at[i],
        )
        for i, bufs in enumerate(b.rings)
    ]


def last_kernel(b):
    core, seq = lax.axis_index(S), lax.axis_index(SQ)
    here = chip()
    greet(
        [device_at(moved(here, axis, by)) for axis in range(3) for by in (1, 2, 3)]
        + [sibling_device(), {SQ: lax.rem(seq + 1, 8)}, {SQ: lax.rem(seq + 7, 8)}]
    )
    moves = Moves(b.local, b.send, b.recv)

    def mixer_rings(i, grads, bufs, sums):
        parts = [g.reshape(ring_shape(g.shape[-1])) for g in grads]
        return Scatter(parts, bufs, sums, b.ssend.at[i], b.srecv.at[i], b.sload.at[i])

    r0, r1, r2 = ffn_rings(b, (b.gate_grad, b.up_grad, b.down_grad), (b.sum_g, b.sum_u, b.sum_d))
    ring2 = mixer_rings(3, (b.qw0_grad, b.qw1_grad, b.mo1_grad), b.ring2, (b.sum_q0, b.sum_q1, b.sum_mo1))
    ring3 = mixer_rings(4, (b.ci0_grad, b.ci1_grad, b.mt_grad), b.ring3, (b.sum_c0, b.sum_c1, b.sum_mt))
    ring2.start(0)
    norm_rows(b.h1, b.gains.at[0, 1:2], b.normed)
    transpose_into(b.normed, b.normed_t)
    transpose_into(b.dz_in, b.turned)
    mo0_load = moves.local(b.mo0_in, b.mo)
    p1_load = moves.local(b.p1_in, b.p1)
    ci_loads = [moves.local(w, b.proj.at[:, pl.ds(i * 768, 768)]) for i, w in enumerate((b.ci0, b.ci1))]
    fill_perm(b.perm)

    def tick2():
        ring2.forward(0)

    def tick3():
        r0.start(0)

    def tick5():
        ring2.advance(0)

    def tick6():
        r1.start(0)
        r0.forward(0)

    def tick8():
        ring2.forward(1)

    ticks = {2: tick2, 3: tick3, 5: tick5, 6: tick6, 8: tick8}
    ffn_loop(
        b, (b.gate0, b.up0, b.down0), (b.gate_grad, b.up_grad, b.down_grad),
        b.normed, b.normed_t, b.dz_in, b.turned, b.partial, None, ticks, False, (3, 6),
    )
    swap = moves.sibling(b.partial, b.other0)
    ring2.advance(1)
    swap.wait_recv()
    moves.done(swap)
    r2.start(0)
    norm_back_rows(b.h1, b.gains.at[0, 1:2], (b.partial, b.other0), b.dz_in, b.dh1, b.d_ffn0)

    def rounded0(rows):
        b.do[rows] = low(b.dh1[rows])

    by_rows(256, rounded0)
    mo0_load.wait()
    p1_load.wait()

    def mixed(i, carry):
        rows = pl.ds(pl.multiple_of(core * 512 + i * 128, 128), 128)
        cols = pl.ds(pl.multiple_of(i * 128, 128), 128)
        middle_cols = pl.ds(pl.multiple_of(512 + i * 128, 128), 128)
        dm = times_transposed(b.do[...], b.mo[rows, :])
        taps = b.taps[:, cols]
        for m in range(2):
            part = slice(m * 128, m * 128 + 128)
            conv = sum(taps[j : j + 1] * b.pad[m, 6 + j : 134 + j, cols] for j in range(3))
            b.dp1[part, middle_cols] = low(dm[part] * conv)
            b.dconv[m, :128, cols] = dm[part] * b.p1[part, middle_cols]
        return carry

    lax.fori_loop(0, 4, mixed, 0)
    rim = moves.remote(b.dconv.at[:, pl.ds(0, 8)], b.rim, {SQ: lax.rem(seq + 7, 8)})
    r1.forward(0)
    r0.advance(0)
    transpose_into(b.m1, b.turned)
    staged(moves, b.turned, lambda k: own_columns(b.do, k), slots(b.sg), places(b.mt_grad, 2))
    ring2.forward(2)
    norm_rows(b.x, b.gains.at[0, 0:1], b.normed)
    permuted(b.normed, b.perm, b.high)
    transpose_into(b.high, b.normed_t)
    rim.wait_recv()
    b.dconv[:, 128:] = jnp.where(seq < 7, b.rim[...], 0.0)
    b.d_taps[...] = jnp.zeros_like(b.d_taps)

    def conv_back(i, carry):
        cols = pl.ds(pl.multiple_of(i * 128, 128), 128)
        last_cols = pl.ds(pl.multiple_of(1024 + i * 128, 128), 128)
        taps = b.taps[:, cols]
        for m in range(2):
            part = slice(m * 128, m * 128 + 128)
            dconv = b.dconv[m, :128, cols]
            for j in range(3):
                b.d_taps[j : j + 1, cols] += jnp.sum(dconv * b.pad[m, 6 + j : 134 + j, cols], 0, keepdims=True)
            dbx = sum(taps[2 - j : 3 - j] * b.dconv[m, j : 128 + j, cols] for j in range(3))
            b.dp1[part, cols] = low(dbx * b.p1[part, last_cols])
            b.dp1[part, last_cols] = low(dbx * b.p1[part, cols])
        return carry

    lax.fori_loop(0, 4, conv_back, 0)
    r2.forward(0)
    for x in range(4):
        tile = low(b.d_taps[:, x * 128 : x * 128 + 128])
        tile = jnp.broadcast_to(jnp.concatenate([tile, tile], 0), (16, 16, 128))
        b.wu[0, x * 256 : x * 256 + 256, :128] = tile.reshape(256, 128)
    moves.keep(b.wu.at[0, :, pl.ds(0, 128)], b.mt_grad.at[:, pl.ds(512, 128)])
    staged(
        moves,
        b.normed_t,
        lambda k: b.dp1[:, k * 256 : k * 256 + 256],
        slots(b.su, b.sd, b.wg),
        places(b.ci0_grad, 3) + places(b.ci1_grad, 3),
    )
    moves.flush()
    ring3.start(0)
    r1.advance(0)
    r0.forward(1)
    ring2.finish(2)
    for copy in ci_loads:
        copy.wait()

    def back1(cols):
        b.partial[:, cols] = times_transposed(b.dp1[...], b.proj[cols, :])

    swaps = swapped_columns(moves, back1, b.partial, b.other)
    r2.advance(0)
    for swap in swaps:
        swap.wait_recv()
        moves.done(swap)
    unpermuted(b, b.partial, b.other, b.partial)
    norm_back_rows(b.x, b.gains.at[0, 0:1], (b.partial,), b.dh1, b.do, b.d_mix0)

    moves.keep(b.do.at[:, core_columns(512)], b.dx_out)

    first = core == 0
    small = Small(b.sums, b.qk_other, b.arrivals, b.small_send, b.small_recv)
    b.sums[0] = jnp.zeros((8, 1024), F32)
    b.sums[0, 0:1] = jnp.sum(jnp.where(first, b.d_mix0[...], b.d_mix1[...]), 0, keepdims=True)
    b.sums[0, 1:2] = jnp.sum(jnp.where(first, b.d_ffn0[...], b.d_ffn1[...]), 0, keepdims=True)
    small.sibling(b.d_qk).start()
    small.sibling(b.d_qk).wait_recv()
    b.sums[0, 2:4, :128] = b.d_qk[0:2] + b.qk_other[0:2]
    small.start(0)
    r1.forward(1)
    r0.advance(1)
    ring3.forward(0)
    small.finish(0)
    small.start(1)
    r2.forward(1)
    r1.advance(1)
    r0.forward(2)
    ring3.advance(0)
    small.finish(1)
    small.start(2)
    r0.finish(2)
    r2.advance(1)
    r1.forward(2)
    ring3.forward(1)
    small.finish(2)
    b.small[...] = b.sums[3]
    r1.finish(2)
    r2.forward(2)
    ring3.advance(1)
    r2.finish(2)
    ring3.forward(2)
    ring3.finish(2)

    mine = (pl.ds(pl.multiple_of(core * 8, 8), 8), pl.ds(pl.multiple_of(8 - core * 8, 8), 8))
    column = 0
    for ref in (b.sum_c0, b.sum_c1, b.sum_q0, b.sum_q1):
        width = ref.shape[1]
        home = b.mix_out.at[core, :, pl.ds(column, width)]
        moves.keep(ref.at[mine[0]], home)
        moves.sibling(ref.at[mine[1]], home)
        column += width
    pairs = (
        (1024, 2304, (b.sum_g, b.sum_g1)),
        (5632, 2304, (b.sum_u, b.sum_u1)),
        (10240, 2304, (b.sum_d, b.sum_d1)),
        (0, 512, (b.sum_mt, b.sum_mo1)),
    )

    def trade(k, block):
        first, n, sources = pairs[k]
        home = b.block_out.at[:, pl.ds(first + block * n, n)]
        keep = pltpu.make_async_copy(sources[block].at[:, pl.ds(0, n)], home, b.trade.at[k])
        give = pltpu.make_async_remote_copy(
            src_ref=sources[1 - block].at[:, pl.ds(0, n)],
            dst_ref=home,
            send_sem=b.trade.at[4 + k],
            recv_sem=b.trade.at[8 + k],
            device_id=sibling_device(),
            device_id_type=MESH,
        )
        return keep, give

    for block in range(2):

        @pl.when(core == block)
        def _():
            for k in range(4):
                for copy in trade(k, block):
                    copy.start()

    for k in range(4):
        keep, give = trade(k, 0)
        keep.wait()
        give.wait()
    for each in (r0, r1, r2, ring2, ring3):
        each.settle()
    small.settle()
    small.sibling(b.d_qk).wait_send()
    for copy in moves.sent[-4:]:
        copy.wait_recv()
    moves.settle()


def own_columns(ref, k):
    return ref[:, pl.ds(pl.multiple_of(lax.axis_index(S) * 512 + k * 256, 256), 256)]


def ring_scratch(first, widths):
    return {first + str(i): s for i, s in enumerate(scatter_scratch(widths))}


def ring_names(*widths):
    return [ring_scratch(chr(97 + i), w) for i, w in enumerate(widths)]


def sums(width, where=None):
    return vm(16, width) if where is None else ((16, width), F32, where)


def backward(qk, cosine, sine, w):
    thin, partial_gain = ((1024, 512), BF, ANY), ((8, 1024), F32, VM)
    rings = ring_names((640,) * 3, (640,) * 3, (512,) * 3, (512,) * 3)

    def body(b):
        b.rings = [[getattr(b, name) for name in ring] for ring in rings]
        backward_kernel(b)

    return launch(
        body,
        "backward",
        3,
        dict(
            gains=(w.gains_out, VM), qk=(qk, VM), cosine=(cosine, VM), sine=(sine, VM),
            dh2=(w.dh2, VM), att=(w.att_out, VM), z=(w.z_out, VM),
            qw0=(flat(w.qw0_out), ANY), qw1=(flat(w.qw1_out), ANY), mo1_in=(flat(w.mo1_out), ANY),
            packed_in=(w.packed_out, ANY), p2_in=(w.p2_out, ANY),
            rg=(w.gate_grad, ANY), ru=(w.up_grad, ANY), rd=(w.down_grad, ANY),
        ),
        dict(
            qw0_grad=thin, qw1_grad=thin, mo1_grad=thin, d_qk=((8, 128), F32, VM), d_mix1=partial_gain,
            dz=((256, 1024), BF, VM), sum_g=sums(2304, VM), sum_u=sums(2304, VM), sum_d=sums(2304, VM),
        ),
        dict(
            mo=bf(1024, 1024), proj=bf(1024, 1024), perm=bf(1024, 1024), ones=vm(128, 128),
            packed=bf(8, 128, 256), p2=vm(256, 1024), do=bf(256, 1024),
            out_att=bf(8, 128, 128), d_att=bf(8, 128, 128), turned=bf(1024, 256), dkv=vm(1024, 128), out=bf(8, 128, 256),
            d_packed=bf(8, 128, 256), normed=bf(256, 1024), normed_t=bf(1024, 256), dp2=bf(256, 1024),
            high=bf(256, 1024), rest=bf(256, 1024), partial=vm(256, 1024), other=vm(256, 1024),
            sg=bf(2, 1024, 256), su=bf(2, 1024, 256), sd=bf(2, 1024, 256),
            local=dma(24), send=dma(24), recv=dma(24),
            ssend=dma(4, 54), srecv=dma(4, 54), sload=dma(4, 36),
            **rings[0], **rings[1], **rings[2], **rings[3],
        ),
    )


def last(x, w, back):
    wide, mid = [((1024, n), BF, ANY) for n in (2304, 768)]
    rings = ring_names((768,) * 3, (768,) * 3, (768,) * 3, (512,) * 3, (768, 768, 640))

    def body(b):
        *b.rings, b.ring2, b.ring3 = [[getattr(b, name) for name in ring] for ring in rings]
        last_kernel(b)

    def out(*shape, where=ANY):
        return (shape, F32, where)

    return launch(
        body,
        "last",
        4,
        dict(
            gains=(w.gains_out, VM), h1=(w.h1_out, VM), dz_in=(back.dz, VM), d_qk=(back.d_qk, VM), d_mix1=(back.d_mix1, VM),
            gate0=(flat(w.gate0_out), ANY), up0=(flat(w.up0_out), ANY), down0=(flat(w.down0_out), ANY),
            qw0_grad=(back.qw0_grad, ANY), qw1_grad=(back.qw1_grad, ANY), mo1_grad=(back.mo1_grad, ANY),
            x=(x, VM), taps=(w.taps_out, VM), m1=(w.m1_out, VM), pad=(w.pad_out, VM), d_ffn1=(w.d_ffn, VM),
            mo0_in=(flat(w.mo0_out), ANY), p1_in=(w.p1_out, ANY), ci0=(flat(w.ci0_out), ANY), ci1=(flat(w.ci1_out), ANY),
            sum_g1=(back.sum_g, VM), sum_u1=(back.sum_u, VM), sum_d1=(back.sum_d, VM),
        ),
        dict(
            gate_grad=wide, up_grad=wide, down_grad=wide, ci0_grad=mid, ci1_grad=mid, mt_grad=((1024, 640), BF, ANY),
            dx_out=((256, 512), BF, ANY), small=out(8, 1024, where=VM), mix_out=out(2, 8, 2560),
            block_out=out(16, 14848),
            sum_mt=out(16, 640, where=VM),
        ),
        dict(
            mo=bf(1024, 1024), proj=bf(1024, 1536), perm=bf(1024, 1024), p1=vm(256, 1536), do=bf(256, 1024),
            turned=bf(1024, 256), normed=bf(256, 1024), normed_t=bf(1024, 256), high=bf(256, 1024), rest=bf(256, 1024),
            partial=vm(256, 1024), other=vm(256, 1024), other0=vm(256, 1024), dh1=vm(256, 1024),
            dp1=bf(256, 1536), dconv=vm(2, 136, 512), rim=vm(2, 8, 512), d_taps=vm(8, 512),
            d_ffn0=vm(8, 1024), d_mix0=vm(8, 1024), sum_q0=sums(512), sum_q1=sums(512),
            sum_mo1=sums(512), sum_g=sums(2304), sum_u=sums(2304), sum_d=sums(2304), sum_c0=sums(768), sum_c1=sums(768),
            sums=vm(4, 8, 1024), qk_other=vm(8, 128), arrivals=vm(9, 8, 1024), small_send=dma(10), small_recv=dma(10),
            local=dma(24), send=dma(20), recv=dma(20), trade=dma(12),
            ssend=dma(5, 54), srecv=dma(5, 54), sload=dma(5, 36), **ffn_scratch(),
            **rings[0], **rings[1], **rings[2], **rings[3], **rings[4],
        ),
    )


def low(v):
    return v.astype(BF)


def matmul(left, right):
    return jnp.dot(left, right, preferred_element_type=F32)


def times_transposed(left, right):
    return lax.dot_general(left, right, (((1,), (1,)), ((), ())), preferred_element_type=F32)


def transposed_times(left, right):
    return lax.dot_general(left, right, (((0,), (0,)), ((), ())), preferred_element_type=F32)


def both_halves(conv_in, qkv):
    b = conv_in.reshape(8, 3, 2, 512).transpose(2, 0, 1, 3).reshape(2, 8, 1536)
    q = qkv[:, :1024].reshape(8, 2, 512).transpose(1, 0, 2)
    kv = qkv[:, 1024:].reshape(8, 2, 2, 4, 64).transpose(2, 0, 3, 1, 4).reshape(2, 8, 512)
    return jnp.concatenate([b, q, kv], 2)


def from_halves(grads):
    conv = grads[:, :, :1536].reshape(2, 8, 3, 512).transpose(1, 2, 0, 3).reshape(8, 3072)
    q = grads[:, :, 1536:2048].transpose(1, 0, 2).reshape(8, 1024)
    kv = grads[:, :, 2048:].reshape(2, 8, 4, 2, 64).transpose(1, 3, 0, 2, 4).reshape(8, 1024)
    return conv, jnp.concatenate([q, kv], 1)


def rope_tables():
    positions = (lax.axis_index(SQ) * 128 + jnp.arange(128)).astype(F32)
    frequency = 1000000.0 ** (-jnp.arange(32).astype(F32) * 2.0 / 64)
    angles = positions[:, None] * frequency[None, :]
    cosine, sine = jnp.cos(angles), jnp.sin(angles)
    return jnp.concatenate([cosine] * 4, 1), jnp.concatenate([-sine, sine] * 2, 1)


def shards(
    inputs,
    cotangent,
    conv_in,
    conv_kernel,
    qkv_weight,
    qk_gain,
    mix_gain,
    ffn_gain,
    mix_out,
    w_gate,
    w_up,
    w_down,
):
    place = lax.axis_index((DP, SQ)) % 16 * 8
    x = inputs.reshape(256, 1024)
    cot = cotangent.reshape(256, 1024)
    gains = jnp.pad(jnp.concatenate([mix_gain, ffn_gain], 0).astype(F32), ((0, 6), (0, 0)))
    qk = qk_gain.astype(F32)
    qk = jnp.concatenate([qk, jnp.concatenate([qk[:1], jnp.ones((1, 64), F32)], 0)], 1)
    cosine, sine = rope_tables()
    taps = lax.dynamic_update_slice(jnp.zeros((16, 128), BF), conv_kernel, (0, place))
    mix = both_halves(conv_in, qkv_weight).astype(F32)
    saved = forward(x, cot, gains, qk, cosine, sine, taps, mix, (w_gate[0], w_up[0], w_down[0].T, mix_out[0]))
    end = last(x, saved, backward(qk, cosine, sine, saved))
    conv_in_grad, qkv_grad = from_halves(end.mix_out)
    q_sum, k_sum = end.small[2, :128], end.small[3, :64]

    mo_grad, gate_grad, up_grad, down_grad = jnp.split(end.block_out, (1024, 5632, 10240), 1)
    return (
        saved.result.reshape(2, 1, 128, 512),
        end.dx_out.reshape(2, 1, 128, 512),
        conv_in_grad,
        lax.dynamic_slice(end.sum_mt, (0, 512 + place), (3, 8)),
        qkv_grad,
        jnp.stack([q_sum[:64] + q_sum[64:], k_sum]),
        end.small[0:1],
        end.small[1:2],
        mo_grad[None],
        gate_grad[None],
        up_grad[None],
        down_grad.T[None],
    )


def solution(mesh):
    every = (S, DP, SQ)
    weight = P(S, (DP, SQ), None)
    tokens = P(None, DP, SQ, None)
    in_specs = (
        tokens,
        tokens,
        P(every, None),
        P(None, every),
        P(every, None),
        P(),
        P(S, None),
        P(S, None),
        weight,
        weight,
        weight,
        P(S, None, (DP, SQ)),
    )
    tokens = P(None, DP, SQ, S)
    out_specs = (
        tokens,
        tokens,
        P(every, None),
        P(None, every),
        P(every, None),
        P(),
        P(S, None),
        P(S, None),
        weight,
        weight,
        weight,
        P(S, None, (DP, SQ)),
    )
    return jax.shard_map(shards, mesh=mesh, in_specs=in_specs, out_specs=out_specs, check_vma=False)
```

```python
import functools

import jax
import jax.numpy as jnp
from jax import lax
from jax.experimental import pallas as pl
from jax.experimental.pallas import tpu as pltpu
from jax.sharding import PartitionSpec as P

EPSILON = 1e-05
S, DP, SQ = "section", "dp", "seq"
MESH = pl.DeviceIdType.MESH
ANY = pl.BlockSpec(memory_space=pl.ANY)
BF, F32 = jnp.bfloat16, jnp.float32
ORDERS = ((0, 1, 2), (1, 2, 0), (2, 0, 1))
MIB = 2**20


def chip():
    dp, sq = lax.axis_index(DP), lax.axis_index(SQ)
    return (dp // 2, 2 * (sq % 2) + dp % 2, sq // 2)


def device_at(place):
    x, y, z = place
    return {DP: x * 2 + y % 2, SQ: z * 2 + y // 2}


def moved(place, axis, by):
    return tuple((v + by) % 4 if i == axis else v for i, v in enumerate(place))


def spot(place, kept=(0, 1, 2)):
    x, y, z = place

    def one(axis, value, take):
        if axis not in kept:
            return 0
        return slice(None) if value is None else take(value)

    return (
        one(0, x, lambda v: v),
        one(1, y, lambda v: v % 2),
        one(2, z, lambda v: v),
        one(1, y, lambda v: v // 2),
    )


def halves(width):
    first = (width // 256) * 128
    return (pl.ds(0, first), pl.ds(first, width - first))


def greet(devices):
    barrier = pltpu.get_barrier_semaphore()
    for device in devices:
        pl.semaphore_signal(barrier, inc=1, device_id=device, device_id_type=MESH)
    pl.semaphore_wait(barrier, len(devices))


class Gather:
    def __init__(self, bufs, send, recv, turn=0):
        self.bufs, self.send, self.recv, self.turn = bufs, send, recv, turn
        self.here = chip()

    def copy(self, colour, phase, kind):
        order = ORDERS[colour]
        axis, done = order[phase], order[:phase]
        buf = self.bufs[colour]
        half = halves(buf.shape[-1])
        step, part, to = ((0, 0, 1), (0, 1, 1), (0, 1, -1), (0, 0, -1), (-1, 0, 1), (1, 1, -1))[kind]
        source = moved(self.here, axis, step)
        block = tuple(None if i in done else v for i, v in enumerate(source))
        ref = buf.at[spot(block) + (slice(None), half[part])]
        slot = (colour * 3 + (phase + self.turn) % 3) * 6 + kind
        return pltpu.make_async_remote_copy(
            src_ref=ref,
            dst_ref=ref,
            send_sem=self.send.at[slot],
            recv_sem=self.recv.at[slot],
            device_id=device_at(moved(self.here, axis, to)),
            device_id_type=MESH,
        )

    def start(self, phase, pairs=((0, 2), (1, 3))):
        for pair in pairs:
            for kind in pair:
                for colour in range(3):
                    self.copy(colour, phase, kind).start()

    def forward(self, phase):
        for got, then in ((0, 4), (2, 5)):
            for colour in range(3):
                self.copy(colour, phase, got).wait_recv()
                self.copy(colour, phase, then).start()

    def finish(self, phase):
        for kind in (1, 3, 4, 5):
            for colour in range(3):
                self.copy(colour, phase, kind).wait_recv()

    def settle(self, phases=range(3)):
        for phase in phases:
            for kind in range(6):
                for colour in range(3):
                    self.copy(colour, phase, kind).wait_send()


def lead(kept):
    return (4 if 0 in kept else 1, 2 if 1 in kept else 1, 4 if 2 in kept else 1, 2 if 1 in kept else 1)


def one_block(place, axis):
    x, y, z = place
    every = slice(None)
    return (
        pl.ds(x, 1) if axis == 0 else every,
        pl.ds(y % 2, 1) if axis == 1 else every,
        pl.ds(z, 1) if axis == 2 else every,
        pl.ds(y // 2, 1) if axis == 1 else every,
        every,
    )


def scatter_scratch(widths):
    shapes = []
    for colour, width in enumerate(widths):
        for phase in range(3):
            rows = lead(ORDERS[colour][phase + 1 :]) + (16,)
            pair = [rows + (h.size,) for h in halves(width)]
            shapes += pair + pair + [rows + (width,)] * 2
    return [pltpu.VMEM(s, BF) for s in shapes]


class Scatter:
    def __init__(self, parts, bufs, results, send, recv, load):
        self.parts, self.results = parts, results
        self.halves = [halves(p.shape[-1]) for p in parts]
        self.bufs = []
        for c, half in enumerate(self.halves):
            sizes = [h.size for h in half] * 2 + [parts[c].shape[-1]] * 2
            of_colour = [bufs[(c * 3 + p) * 6 :][:6] for p in range(3)]
            self.bufs.append([[b.at[..., pl.ds(0, n)] for b, n in zip(bs, sizes)] for bs in of_colour])
        self.send, self.recv, self.load = send, recv, load
        self.here = chip()

    def source(self, colour, phase, by, side):
        axis = ORDERS[colour][phase]
        block = one_block(moved(self.here, axis, by), axis)
        if phase == 0:
            return self.parts[colour].at[block + (self.halves[colour][side],)]
        return self.bufs[colour][phase - 1][2 + side].at[block + (slice(None),)]

    def loads(self, colour, phase, which):
        side = which % 2
        by = 0 if which >= 2 else (1, -1)[side]
        target = self.bufs[colour][phase][which]
        slot = (colour * 3 + phase) * 4 + which
        return pltpu.make_async_copy(self.source(colour, phase, by, side), target, self.load.at[slot])

    def copy(self, colour, phase, kind):
        half = self.halves[colour]
        bufs = self.bufs[colour][phase]
        side = kind % 2
        to = (1, -1)[side]
        last = bufs[4 + side]
        if kind < 2:
            src, dst = self.source(colour, phase, 2, side), bufs[2 + side]
        elif kind < 4:
            src, dst = self.source(colour, phase, to, 1 - side), last.at[..., half[1 - side]]
        else:
            src, dst = bufs[side], last.at[..., half[side]]
        slot = (colour * 3 + phase) * 6 + kind
        return pltpu.make_async_remote_copy(
            src_ref=src,
            dst_ref=dst,
            send_sem=self.send.at[slot],
            recv_sem=self.recv.at[slot],
            device_id=device_at(moved(self.here, ORDERS[colour][phase], to)),
            device_id_type=MESH,
        )

    def start(self, phase, colours=(0, 1, 2)):
        for colour in colours:
            for which in range(2):
                self.loads(colour, phase, which).start()
        for kind in range(4):
            for colour in colours:
                self.copy(colour, phase, kind).start()

    def forward(self, phase):
        for side in range(2):
            for colour in range(3):
                self.loads(colour, phase, side).wait()
                self.copy(colour, phase, side).wait_recv()
                bufs = self.bufs[colour][phase]
                added(bufs[side], (bufs[2 + side],), bufs[side])
                self.copy(colour, phase, 4 + side).start()
                self.loads(colour, phase, 2 + side).start()

    def advance(self, phase):
        for colour in range(3):
            self.finish(phase, (colour,))
            self.start(phase + 1, (colour,))

    def finish(self, phase, colours=(0, 1, 2)):
        for colour in colours:
            for which in (2, 3):
                self.loads(colour, phase, which).wait()
            for kind in range(2, 6):
                self.copy(colour, phase, kind).wait_recv()
            bufs = self.bufs[colour][phase]
            for side, half in enumerate(self.halves[colour]):
                last = [bufs[4 + i].at[..., half] for i in range(2)]
                out = bufs[2 + side] if phase < 2 else self.results[colour].at[:, half]
                added(bufs[2 + side], last, out)

    def settle(self):
        for phase in range(3):
            for kind in range(6):
                for colour in range(3):
                    self.copy(colour, phase, kind).wait_send()


def added(base, others, out):
    sizes = base.shape[:4]
    _, b, c, d = sizes
    count = sizes[0] * b * c * d
    group = 4 if count % 4 == 0 else 1

    def one(i):
        at = (i // (b * c * d), (i // (c * d)) % b, (i // d) % c, i % d)
        total = base[at].astype(F32)
        for other in others:
            total = total + other[at].astype(F32)
        if len(out.shape) == 2:
            out[...] = total.astype(out.dtype)
        else:
            out[at] = total.astype(out.dtype)

    def step(i, carry):
        for j in range(group):
            one(i * group + j)
        return carry

    lax.fori_loop(0, count // group, step, 0)


class Small:
    def __init__(self, sums, other, slots, send, recv):
        self.sums, self.other, self.slots = sums, other, slots
        self.send, self.recv = send, recv
        self.here = chip()

    def sibling(self, source):
        return pltpu.make_async_remote_copy(
            src_ref=source,
            dst_ref=self.other,
            send_sem=self.send.at[9],
            recv_sem=self.recv.at[9],
            device_id={S: 1 - lax.axis_index(S)},
            device_id_type=MESH,
        )

    def copy(self, phase, by):
        slot = phase * 3 + by - 1
        return pltpu.make_async_remote_copy(
            src_ref=self.sums.at[phase],
            dst_ref=self.slots.at[slot],
            send_sem=self.send.at[slot],
            recv_sem=self.recv.at[slot],
            device_id=device_at(moved(self.here, phase, by)),
            device_id_type=MESH,
        )

    def start(self, phase):
        for by in (1, 2, 3):
            self.copy(phase, by).start()

    def finish(self, phase):
        for by in (1, 2, 3):
            self.copy(phase, by).wait_recv()
        one, two, three = [self.slots[phase * 3 + i] for i in range(3)]
        self.sums[phase + 1] = (self.sums[phase] + two) + (one + three)

    def settle(self):
        for phase in range(3):
            for by in (1, 2, 3):
                self.copy(phase, by).wait_send()


class Bag:
    def __init__(self, **items):
        self.__dict__.update(items)


def launch(body, name, cid, ins, outs, scratch):
    def kernel(*refs):
        body(Bag(**dict(zip([*ins, *outs, *scratch], refs))))

    got = pl.pallas_call(
        kernel,
        name=name,
        out_shape=[jax.ShapeDtypeStruct(shape, dtype) for shape, dtype, _ in outs.values()],
        in_specs=[where for _, where in ins.values()],
        out_specs=[where for _, _, where in outs.values()],
        scratch_shapes=list(scratch.values()),
        compiler_params=pltpu.CompilerParams(
            collective_id=cid, has_side_effects=True, vmem_limit_bytes=60 * MIB
        ),
    )(*[value for value, _ in ins.values()])
    return Bag(**dict(zip(outs, got)))


VM = pl.BlockSpec(memory_space=pltpu.VMEM)


def vm(*shape, dtype=F32):
    return pltpu.VMEM(shape, dtype)


class Moves:
    def __init__(self, local, send, recv):
        self.sems = local, send, recv
        self.kept, self.sent = [], []
        self.locals = self.remotes = 0

    def local(self, src, dst):
        copy = pltpu.make_async_copy(src, dst, self.sems[0].at[self.locals])
        self.locals += 1
        copy.start()
        return copy

    def keep(self, src, dst):
        self.kept.append(self.local(src, dst))

    def remote(self, src, dst, device):
        slot = self.remotes
        self.remotes += 1
        copy = pltpu.make_async_remote_copy(
            src_ref=src,
            dst_ref=dst,
            send_sem=self.sems[1].at[slot],
            recv_sem=self.sems[2].at[slot],
            device_id=device,
            device_id_type=MESH,
        )
        copy.start()
        self.sent.append(copy)
        return copy

    def sibling(self, src, dst):
        return self.remote(src, dst, {S: 1 - lax.axis_index(S)})

    def mates(self, src, dst):
        me = lax.axis_index(SQ)
        copies = [self.remote(src(lax.rem(me + j, 8)), dst, {SQ: lax.rem(me + j, 8)}) for j in range(1, 8)]
        return [self.local(src(me), dst)], copies

    def done(self, copy):
        copy.wait_send()
        self.sent = [c for c in self.sent if c is not copy]

    def flush(self):
        for copy in self.kept:
            copy.wait()
        self.kept = []

    def settle(self):
        self.flush()
        for copy in self.sent:
            copy.wait_send()


def arrived(moves):
    own, copies = moves
    for copy in own:
        copy.wait()
    for copy in copies:
        copy.wait_recv()


def mate_devices():
    me = lax.axis_index(SQ)
    return [{SQ: lax.rem(me + j, 8)} for j in range(1, 8)]


def across_devices():
    here = chip()
    return [device_at(moved(here, axis, by)) for axis in range(2) for by in (1, -1)]


def sibling_device():
    return {S: 1 - lax.axis_index(S)}


def by_rows(rows, step, size=32):
    def body(i, carry):
        step(pl.ds(pl.multiple_of(i * size, size), size))
        return carry

    lax.fori_loop(0, rows // size, body, 0)


def by_columns(width, step, size=256):
    def body(i, carry):
        step(pl.ds(pl.multiple_of(i * size, size), size))
        return carry

    lax.fori_loop(0, width // size, body, 0)


def core_columns(size):
    return pl.ds(pl.multiple_of(lax.axis_index(S) * size, size), size)


def inverse_norm(v):
    return lax.rsqrt(jnp.mean(v * v, axis=-1, keepdims=True) + EPSILON)


def norm_rows(src, gain, dst):
    def step(rows):
        v = src[rows].astype(F32)
        dst[rows] = low(v * inverse_norm(v) * gain[...])

    by_rows(256, step)


def norm_back_rows(src, gain, upstreams, residual, out, d_gain):
    d_gain[...] = jnp.zeros_like(d_gain)

    def step(rows):
        v = src[rows].astype(F32)
        up = sum(u[rows] for u in upstreams)
        r = inverse_norm(v)
        t = up * gain[...]
        dv = r * (t - v * (r * r * jnp.mean(t * v, axis=-1, keepdims=True)))
        out[rows] = (residual[rows].astype(F32) + dv).astype(out.dtype)
        scaled = up * (v * r)
        d_gain[...] += scaled[:8] + scaled[8:16] + scaled[16:24] + scaled[24:]

    by_rows(256, step)


def transpose_into(src, dst):
    def step(cols):
        dst[cols, :] = src[:, cols].astype(F32).T.astype(BF)

    by_columns(1024, step, 128)


def lanes(width=128):
    return lax.broadcasted_iota(jnp.int32, (1, width), 1)


def head_mean(v, ones):
    return jnp.dot(v, ones, precision=lax.Precision.HIGHEST, preferred_element_type=F32)


def qk_gain(b, chunk):
    return b.qk[chunk // 4 : chunk // 4 + 1]


def half_turn(v):
    return jnp.where(lanes() % 64 < 32, pltpu.roll(v, 96, 1), pltpu.roll(v, 32, 1))


def head_lanes(v, head, upper):
    v = v.astype(F32)
    if head != upper:
        v = pltpu.roll(v, 64, 1)
    return jnp.where(lanes() >= 64 if upper else lanes() < 64, v, 0.0)


def block_probs(b, block, head):
    count = 256 * (block + 1)
    q = head_lanes(b.packed[2 * block : 2 * block + 2, :, :128].reshape(256, 128), head, 0)
    kv = b.packed[: 2 * block + 2, :, 128:].reshape(count, 128)
    scores = times_transposed(low(q), kv) * 0.125
    row = lax.broadcasted_iota(jnp.int32, (256, count), 0) + 256 * block
    col = lax.broadcasted_iota(jnp.int32, (256, count), 1)
    e = jnp.exp(jnp.where(row >= col, scores, -1e9))
    return q, kv, e * (1.0 / jnp.sum(e, -1, keepdims=True))


def flat(value):
    return value.reshape(-1, value.shape[-1])


def ring_shape(width):
    return (4, 2, 4, 2, 16, width)


def fill_perm(perm):
    def step(cols):
        p = lax.broadcasted_iota(jnp.int32, (1024, 256), 1) + cols.start
        row = lax.broadcasted_iota(jnp.int32, (1024, 256), 0)
        natural = (p & 8) * 64 + (p >> 4) * 8 + (p & 7)
        perm[:, cols] = jnp.where(row == natural, 1.0, 0.0).astype(BF)

    by_columns(1024, step)


def fill_ones(ones):
    row = lax.broadcasted_iota(jnp.int32, (128, 128), 0)
    col = lax.broadcasted_iota(jnp.int32, (128, 128), 1)
    ones[...] = jnp.where(row // 64 == col // 64, 1.0 / 64.0, 0.0)


def forward_kernel(b):
    core, seq = lax.axis_index(S), lax.axis_index(SQ)
    greet(across_devices() + mate_devices() + [sibling_device()])
    moves = Moves(b.local, b.send, b.recv)
    here = spot(chip())
    half, other_half = core_columns(512), pl.ds(pl.multiple_of(512 - core * 512, 512), 512)

    mine = pl.ds(pl.multiple_of(core * 8, 8), 8)
    waits = [
        moves.local(b.mix_in.at[core], b.mix.at[mine]),
        moves.local(b.gains_in, b.gains.at[core]),
        moves.local(b.taps_in, b.mt.at[here + (slice(None), pl.ds(512, 128))]),
    ]
    swaps = [
        moves.sibling(b.mix_in.at[1 - core], b.mix.at[mine]),
        moves.sibling(b.gains_in, b.gains.at[core]),
    ]
    shards = (
        (b.gate_in, 2304, (b.gate0, b.gate1)),
        (b.up_in, 2304, (b.up0, b.up1)),
        (b.down_in, 2304, (b.down0, b.down1)),
        (b.mo, 512, (b.mt, b.mo1)),
    )

    def trade(k, block):
        w, n, homes = shards[k]
        home = homes[block].at[here + (slice(None), pl.ds(0, n))]
        keep = pltpu.make_async_copy(w.at[:, pl.ds(block * n, n)], home, b.trade.at[k])
        give = pltpu.make_async_remote_copy(
            src_ref=w.at[:, pl.ds((1 - block) * n, n)],
            dst_ref=home,
            send_sem=b.trade.at[4 + k],
            recv_sem=b.trade.at[8 + k],
            device_id=sibling_device(),
            device_id_type=MESH,
        )
        return keep, give

    for block in range(2):

        @pl.when(core == block)
        def _():
            for k in (3, 0, 1, 2):
                for copy in trade(k, block):
                    copy.start()

    for copy in waits:
        copy.wait()
    for copy in swaps:
        copy.wait_recv()
    b.ci0[here] = low(b.mix[:, :768])
    b.ci1[here] = low(b.mix[:, 768:1536])
    b.qw0[here] = low(b.mix[:, 1536:2048])
    b.qw1[here] = low(b.mix[:, 2048:])
    for k in (3, 0, 1, 2):
        keep, give = trade(k, 0)
        keep.wait()
        give.wait_recv()
    moves.keep(b.gains, b.gains_out)

    rings = [
        Gather(bufs, b.gsend.at[i], b.grecv.at[i])
        for i, bufs in enumerate(
            (
                (b.ci0, b.ci1, b.mt),
                (b.gate0, b.up0, b.down0),
                (b.qw0, b.qw1, b.mo1),
                (b.gate1, b.up1, b.down1),
            )
        )
    ]
    ring_a, ring_b, ring_c, ring_d = rings
    firsts = [
        Gather([w.at[..., cols] for w in (b.gate0, b.up0, b.down0)], b.gsend.at[j], b.grecv.at[j], turn)
        for cols, j, turn in ((pl.ds(0, 1280), 1, 0), (pl.ds(1280, 1024), 4, 2))
    ]
    lasts = [
        Gather([w.at[..., pl.ds(768 * i, 768)] for w in (b.gate1, b.up1, b.down1)], b.gsend.at[j], b.grecv.at[j], turn)
        for i, (j, turn) in enumerate(((3, 0), (4, 0), (4, 1)))
    ]
    for ring in rings:
        ring.start(0)
    norm_rows(b.x, b.gains.at[0, 0:1], b.normed)
    fill_perm(b.perm)
    fill_ones(b.ones)
    permuted(b.normed, b.perm, b.turned)
    for ring in rings:
        ring.forward(0)
    ring_a.finish(0)
    ring_a.start(1)
    ring_b.finish(0)
    ring_b.start(1)
    ring_a.forward(1)
    ring_a.finish(1)
    ring_a.start(2)
    ring_b.forward(1)
    ring_c.finish(0)
    ring_c.start(1)
    ring_a.forward(2)
    ring_b.finish(1)
    for ring in firsts:
        ring.start(2)
    ring_a.finish(2)

    def other_mo(source, target):
        return moves.sibling(source.at[..., pl.ds(0, 512)], target)

    mo0_swap = other_mo(b.mt, b.mo0_other)
    ring_d.finish(0)
    for x in range(4):
        rows = flat(b.mt[x, :, :, :, :, 512:]).reshape(16, 16, 128)
        b.taps[:, x * 128 : x * 128 + 128] = jnp.sum(rows.astype(F32), 0)[:8]
    for i, ci in enumerate((b.ci0, b.ci1)):
        for j in range(3):
            cols = slice(j * 256, j * 256 + 256)
            b.p1[:, i * 768 + j * 256 : i * 768 + j * 256 + 256] = matmul(b.turned[...], flat(ci[..., cols]))
    moves.keep(b.p1, b.p1_out)
    ring_c.forward(1)

    def gated(rows):
        b.bx[rows] = low(b.p1[rows, :512] * b.p1[rows, 1024:]).astype(F32)

    by_rows(256, gated)
    for m in range(2):
        b.pad[m, 8:] = b.bx[m * 128 : m * 128 + 128]
    rim = moves.remote(b.pad.at[:, pl.ds(128, 8)], b.rim, {SQ: lax.rem(seq + 1, 8)})
    for ring in firsts:
        ring.forward(2)
    rim.wait_recv()
    b.pad[:, :8] = jnp.where(seq > 0, b.rim[...], 0.0)
    moves.keep(b.pad, b.pad_out)

    def convolve(cols):
        taps = b.taps[:, cols]
        for m in range(2):
            conv = sum(taps[j : j + 1] * b.pad[m, 6 + j : 134 + j, cols] for j in range(3))
            rows = slice(m * 128, m * 128 + 128)
            gate = b.p1[rows, pl.ds(pl.multiple_of(cols.start + 512, 128), 128)]
            b.m1[rows, pl.ds(pl.multiple_of(core * 512 + cols.start, 128), 128)] = low(gate * conv)

    by_columns(512, convolve, 128)
    swap = moves.sibling(b.m1.at[:, half], b.m1.at[:, half])
    swap.wait_recv()
    moves.keep(b.m1, b.m1_out)
    moves.keep(b.taps, b.taps_out)
    mo0_swap.wait_recv()
    b.h1[:, half] = b.x[:, half].astype(F32) + matmul(b.m1[...], flat(b.mt[..., :512]))
    b.h1[:, other_half] = b.x[:, other_half].astype(F32) + matmul(b.m1[...], flat(b.mo0_other[...]))
    moves.keep(b.h1, b.h1_out)
    norm_rows(b.h1, b.gains.at[0, 1:2], b.normed)
    ring_c.finish(1)
    ring_c.start(2)
    ring_d.start(1)

    def hidden(cols):
        g = matmul(b.normed[...], flat(b.gate0[..., cols]))
        u = matmul(b.normed[...], flat(b.up0[..., cols]))
        b.active[:, cols] = low(g / (1.0 + jnp.exp(-g)) * u)

    firsts[0].finish(2)
    by_columns(1280, hidden)

    def contract_first(x, carry):
        cols = pl.ds(pl.multiple_of(x * 256, 256), 256)
        b.f[:, cols] = times_transposed(b.active[:, :1280], flat(b.down0[x, :, :, :, :, :1280]))
        return carry

    lax.fori_loop(0, 4, contract_first, 0)
    firsts[1].finish(2)
    by_columns(1024, lambda cols: hidden(pl.ds(pl.multiple_of(cols.start + 1280, 256), 256)))
    ring_d.forward(1)
    ring_c.forward(2)

    def contract(cols):
        down = flat(b.down0[cols.start // 256, :, :, :, :, 1280:])
        b.f[:, cols] += times_transposed(b.active[:, 1280:], down)

    swaps = swapped_columns(moves, contract, b.f, b.f_other)
    for swap in swaps:
        swap.wait_recv()

    def passed(rows):
        b.z[rows] = low(b.h1[rows] + (b.f[rows] + b.f_other[rows]))

    by_rows(256, passed)
    for swap in swaps:
        moves.done(swap)
    moves.keep(b.z, b.z_out)

    ring_d.finish(1)
    lasts[0].start(2)
    norm_rows(b.z, b.gains.at[1, 0:1], b.normed)
    permuted(b.normed, b.perm, b.turned)
    ring_c.finish(2)
    mo1_swap = other_mo(b.mo1, b.mo1_other)
    for i, qw in enumerate((b.qw0, b.qw1)):
        for j in range(2):
            cols = slice(j * 256, j * 256 + 256)
            b.p2[:, i * 512 + j * 256 : i * 512 + j * 256 + 256] = matmul(b.turned[...], flat(qw[..., cols]))
    moves.keep(b.p2, b.p2_out)
    for chunk in range(8):
        cols = slice(chunk * 128, chunk * 128 + 128)
        head, place = chunk % 4, pl.ds(chunk // 4 * 128, 128)
        for m in range(2):
            v = b.p2[m * 128 : m * 128 + 128, cols]
            y = v * lax.rsqrt(head_mean(v * v, b.ones[...]) + EPSILON) * qk_gain(b, chunk)
            y = y * b.cosine[...] + half_turn(y) * b.sine[...]
            if chunk >= 4:
                y = jnp.where(lanes() < 64, y, v)
            b.out[m * 4 + head, :, place] = low(y)
    exchange = moves.mates(lambda j: b.out.at[j], b.packed.at[seq])
    lasts[0].forward(2)
    lasts[1].start(2, ((0, 2),))
    for ring_out, ref in (
        (b.ci0_out, b.ci0), (b.ci1_out, b.ci1), (b.gate0_out, b.gate0), (b.up0_out, b.up0),
        (b.down0_out, b.down0), (b.qw0_out, b.qw0), (b.qw1_out, b.qw1),
    ):
        moves.keep(ref, ring_out)
    transpose_into(b.cot, b.cot_t)
    arrived(exchange)
    moves.keep(b.packed, b.packed_out)
    for block in range(4):
        results = []
        for head in range(2):
            _, kv, probs = block_probs(b, block, head)
            results.append(matmul(low(probs), kv))
        joint = jnp.where(lanes() < 64, pltpu.roll(results[0], 64, 1), results[1])
        b.att_rows[2 * block : 2 * block + 2] = low(joint).reshape(2, 128, 128)
    rows = pl.ds(pl.multiple_of(seq // 4 * 128, 128), 128)
    cols = pl.ds(pl.multiple_of(core * 512 + seq % 4 * 128, 128), 128)
    exchange = moves.mates(lambda j: b.att_rows.at[j], b.att.at[rows, cols])
    lasts[1].start(2, ((1, 3),))
    lasts[1].forward(2)
    lasts[2].start(2)
    mo1_swap.wait_recv()
    for out, own, other in ((b.mo0_out, b.mt, b.mo0_other), (b.mo1_out, b.mo1, b.mo1_other)):
        moves.keep(own.at[..., pl.ds(0, 512)], out.at[..., half])
        moves.keep(other, out.at[..., other_half])
    arrived(exchange)
    swap = moves.sibling(b.att.at[:, half], b.att.at[:, half])
    swap.wait_recv()
    moves.keep(b.att, b.att_out)
    b.h2[:, half] = b.z[:, half].astype(F32) + matmul(b.att[...], flat(b.mo1[...]))
    b.h2[:, other_half] = b.z[:, other_half].astype(F32) + matmul(b.att[...], flat(b.mo1_other[...]))

    norm_rows(b.h2, b.gains.at[1, 1:2], b.normed)
    transpose_into(b.normed, b.normed_t)

    def tick3():
        lasts[2].forward(2)
        lasts[1].finish(2)

    ffn_loop(
        b, [flat_ref(w) for w in (b.gate1, b.up1, b.down1)], (b.gate_grad, b.up_grad, b.down_grad),
        b.normed, b.normed_t, b.cot, b.cot_t, b.f, b.f1,
        {0: functools.partial(lasts[0].finish, 2), 3: tick3, 6: functools.partial(lasts[2].finish, 2)}, True,
    )
    da_swap = moves.sibling(b.f, b.da_other)
    f_swap = moves.sibling(b.f1.at[:, other_half], b.f1_other)
    da_swap.wait_recv()
    norm_back_rows(b.h2, b.gains.at[1, 1:2], (b.f, b.da_other), b.cot, b.dh2, b.d_ffn)
    f_swap.wait_recv()

    def finish(rows):
        b.result[rows] = low(b.h2[rows, half] + (b.f1[rows, half] + b.f1_other[rows]))

    by_rows(256, finish)
    ring_a.settle()
    ring_c.settle()
    ring_b.settle(range(2))
    ring_d.settle(range(2))
    for ring in firsts + lasts:
        ring.settle(range(2, 3))
    for k in range(4):
        trade(k, 0)[1].wait_send()
    moves.settle()


def flat_ref(ref):
    return ref.reshape(1024, ref.shape[-1])


def swapped_columns(moves, step, ref, target):
    swaps = []
    for i in range(4):
        cols = pl.ds(256 * i, 256)
        step(cols)
        swaps.append(moves.sibling(ref.at[:, cols], target.at[:, cols]))
    return swaps


def permuted(src, perm, dst):
    def step(cols):
        dst[:, cols] = low(matmul(src[...], perm[:, cols]))

    by_columns(1024, step)


def dma(*count):
    return pltpu.SemaphoreType.DMA(count)


def bf(*shape):
    return pltpu.VMEM(shape, BF)


def forward(x, cot, gains_in, qk, cosine, sine, taps, mix_in, weights):
    def saved(*shape, dtype=BF):
        return (shape, dtype, ANY)

    wide, thin = ring_shape(2304), ring_shape(512)
    wg, wu, wd, mo = weights
    return launch(
        forward_kernel,
        "forward",
        1,
        dict(
            x=(x, VM), cot=(cot, VM), gains_in=(gains_in, VM), qk=(qk, VM), cosine=(cosine, VM), sine=(sine, VM),
            taps_in=(taps, VM), mix_in=(mix_in, VM),
            gate_in=(wg, ANY), up_in=(wu, ANY), down_in=(wd, ANY), mo=(mo, ANY),
        ),
        dict(
            gate1=saved(*wide), up1=saved(*wide), down1=saved(*wide), ci0_out=saved(*ring_shape(768)),
            ci1_out=saved(*ring_shape(768)), gate0_out=saved(*wide), up0_out=saved(*wide),
            down0_out=saved(*wide), qw0_out=saved(*thin), qw1_out=saved(*thin),
            mo0_out=saved(*ring_shape(1024)), mo1_out=saved(*ring_shape(1024)),
            gains_out=saved(2, 8, 1024, dtype=F32), taps_out=saved(8, 512, dtype=F32),
            p1_out=saved(256, 1536, dtype=F32), pad_out=saved(2, 136, 512, dtype=F32),
            m1_out=saved(256, 1024), h1_out=saved(256, 1024, dtype=F32), z_out=saved(256, 1024),
            p2_out=saved(256, 1024, dtype=F32), packed_out=saved(8, 128, 256),
            att_out=saved(256, 1024), gate_grad=saved(1024, 2304), up_grad=saved(1024, 2304), down_grad=saved(1024, 2304),
            dh2=((256, 1024), F32, VM), d_ffn=((8, 1024), F32, VM), result=((256, 512), BF, VM),
        ),
        dict(
            mix=vm(16, 2560), gains=vm(2, 8, 1024), taps=vm(8, 512), perm=bf(1024, 1024),
            ci0=bf(*ring_shape(768)), ci1=bf(*ring_shape(768)), mt=bf(*ring_shape(640)),
            gate0=bf(*wide), up0=bf(*wide), down0=bf(*wide), qw0=bf(*thin), qw1=bf(*thin), mo1=bf(*thin),
            mo0_other=bf(*thin), mo1_other=bf(*thin),
            normed=bf(256, 1024), turned=bf(256, 1024), p1=vm(256, 1536), bx=vm(256, 512), pad=vm(2, 136, 512),
            rim=vm(2, 8, 512), m1=bf(256, 1024), h1=vm(256, 1024), active=bf(256, 2304),
            f=vm(256, 1024), f_other=vm(256, 1024), z=bf(256, 1024), p2=vm(256, 1024),
            out=bf(8, 128, 256), packed=bf(8, 128, 256), att_rows=bf(8, 128, 128), att=bf(256, 1024),
            h2=vm(256, 1024), ones=vm(128, 128), normed_t=bf(1024, 256), cot_t=bf(1024, 256), f1=vm(256, 1024),
            f1_other=vm(256, 512), da_other=vm(256, 1024), local=dma(40), send=dma(32), recv=dma(32), trade=dma(12),
            gsend=dma(5, 54), grecv=dma(5, 54), **ffn_scratch(),
        ),
    )


def ffn_scratch():
    return dict(
        wg=bf(2, 1024, 256), wu=bf(2, 1024, 256), wd=bf(2, 1024, 256),
        sg=bf(2, 1024, 256), su=bf(2, 1024, 256), sd=bf(2, 1024, 256),
        load=pltpu.SemaphoreType.DMA((2, 3)), store=pltpu.SemaphoreType.DMA((2, 3)),
    )


def ffn_loop(b, weights, grads, normed, normed_t, df, df_t, da, f=None, ticks=None, gated=False, stored=()):
    ticks = ticks or {}
    bounds = sorted({0, 9, *ticks})

    def columns(i):
        return pl.ds(pl.multiple_of(i * 256, 256), 256)

    def loads(i, slot):
        return [
            pltpu.make_async_copy(w.at[:, columns(i)], d.at[slot], b.load.at[slot, k])
            for k, (w, d) in enumerate(zip(weights, (b.wg, b.wu, b.wd)))
        ]

    def stores(i, slot):
        return [
            pltpu.make_async_copy(s.at[slot], g.at[:, columns(i)], b.store.at[slot, k])
            for k, (g, s) in enumerate(zip(grads, (b.sg, b.su, b.sd)))
        ]

    da[...] = jnp.zeros_like(da)
    if f is not None:
        f[...] = jnp.zeros_like(f)

    def last_stored(begin):
        return max((s for s in stored if s <= begin), default=0)

    def step(begin, end, i, carry):
        slot = lax.rem(i, 2)
        for copy in loads(i, slot):
            copy.wait()

        @pl.when(i + 1 < end)
        def _():
            for copy in loads(i + 1, 1 - slot):
                copy.start()

        gate, up, down = b.wg.at[slot], b.wu.at[slot], b.wd.at[slot]
        g = matmul(normed[...], gate[...])
        u = matmul(normed[...], up[...])
        ds = matmul(df[...], down[...])
        sig = 1.0 / (1.0 + jnp.exp(-g))
        silu = g * sig
        s = low(silu * u)
        dg = low(ds * u * (sig * (1.0 + g * (1.0 - sig))))
        du = low(ds * silu)
        if f is not None:
            f[...] += times_transposed(s, down[...])
        da[...] += times_transposed(dg, gate[...]) + times_transposed(du, up[...])

        @pl.when(i >= last_stored(begin) + 2)
        def _():
            for copy in stores(i - 2, slot):
                copy.wait()

        b.sg[slot] = low(matmul(normed_t[...], dg))
        b.su[slot] = low(matmul(normed_t[...], du))
        b.sd[slot] = low(matmul(df_t[...], s))
        for copy in stores(i, slot):
            copy.start()
        return carry

    for start, end in zip(bounds, bounds[1:]):
        if start in stored:
            for copy in stores(start - 2, start % 2) + stores(start - 1, 1 - start % 2):
                copy.wait()
        if start in ticks:
            ticks[start]()
        if gated or start == 0:
            for copy in loads(start, start % 2):
                copy.start()
        lax.fori_loop(start, end, functools.partial(step, start, end if gated else 9), 0)
    for copy in stores(7, 1) + stores(8, 0):
        copy.wait()


def staged(moves, left_t, right, slots, dests):
    for k, (slot, dest) in enumerate(zip(slots, dests)):
        slot[...] = low(matmul(left_t[...], right(k)))
        moves.keep(slot, dest)


def slots(*stacks):
    return [stack.at[i] for stack in stacks for i in range(2)]


def places(grad, count):
    return [grad.at[:, pl.ds(256 * k, 256)] for k in range(count)]


def unpermuted(b, mine, theirs, out):
    def step(cols):
        total = mine[:, cols] + theirs[:, cols]
        high = low(total)
        b.high[:, cols] = high
        b.rest[:, cols] = low(total - high.astype(F32))

    by_columns(1024, step)

    def turn(cols):
        out[:, cols] = times_transposed(b.high[...], b.perm[cols, :]) + times_transposed(b.rest[...], b.perm[cols, :])

    by_columns(1024, turn)


def backward_kernel(b):
    core, seq = lax.axis_index(S), lax.axis_index(SQ)
    greet(across_devices() + mate_devices() + [sibling_device()])
    moves = Moves(b.local, b.send, b.recv)
    r0, r1, r2, r3 = ffn_rings(b, (b.rg, b.ru, b.rd), (b.sum_g, b.sum_u, b.sum_d))
    r0.start(0)
    mo1_load = moves.local(b.mo1_in, b.mo)
    packed_load = moves.local(b.packed_in, b.packed)
    attn_loads = [
        moves.local(w, b.proj.at[:, pl.ds(i * 512, 512)]) for i, w in enumerate((b.qw0, b.qw1))
    ]
    p2_load = moves.local(b.p2_in, b.p2)
    fill_perm(b.perm)
    fill_ones(b.ones)

    def rounded(rows):
        b.do[rows] = low(b.dh2[rows])

    by_rows(256, rounded)
    mo1_load.wait()
    for h in range(4):
        rows = pl.ds(pl.multiple_of(core * 512 + h * 128, 128), 128)
        d_att = low(times_transposed(b.do[...], b.mo[rows, :]))
        for m in range(2):
            b.out_att[m * 4 + h] = d_att[m * 128 : m * 128 + 128]
    exchange = moves.mates(lambda j: b.out_att.at[j], b.d_att.at[seq])
    r1.start(0)
    r2.start(0)
    transpose_into(b.att, b.turned)
    staged(moves, b.turned, lambda k: own_columns(b.do, k), slots(b.sg), places(b.mo1_grad, 2))
    packed_load.wait()
    norm_rows(b.z, b.gains.at[1, 0:1], b.normed)
    permuted(b.normed, b.perm, b.high)
    transpose_into(b.high, b.normed_t)
    arrived(exchange)
    r3.start(0)
    b.dkv[...] = jnp.zeros_like(b.dkv)
    for block in range(4):
        count = 256 * (block + 1)
        results = []
        for head in range(2):
            q, kv, probs = block_probs(b, block, head)
            up = low(head_lanes(b.d_att[2 * block : 2 * block + 2].reshape(256, 128), head, 1))
            dp = times_transposed(up, kv)
            ds = low(probs * (dp - jnp.sum(dp * probs, -1, keepdims=True)))
            b.dkv[:count] += transposed_times(ds, low(q * 0.125)) + transposed_times(low(probs), up)
            results.append(matmul(ds, kv) * 0.125)
        joint = jnp.where(lanes() < 64, results[0], pltpu.roll(results[1], 64, 1))
        b.out[2 * block : 2 * block + 2, :, :128] = low(joint).reshape(2, 128, 128)
    for j in range(8):
        b.out[j, :, 128:] = low(b.dkv[j * 128 : j * 128 + 128])
    exchange = moves.mates(lambda j: b.out.at[j], b.d_packed.at[seq])
    rings = (r0, r1, r2, r3)
    for each in rings:
        each.forward(0)
    p2_load.wait()
    arrived(exchange)
    b.d_qk[...] = jnp.zeros_like(b.d_qk)
    for chunk in range(8):
        cols = slice(chunk * 128, chunk * 128 + 128)
        head, place = chunk % 4, slice(chunk // 4 * 128, chunk // 4 * 128 + 128)
        for m in range(2):
            v = b.p2[m * 128 : m * 128 + 128, cols]
            up = b.d_packed[m * 4 + head, :, place].astype(F32)
            r = lax.rsqrt(head_mean(v * v, b.ones[...]) + EPSILON)
            dy = up * b.cosine[...] + half_turn(up * b.sine[...])
            t = dy * qk_gain(b, chunk)
            dv = r * (t - v * (r * r * head_mean(t * v, b.ones[...])))
            b.d_qk[chunk // 4 : chunk // 4 + 1] += jnp.sum(dy * (v * r), 0, keepdims=True)
            if chunk >= 4:
                dv = jnp.where(lanes() < 64, dv, up)
            b.dp2[m * 128 : m * 128 + 128, cols] = low(dv)
    for copy in attn_loads:
        copy.wait()

    def back2(cols):
        b.partial[:, cols] = times_transposed(b.dp2[...], b.proj[cols, :])

    for each in rings:
        each.advance(0)
    swaps = swapped_columns(moves, back2, b.partial, b.other)
    staged(
        moves,
        b.normed_t,
        lambda k: b.dp2[:, k * 256 : k * 256 + 256],
        slots(b.su, b.sd),
        places(b.qw0_grad, 2) + places(b.qw1_grad, 2),
    )
    for each in rings:
        each.forward(1)
    for swap in swaps:
        swap.wait_recv()
        moves.done(swap)
    unpermuted(b, b.partial, b.other, b.partial)
    for each in rings:
        each.advance(1)
    norm_back_rows(b.z, b.gains.at[1, 0:1], (b.partial,), b.dh2, b.dz, b.d_mix1)
    for each in rings:
        each.forward(2)
    for each in rings:
        each.finish(2)
        each.settle()
    moves.settle()


def ffn_rings(b, grads, sums):
    widths = [bufs[-1].shape[-1] for bufs in b.rings]
    cols = [pl.ds(sum(widths[:i]), w) for i, w in enumerate(widths)]
    grads = [g.reshape(ring_shape(2304)) for g in grads]
    return [
        Scatter(
            [g.at[..., cols[i]] for g in grads], bufs, [s.at[:, cols[i]] for s in sums],
            b.ssend.at[i], b.srecv.at[i], b.sload.at[i],
        )
        for i, bufs in enumerate(b.rings)
    ]


def last_kernel(b):
    core, seq = lax.axis_index(S), lax.axis_index(SQ)
    here = chip()
    greet(
        [device_at(moved(here, axis, by)) for axis in range(3) for by in (1, 2, 3)]
        + [sibling_device(), {SQ: lax.rem(seq + 1, 8)}, {SQ: lax.rem(seq + 7, 8)}]
    )
    moves = Moves(b.local, b.send, b.recv)

    def mixer_rings(i, grads, bufs, sums):
        parts = [g.reshape(ring_shape(g.shape[-1])) for g in grads]
        return Scatter(parts, bufs, sums, b.ssend.at[i], b.srecv.at[i], b.sload.at[i])

    r0, r1, r2 = ffn_rings(b, (b.gate_grad, b.up_grad, b.down_grad), (b.sum_g, b.sum_u, b.sum_d))
    ring2 = mixer_rings(3, (b.qw0_grad, b.qw1_grad, b.mo1_grad), b.ring2, (b.sum_q0, b.sum_q1, b.sum_mo1))
    ring3 = mixer_rings(4, (b.ci0_grad, b.ci1_grad, b.mt_grad), b.ring3, (b.sum_c0, b.sum_c1, b.sum_mt))
    ring2.start(0)
    norm_rows(b.h1, b.gains.at[0, 1:2], b.normed)
    transpose_into(b.normed, b.normed_t)
    transpose_into(b.dz_in, b.turned)
    mo0_load = moves.local(b.mo0_in, b.mo)
    p1_load = moves.local(b.p1_in, b.p1)
    ci_loads = [moves.local(w, b.proj.at[:, pl.ds(i * 768, 768)]) for i, w in enumerate((b.ci0, b.ci1))]
    fill_perm(b.perm)

    def tick2():
        ring2.forward(0)

    def tick3():
        r0.start(0)

    def tick5():
        ring2.advance(0)

    def tick6():
        r1.start(0)
        r0.forward(0)

    def tick8():
        ring2.forward(1)

    ticks = {2: tick2, 3: tick3, 5: tick5, 6: tick6, 8: tick8}
    ffn_loop(
        b, (b.gate0, b.up0, b.down0), (b.gate_grad, b.up_grad, b.down_grad),
        b.normed, b.normed_t, b.dz_in, b.turned, b.partial, None, ticks, False, (3, 6),
    )
    swap = moves.sibling(b.partial, b.other0)
    ring2.advance(1)
    swap.wait_recv()
    moves.done(swap)
    r2.start(0)
    norm_back_rows(b.h1, b.gains.at[0, 1:2], (b.partial, b.other0), b.dz_in, b.dh1, b.d_ffn0)

    def rounded0(rows):
        b.do[rows] = low(b.dh1[rows])

    by_rows(256, rounded0)
    mo0_load.wait()
    p1_load.wait()

    def mixed(i, carry):
        rows = pl.ds(pl.multiple_of(core * 512 + i * 128, 128), 128)
        cols = pl.ds(pl.multiple_of(i * 128, 128), 128)
        middle_cols = pl.ds(pl.multiple_of(512 + i * 128, 128), 128)
        dm = times_transposed(b.do[...], b.mo[rows, :])
        taps = b.taps[:, cols]
        for m in range(2):
            part = slice(m * 128, m * 128 + 128)
            conv = sum(taps[j : j + 1] * b.pad[m, 6 + j : 134 + j, cols] for j in range(3))
            b.dp1[part, middle_cols] = low(dm[part] * conv)
            b.dconv[m, :128, cols] = dm[part] * b.p1[part, middle_cols]
        return carry

    lax.fori_loop(0, 4, mixed, 0)
    rim = moves.remote(b.dconv.at[:, pl.ds(0, 8)], b.rim, {SQ: lax.rem(seq + 7, 8)})
    r1.forward(0)
    r0.advance(0)
    transpose_into(b.m1, b.turned)
    staged(moves, b.turned, lambda k: own_columns(b.do, k), slots(b.sg), places(b.mt_grad, 2))
    ring2.forward(2)
    norm_rows(b.x, b.gains.at[0, 0:1], b.normed)
    permuted(b.normed, b.perm, b.high)
    transpose_into(b.high, b.normed_t)
    rim.wait_recv()
    b.dconv[:, 128:] = jnp.where(seq < 7, b.rim[...], 0.0)
    b.d_taps[...] = jnp.zeros_like(b.d_taps)

    def conv_back(i, carry):
        cols = pl.ds(pl.multiple_of(i * 128, 128), 128)
        last_cols = pl.ds(pl.multiple_of(1024 + i * 128, 128), 128)
        taps = b.taps[:, cols]
        for m in range(2):
            part = slice(m * 128, m * 128 + 128)
            dconv = b.dconv[m, :128, cols]
            for j in range(3):
                b.d_taps[j : j + 1, cols] += jnp.sum(dconv * b.pad[m, 6 + j : 134 + j, cols], 0, keepdims=True)
            dbx = sum(taps[2 - j : 3 - j] * b.dconv[m, j : 128 + j, cols] for j in range(3))
            b.dp1[part, cols] = low(dbx * b.p1[part, last_cols])
            b.dp1[part, last_cols] = low(dbx * b.p1[part, cols])
        return carry

    lax.fori_loop(0, 4, conv_back, 0)
    r2.forward(0)
    for x in range(4):
        tile = low(b.d_taps[:, x * 128 : x * 128 + 128])
        tile = jnp.broadcast_to(jnp.concatenate([tile, tile], 0), (16, 16, 128))
        b.wu[0, x * 256 : x * 256 + 256, :128] = tile.reshape(256, 128)
    moves.keep(b.wu.at[0, :, pl.ds(0, 128)], b.mt_grad.at[:, pl.ds(512, 128)])
    staged(
        moves,
        b.normed_t,
        lambda k: b.dp1[:, k * 256 : k * 256 + 256],
        slots(b.su, b.sd, b.wg),
        places(b.ci0_grad, 3) + places(b.ci1_grad, 3),
    )
    moves.flush()
    ring3.start(0)
    r1.advance(0)
    r0.forward(1)
    ring2.finish(2)
    for copy in ci_loads:
        copy.wait()

    def back1(cols):
        b.partial[:, cols] = times_transposed(b.dp1[...], b.proj[cols, :])

    swaps = swapped_columns(moves, back1, b.partial, b.other)
    r2.advance(0)
    r0.advance(1)
    r1.forward(1)
    for swap in swaps:
        swap.wait_recv()
        moves.done(swap)
    ring3.forward(0)
    unpermuted(b, b.partial, b.other, b.partial)
    r2.forward(1)
    r1.advance(1)
    r0.forward(2)
    norm_back_rows(b.x, b.gains.at[0, 0:1], (b.partial,), b.dh1, b.do, b.d_mix0)

    ring3.advance(0)
    moves.keep(b.do.at[:, core_columns(512)], b.dx_out)

    first = core == 0
    small = Small(b.sums, b.qk_other, b.arrivals, b.small_send, b.small_recv)
    b.sums[0] = jnp.zeros((8, 1024), F32)
    b.sums[0, 0:1] = jnp.sum(jnp.where(first, b.d_mix0[...], b.d_mix1[...]), 0, keepdims=True)
    b.sums[0, 1:2] = jnp.sum(jnp.where(first, b.d_ffn0[...], b.d_ffn1[...]), 0, keepdims=True)
    small.sibling(b.d_qk).start()
    small.sibling(b.d_qk).wait_recv()
    b.sums[0, 2:4, :128] = b.d_qk[0:2] + b.qk_other[0:2]
    small.start(0)
    r2.advance(1)
    r1.forward(2)
    ring3.forward(1)
    r0.finish(2)
    small.finish(0)
    small.start(1)
    ring3.advance(1)
    r2.forward(2)
    r1.finish(2)
    small.finish(1)
    small.start(2)
    ring3.forward(2)
    r2.finish(2)
    small.finish(2)
    b.small[...] = b.sums[3]
    ring3.finish(2)

    mine = (pl.ds(pl.multiple_of(core * 8, 8), 8), pl.ds(pl.multiple_of(8 - core * 8, 8), 8))
    column = 0
    for ref in (b.sum_c0, b.sum_c1, b.sum_q0, b.sum_q1):
        width = ref.shape[1]
        home = b.mix_out.at[core, :, pl.ds(column, width)]
        moves.keep(ref.at[mine[0]], home)
        moves.sibling(ref.at[mine[1]], home)
        column += width
    pairs = (
        (1024, 2304, (b.sum_g, b.sum_g1)),
        (5632, 2304, (b.sum_u, b.sum_u1)),
        (10240, 2304, (b.sum_d, b.sum_d1)),
        (0, 512, (b.sum_mt, b.sum_mo1)),
    )

    def trade(k, block):
        first, n, sources = pairs[k]
        home = b.block_out.at[:, pl.ds(first + block * n, n)]
        keep = pltpu.make_async_copy(sources[block].at[:, pl.ds(0, n)], home, b.trade.at[k])
        give = pltpu.make_async_remote_copy(
            src_ref=sources[1 - block].at[:, pl.ds(0, n)],
            dst_ref=home,
            send_sem=b.trade.at[4 + k],
            recv_sem=b.trade.at[8 + k],
            device_id=sibling_device(),
            device_id_type=MESH,
        )
        return keep, give

    for block in range(2):

        @pl.when(core == block)
        def _():
            for k in range(4):
                for copy in trade(k, block):
                    copy.start()

    for k in range(4):
        keep, give = trade(k, 0)
        keep.wait()
        give.wait()
    for each in (r0, r1, r2, ring2, ring3):
        each.settle()
    small.settle()
    small.sibling(b.d_qk).wait_send()
    for copy in moves.sent[-4:]:
        copy.wait_recv()
    moves.settle()


def own_columns(ref, k):
    return ref[:, pl.ds(pl.multiple_of(lax.axis_index(S) * 512 + k * 256, 256), 256)]


def ring_scratch(first, widths):
    return {first + str(i): s for i, s in enumerate(scatter_scratch(widths))}


def ring_names(*widths):
    return [ring_scratch(chr(97 + i), w) for i, w in enumerate(widths)]


def sums(width, where=None):
    return vm(16, width) if where is None else ((16, width), F32, where)


def backward(qk, cosine, sine, w):
    thin, partial_gain = ((1024, 512), BF, ANY), ((8, 1024), F32, VM)
    rings = ring_names((640,) * 3, (640,) * 3, (512,) * 3, (512,) * 3)

    def body(b):
        b.rings = [[getattr(b, name) for name in ring] for ring in rings]
        backward_kernel(b)

    return launch(
        body,
        "backward",
        3,
        dict(
            gains=(w.gains_out, VM), qk=(qk, VM), cosine=(cosine, VM), sine=(sine, VM),
            dh2=(w.dh2, VM), att=(w.att_out, VM), z=(w.z_out, VM),
            qw0=(flat(w.qw0_out), ANY), qw1=(flat(w.qw1_out), ANY), mo1_in=(flat(w.mo1_out), ANY),
            packed_in=(w.packed_out, ANY), p2_in=(w.p2_out, ANY),
            rg=(w.gate_grad, ANY), ru=(w.up_grad, ANY), rd=(w.down_grad, ANY),
        ),
        dict(
            qw0_grad=thin, qw1_grad=thin, mo1_grad=thin, d_qk=((8, 128), F32, VM), d_mix1=partial_gain,
            dz=((256, 1024), BF, VM), sum_g=sums(2304, VM), sum_u=sums(2304, VM), sum_d=sums(2304, VM),
        ),
        dict(
            mo=bf(1024, 1024), proj=bf(1024, 1024), perm=bf(1024, 1024), ones=vm(128, 128),
            packed=bf(8, 128, 256), p2=vm(256, 1024), do=bf(256, 1024),
            out_att=bf(8, 128, 128), d_att=bf(8, 128, 128), turned=bf(1024, 256), dkv=vm(1024, 128), out=bf(8, 128, 256),
            d_packed=bf(8, 128, 256), normed=bf(256, 1024), normed_t=bf(1024, 256), dp2=bf(256, 1024),
            high=bf(256, 1024), rest=bf(256, 1024), partial=vm(256, 1024), other=vm(256, 1024),
            sg=bf(2, 1024, 256), su=bf(2, 1024, 256), sd=bf(2, 1024, 256),
            local=dma(24), send=dma(24), recv=dma(24),
            ssend=dma(4, 54), srecv=dma(4, 54), sload=dma(4, 36),
            **rings[0], **rings[1], **rings[2], **rings[3],
        ),
    )


def last(x, w, back):
    wide, mid = [((1024, n), BF, ANY) for n in (2304, 768)]
    rings = ring_names((768,) * 3, (768,) * 3, (768,) * 3, (512,) * 3, (768, 768, 640))

    def body(b):
        *b.rings, b.ring2, b.ring3 = [[getattr(b, name) for name in ring] for ring in rings]
        last_kernel(b)

    def out(*shape, where=ANY):
        return (shape, F32, where)

    return launch(
        body,
        "last",
        4,
        dict(
            gains=(w.gains_out, VM), h1=(w.h1_out, VM), dz_in=(back.dz, VM), d_qk=(back.d_qk, VM), d_mix1=(back.d_mix1, VM),
            gate0=(flat(w.gate0_out), ANY), up0=(flat(w.up0_out), ANY), down0=(flat(w.down0_out), ANY),
            qw0_grad=(back.qw0_grad, ANY), qw1_grad=(back.qw1_grad, ANY), mo1_grad=(back.mo1_grad, ANY),
            x=(x, VM), taps=(w.taps_out, VM), m1=(w.m1_out, VM), pad=(w.pad_out, VM), d_ffn1=(w.d_ffn, VM),
            mo0_in=(flat(w.mo0_out), ANY), p1_in=(w.p1_out, ANY), ci0=(flat(w.ci0_out), ANY), ci1=(flat(w.ci1_out), ANY),
            sum_g1=(back.sum_g, VM), sum_u1=(back.sum_u, VM), sum_d1=(back.sum_d, VM),
        ),
        dict(
            gate_grad=wide, up_grad=wide, down_grad=wide, ci0_grad=mid, ci1_grad=mid, mt_grad=((1024, 640), BF, ANY),
            dx_out=((256, 512), BF, ANY), small=out(8, 1024, where=VM), mix_out=out(2, 8, 2560),
            block_out=out(16, 14848),
            sum_mt=out(16, 640, where=VM),
        ),
        dict(
            mo=bf(1024, 1024), proj=bf(1024, 1536), perm=bf(1024, 1024), p1=vm(256, 1536), do=bf(256, 1024),
            turned=bf(1024, 256), normed=bf(256, 1024), normed_t=bf(1024, 256), high=bf(256, 1024), rest=bf(256, 1024),
            partial=vm(256, 1024), other=vm(256, 1024), other0=vm(256, 1024), dh1=vm(256, 1024),
            dp1=bf(256, 1536), dconv=vm(2, 136, 512), rim=vm(2, 8, 512), d_taps=vm(8, 512),
            d_ffn0=vm(8, 1024), d_mix0=vm(8, 1024), sum_q0=sums(512), sum_q1=sums(512),
            sum_mo1=sums(512), sum_g=sums(2304), sum_u=sums(2304), sum_d=sums(2304), sum_c0=sums(768), sum_c1=sums(768),
            sums=vm(4, 8, 1024), qk_other=vm(8, 128), arrivals=vm(9, 8, 1024), small_send=dma(10), small_recv=dma(10),
            local=dma(24), send=dma(20), recv=dma(20), trade=dma(12),
            ssend=dma(5, 54), srecv=dma(5, 54), sload=dma(5, 36), **ffn_scratch(),
            **rings[0], **rings[1], **rings[2], **rings[3], **rings[4],
        ),
    )


def low(v):
    return v.astype(BF)


def matmul(left, right):
    return jnp.dot(left, right, preferred_element_type=F32)


def times_transposed(left, right):
    return lax.dot_general(left, right, (((1,), (1,)), ((), ())), preferred_element_type=F32)


def transposed_times(left, right):
    return lax.dot_general(left, right, (((0,), (0,)), ((), ())), preferred_element_type=F32)


def both_halves(conv_in, qkv):
    b = conv_in.reshape(8, 3, 2, 512).transpose(2, 0, 1, 3).reshape(2, 8, 1536)
    q = qkv[:, :1024].reshape(8, 2, 512).transpose(1, 0, 2)
    kv = qkv[:, 1024:].reshape(8, 2, 2, 4, 64).transpose(2, 0, 3, 1, 4).reshape(2, 8, 512)
    return jnp.concatenate([b, q, kv], 2)


def from_halves(grads):
    conv = grads[:, :, :1536].reshape(2, 8, 3, 512).transpose(1, 2, 0, 3).reshape(8, 3072)
    q = grads[:, :, 1536:2048].transpose(1, 0, 2).reshape(8, 1024)
    kv = grads[:, :, 2048:].reshape(2, 8, 4, 2, 64).transpose(1, 3, 0, 2, 4).reshape(8, 1024)
    return conv, jnp.concatenate([q, kv], 1)


def rope_tables():
    positions = (lax.axis_index(SQ) * 128 + jnp.arange(128)).astype(F32)
    frequency = 1000000.0 ** (-jnp.arange(32).astype(F32) * 2.0 / 64)
    angles = positions[:, None] * frequency[None, :]
    cosine, sine = jnp.cos(angles), jnp.sin(angles)
    return jnp.concatenate([cosine] * 4, 1), jnp.concatenate([-sine, sine] * 2, 1)


def shards(
    inputs,
    cotangent,
    conv_in,
    conv_kernel,
    qkv_weight,
    qk_gain,
    mix_gain,
    ffn_gain,
    mix_out,
    w_gate,
    w_up,
    w_down,
):
    place = lax.axis_index((DP, SQ)) % 16 * 8
    x = inputs.reshape(256, 1024)
    cot = cotangent.reshape(256, 1024)
    gains = jnp.pad(jnp.concatenate([mix_gain, ffn_gain], 0).astype(F32), ((0, 6), (0, 0)))
    qk = qk_gain.astype(F32)
    qk = jnp.concatenate([qk, jnp.concatenate([qk[:1], jnp.ones((1, 64), F32)], 0)], 1)
    cosine, sine = rope_tables()
    taps = lax.dynamic_update_slice(jnp.zeros((16, 128), BF), conv_kernel, (0, place))
    mix = both_halves(conv_in, qkv_weight).astype(F32)
    saved = forward(x, cot, gains, qk, cosine, sine, taps, mix, (w_gate[0], w_up[0], w_down[0].T, mix_out[0]))
    end = last(x, saved, backward(qk, cosine, sine, saved))
    conv_in_grad, qkv_grad = from_halves(end.mix_out)
    q_sum, k_sum = end.small[2, :128], end.small[3, :64]

    mo_grad, gate_grad, up_grad, down_grad = jnp.split(end.block_out, (1024, 5632, 10240), 1)
    return (
        saved.result.reshape(2, 1, 128, 512),
        end.dx_out.reshape(2, 1, 128, 512),
        conv_in_grad,
        lax.dynamic_slice(end.sum_mt, (0, 512 + place), (3, 8)),
        qkv_grad,
        jnp.stack([q_sum[:64] + q_sum[64:], k_sum]),
        end.small[0:1],
        end.small[1:2],
        mo_grad[None],
        gate_grad[None],
        up_grad[None],
        down_grad.T[None],
    )


def solution(mesh):
    every = (S, DP, SQ)
    weight = P(S, (DP, SQ), None)
    tokens = P(None, DP, SQ, None)
    in_specs = (
        tokens,
        tokens,
        P(every, None),
        P(None, every),
        P(every, None),
        P(),
        P(S, None),
        P(S, None),
        weight,
        weight,
        weight,
        P(S, None, (DP, SQ)),
    )
    tokens = P(None, DP, SQ, S)
    out_specs = (
        tokens,
        tokens,
        P(every, None),
        P(None, every),
        P(every, None),
        P(),
        P(S, None),
        P(S, None),
        weight,
        weight,
        weight,
        P(S, None, (DP, SQ)),
    )
    return jax.shard_map(shards, mesh=mesh, in_specs=in_specs, out_specs=out_specs, check_vma=False)
```
